32 devices in a mesh: region: 8 (over z, y), scen: 4 (over x, core).
Axes of the slice: x: 2, y: 2, z: 4, core: 2. Of those that a mesh axis runs over, the one named last changes fastest.
Arguments:
- inverse_blocks: float32 [256, 5, 96, 96], P('region')
- block_cols: int32 [256, 5], P('region'), may hold values from 0 to 31, as said below
- source_current: float32 [24576], P('region'), may hold values from -6 to 6
- node_decay: float32 [24576], P('region'), may hold values from 0.3 to 0.95
- node_gain: float32 [24576], P('region'), may hold values from 0.05 to 0.5
- voltage_init: float32 [256, 24576], P('scen', 'region'), may hold values from -6 to 6
- branch_init: float32 [256, 24576], P('scen', 'region'), may hold values from -3 to 3
- wave_init: float32 [8, 256, 2048], P(None, 'scen', 'region'), may hold values from -6 to 6
- line_node: int32 [2048], P('region'), may hold values from 0 to 3071
- line_delay: int32 [2048], P('region'), may hold values from 1 to 8, as said below
- line_admittance: float32 [2048], P('region'), may hold values from 0.19 to 1, as said below
- conv_region: int32 [3072, 1], P('region'), may hold values from 0 to 7; in each aligned block of 384 rows (0 to 383, 384 to 767, ...) at most 115 rows name the same one
- conv_node: int32 [3072], P('region'), may hold values from 0 to 3071
- conv_power: float32 [3072], P('region'), may hold values from 0.3 to 3
- conv_gains: float32 [2, 3072], P(None, 'region'), may hold values from 0.2 to 0.9
- conv_init: float32 [2, 256, 3072], P(None, 'scen', 'region'), may hold values from -3 to 3
- fault_node: int32 [256], P('scen'), may hold values from 0 to 24575
- fault_kind: int32 [256], P('scen'), may hold values from 0 to 3
Outputs:
- voltage: float32 [256, 24576], P('scen', 'region')
- branch_history: float32 [256, 24576], P('scen', 'region')
- wave_history: float32 [8, 256, 2048], P(None, 'scen', 'region')
- conv_state: float32 [2, 256, 3072], P(None, 'scen', 'region')
- envelope: float32 [24576], P('region')
The draws below stay inside these ranges and needn't reach their ends.
Inputs may be any that keep to these rules, and one draw needn't show every extreme that they name: `block_cols`: entry 0 of row b is b mod 32; the 5 entries of a row are distinct. `line_delay`: entry r * 2 * 128 + l with l < 128 equals entry ((r - 1) mod 8) * 2 * 128 + 128 + l: both ends of a line have one delay. `line_admittance`: entry r * 2 * 128 + l with l < 128 equals entry ((r - 1) mod 8) * 2 * 128 + 128 + l: both ends of a line have one admittance. `conv_region`: among the converters of one region index of the mesh (aligned blocks of 384 rows), at most 115 lie in one region, and some region gets exactly 115.
All inputs are finite; a program needn't handle non-finite values.
Results may differ from the reference program's by a relative error of at most 0.00011.
Values sent between devices are 32-bit elements; how exact they have to be, the bound alone decides.
No kernel may reach another device: no remote copies, remote signals or barrier semaphores. Data moves between devices by JAX's collectives and lax.ppermute only.
A program may use at most 128 MiB of HBM per device.

```python
import math
import jax
import jax.numpy as jnp
import numpy as np
from jax import lax

BLK = 96
NB_DEV = 32
KB = 5
LN = 128
DMAX = 8
STEPS = 4
CONV_DEV = 384
KINDS = 4
REGIONS = 8
NODE_DEV = 3072
NODES = 24576
SCEN = 256
LINES = 1024
CONVERTERS = 3072
CAP = 115
N_REGION = 8


def draw_inverse_blocks(key, part):
    block_rows = NODES // BLK
    noise_key, diagonal_key = jax.random.split(key)
    spread = 0.3 * (BLK * KB) ** (-0.5)
    noise_part = jax.random.normal(noise_key, (block_rows, KB, BLK, BLK), jnp.float32)
    diagonal = jax.random.uniform(diagonal_key, (block_rows, 1, 1), jnp.float32, 0.25, 0.35)
    identity = jnp.eye(BLK, dtype=jnp.float32)
    leading = noise_part[:, 0] * spread + diagonal * identity
    return jnp.concatenate([leading[:, None], noise_part[:, 1:] * spread], axis=1)


def draw_block_cols(key, part):
    block_rows = NODES // BLK
    columns = jnp.arange(NB_DEV, dtype=jnp.int32)
    scores = jax.random.randint(key, (block_rows, NB_DEV), 0, 1 << 20, dtype=jnp.int32) * NB_DEV + columns[None, :]
    own_block = jnp.arange(block_rows, dtype=jnp.int32) % NB_DEV
    scores = jnp.where(columns[None, :] == own_block[:, None], -1, scores)
    return jnp.argsort(scores, axis=1, stable=True)[:, :KB].astype(jnp.int32)


def draw_line_delay(key, part):
    region_count = LINES // LN
    delays = jax.random.randint(key, (region_count, LN), 1, DMAX + 1, dtype=jnp.int32)
    delays = delays.at[0, 0].set(DMAX).at[0, 1].set(1)
    return jnp.concatenate([jnp.roll(delays, 1, axis=0), delays], axis=1).reshape(-1).astype(jnp.int32)


def draw_line_admittance(key, part):
    region_count = LINES // LN
    values = jnp.exp(jax.random.uniform(key, (region_count, LN), jnp.float32, math.log(0.2), 0.0))
    return jnp.concatenate([jnp.roll(values, 1, axis=0), values], axis=1).reshape(-1)


def plant(array, key, low, largest):
    extent = array.shape
    index_at = [jax.random.randint(jax.random.fold_in(key, axis), (), 0, extent[axis]) for axis in range(len(extent))]
    array = array.at[tuple(index_at)].set(low)
    longest = extent.index(max(extent))
    index_at[longest] = (index_at[longest] + 1) % extent[longest]
    return array.at[tuple(index_at)].set(largest)


def levels(stream_key, dims, shards, smallest, top_value):
    level = 1.0
    for position, shards_of in shards:
        heights = jax.random.uniform(jax.random.fold_in(jax.random.fold_in(stream_key, 6), position), (shards_of,), jnp.float32, smallest / len(shards), top_value / len(shards))
        level = level * jnp.repeat(jnp.exp(heights), dims[position] // shards_of).reshape((-1,) + (1,) * (len(dims) - 1 - position))
    return level


def routed_block(key, own, number, rows, number_of, top, reach, slope):
    ranking = jax.random.permutation(key, number_of)
    heavy_load, usual = portions_of(number_of, rows * top, reach, slope, True), portions_of(number_of, rows * top, reach, slope, False)
    places = jnp.arange(number_of)

    def named(tallies, rotation):
        used = int((tallies > 0).sum())
        fixed = max(1, used // 4)
        passed = fixed + (places - fixed + rotation * (used - fixed)) % max(1, number_of - fixed)
        return jnp.zeros((number_of,), jnp.int32).at[ranking[jnp.where(places < fixed, places, passed)]].set(jnp.asarray(tallies, jnp.int32))

    tallies = jnp.where(number % 4 == 0, named(heavy_load, number // 4), named(usual, number - number // 4 - 1))
    mixed = jax.random.permutation(jax.random.fold_in(own, 3), number_of)
    source_of, taker = mixed[0:number_of // 2 * 2:2], mixed[1:number_of // 2 * 2:2]
    slack = jnp.minimum(tallies[source_of] - 1, reach - tallies[taker]) // 2
    slack = jnp.where((source_of == ranking[0]) | (taker == ranking[0]) | (tallies[taker] == 0), 0, jnp.maximum(slack, 0))
    passed = jax.random.randint(jax.random.fold_in(own, 4), (number_of // 2,), 0, 1 << 20) % (slack + 1)
    tallies = tallies.at[source_of].add(-passed).at[taker].add(passed)
    members = jnp.searchsorted(jnp.cumsum(tallies), jnp.arange(rows * top), side="right").astype(jnp.int32)
    grid = members.reshape(top, rows).T
    grid = grid[jax.random.permutation(jax.random.fold_in(own, 1), rows)]
    rotation = jax.random.randint(jax.random.fold_in(own, 2), (rows, 1), 0, top)
    return jnp.take_along_axis(grid, (jnp.arange(top)[None, :] + rotation) % top, axis=1)


def portions_of(number_of, total, most, slope, full):
    weights = [(1 << 20) // math.isqrt(grade ** slope) + 1 for grade in range(1, number_of + 1)]
    largest = most if full else min(most, max(-(-total // number_of), total * weights[0] // sum(weights)))
    least = 1 if total - largest >= number_of - 1 else 0
    counts, rest = [largest] + [least] * (number_of - 1), total - largest - least * (number_of - 1)
    while rest > 0:
        candidates = [i for i in range(1, number_of) if counts[i] < largest] or [i for i in range(1, number_of) if counts[i] < most]
        pool, remaining = sum([weights[i] for i in candidates]), rest
        for i in candidates:
            addition = min(most - counts[i], max(1, remaining * weights[i] // pool), rest)
            counts[i] = counts[i] + addition
            rest = rest - addition
    return np.array(counts)


def scatter_about(stream_key, extent, scale, reach, cuts=(), kind=jnp.bfloat16):
    loudness = levels(stream_key, extent, cuts, -0.22, 0.18) if cuts else 1.0
    result = jax.random.normal(stream_key, extent, jnp.float32) * scale * loudness
    return jnp.minimum(jnp.maximum(result, -reach), reach).astype(kind)


def setup_inputs(seed: int = 0) -> dict:
    splits = jax.random.split(jax.random.key(seed), 19)
    inverse_blocks = draw_inverse_blocks(jax.random.fold_in(splits[18], 71), 0)
    block_cols = draw_block_cols(jax.random.fold_in(splits[18], 71), 0)
    source_current = scatter_about(splits[2], (NODES,), 1.0, 6.0, ((0, 8),), jnp.float32)
    node_decay = jnp.clip(0.3 + 0.65 * jax.random.uniform(splits[3], (NODES,), jnp.float32) ** levels(splits[3], (NODES,), ((0, 8),), -0.2, 0.2), 0.3, 0.95)
    node_gain = jnp.clip(jnp.exp(math.log(0.5) - 2.3025851 * jax.random.uniform(splits[4], (NODES,), jnp.float32) ** levels(splits[4], (NODES,), ((0, 8),), -0.2, 0.2)), 0.05, 0.5)
    voltage_init = scatter_about(splits[5], (SCEN, NODES), 1.0, 6.0, ((0, 4), (1, 8)), jnp.float32)
    branch_init = scatter_about(splits[6], (SCEN, NODES), 0.5, 3.0, ((0, 4), (1, 8)), jnp.float32)
    wave_init = scatter_about(splits[7], (DMAX, SCEN, 2 * LINES), 1.0, 6.0, ((1, 4), (2, 8)), jnp.float32)
    line_node = plant(jax.random.randint(splits[8], (2 * LINES,), 0, NODE_DEV), jax.random.fold_in(splits[8], 1), 0, NODE_DEV - 1).astype(jnp.int32)
    line_delay = draw_line_delay(jax.random.fold_in(splits[18], 71), 0)
    line_admittance = draw_line_admittance(jax.random.fold_in(splits[18], 71), 0)
    conv_region_keys = jax.random.split(jax.random.fold_in(splits[11], 1), CONVERTERS // CONV_DEV)
    conv_region_turns = jax.random.permutation(jax.random.fold_in(splits[11], 3), CONVERTERS // CONV_DEV)
    conv_region = jax.vmap(lambda own, number: routed_block(jax.random.fold_in(splits[11], 2), own, number, CONV_DEV, REGIONS, 1, CAP, 1))(conv_region_keys, conv_region_turns).reshape((CONVERTERS, 1))
    conv_node = plant(jax.random.randint(splits[12], (CONVERTERS,), 0, NODE_DEV), jax.random.fold_in(splits[12], 1), 0, NODE_DEV - 1).astype(jnp.int32)
    conv_power = jnp.clip(jnp.exp(math.log(3.0) - 2.3025851 * jax.random.uniform(splits[13], (CONVERTERS,), jnp.float32) ** levels(splits[13], (CONVERTERS,), ((0, 8),), -0.2, 0.2)), 0.3, 3.0)
    conv_gains = jnp.clip(0.2 + 0.7 * jax.random.uniform(splits[14], (2, CONVERTERS), jnp.float32) ** levels(splits[14], (2, CONVERTERS), ((1, 8),), -0.2, 0.2), 0.2, 0.9)
    conv_init = scatter_about(splits[15], (2, SCEN, CONVERTERS), 0.5, 3.0, ((1, 4), (2, 8)), jnp.float32)
    fault_node = plant(jax.random.randint(splits[16], (SCEN,), 0, NODES), jax.random.fold_in(splits[16], 1), 0, NODES - 1).astype(jnp.int32)
    fault_kind = plant(jax.random.randint(splits[17], (SCEN,), 0, KINDS), jax.random.fold_in(splits[17], 1), 0, KINDS - 1).astype(jnp.int32)
    return {"inverse_blocks": inverse_blocks, "block_cols": block_cols, "source_current": source_current, "node_decay": node_decay, "node_gain": node_gain, "voltage_init": voltage_init, "branch_init": branch_init, "wave_init": wave_init, "line_node": line_node, "line_delay": line_delay, "line_admittance": line_admittance, "conv_region": conv_region, "conv_node": conv_node, "conv_power": conv_power, "conv_gains": conv_gains, "conv_init": conv_init, "fault_node": fault_node, "fault_kind": fault_kind}


def apply_inverse(inverse_blocks, global_cols, current):
    scen_count = current.shape[0]
    block_rows = inverse_blocks.shape[0]
    block_width = inverse_blocks.shape[2]
    blocks = current.reshape(scen_count, block_rows, block_width)
    summed = jnp.zeros((scen_count, block_rows, block_width), jnp.float32)
    for column in range(inverse_blocks.shape[1]):
        picked = jnp.take(blocks, global_cols[:, column], axis=1)
        summed = summed + jnp.einsum('sbi,boi->sbo', picked, inverse_blocks[:, column], precision=lax.Precision.HIGHEST)
    return summed.reshape(scen_count, block_rows * block_width)


def reference(inverse_blocks, block_cols, source_current, node_decay, node_gain, voltage_init, branch_init, wave_init, line_node, line_delay, line_admittance, conv_region, conv_node, conv_power, conv_gains, conv_init, fault_node, fault_kind):
    region_count = N_REGION
    block_rows = inverse_blocks.shape[0]
    region_of_block = jnp.arange(block_rows, dtype=jnp.int32) // NB_DEV
    global_cols = (region_of_block[:, None] * NB_DEV + block_cols).astype(jnp.int32)
    end_count = line_node.shape[0]
    end_node = ((jnp.arange(end_count, dtype=jnp.int32) // (2 * LN)) * NODE_DEV + line_node).astype(jnp.int32)
    conv_global = (conv_region[:, 0] * NODE_DEV + conv_node).astype(jnp.int32)
    conductance = 0.25 * jnp.power(jnp.float32(2.0), fault_kind.astype(jnp.float32))
    scen_index = jnp.arange(SCEN, dtype=jnp.int32)
    delay_pick = (line_delay[None, :] == jnp.arange(1, DMAX + 1, dtype=jnp.int32)[:, None]).astype(jnp.float32)
    voltage = voltage_init
    branch = branch_init
    waves = wave_init
    filtered = conv_init[0]
    conv_amps = conv_init[1]
    envelope = jnp.zeros((NODES,), jnp.float32)
    for step_index in range(STEPS):
        drive = jnp.sum(delay_pick[:, None, :] * waves, axis=0)
        branch = node_decay[None, :] * branch + node_gain[None, :] * voltage
        measured = voltage[:, conv_global]
        filtered = filtered + conv_gains[1][None, :] * (measured - filtered)
        target_amps = conv_power[None, :] * filtered / (1.0 + filtered * filtered)
        conv_amps = conv_amps + conv_gains[0][None, :] * (target_amps - conv_amps)
        current = source_current[None, :] - branch
        current = current.at[:, end_node].add(drive)
        current = current.at[:, conv_global].add(conv_amps)
        current = current.at[scen_index, fault_node].add(-conductance * voltage[scen_index, fault_node])
        voltage = apply_inverse(inverse_blocks, global_cols, current)
        envelope = jnp.maximum(envelope, jnp.max(jnp.abs(voltage), axis=0))
        launch = 2.0 * line_admittance[None, :] * voltage[:, end_node] - drive
        split_ends = launch.reshape(SCEN, region_count, 2, LN)
        from_previous = jnp.roll(split_ends[:, :, 1, :], 1, axis=1)
        from_following = jnp.roll(split_ends[:, :, 0, :], -1, axis=1)
        arrived = jnp.stack([from_previous, from_following], axis=2).reshape(SCEN, end_count)
        waves = jnp.concatenate([arrived[None], waves[:-1]], axis=0)
    conv_state = jnp.stack([filtered, conv_amps], axis=0)
    return (voltage, branch, waves, conv_state, envelope)
```

```python
import functools
import math

import jax
import jax.numpy as jnp
from jax import lax
from jax.experimental import pallas as pl
from jax.experimental.pallas import tpu as pltpu
from jax.sharding import PartitionSpec as P

STEPS = 4
LANES = 128
BF = jnp.bfloat16
F32 = jnp.float32
I32 = jnp.int32
VMEM = pl.BlockSpec(memory_space=pltpu.VMEM)
SMEM = pl.BlockSpec(memory_space=pltpu.SMEM)
HBM = pl.BlockSpec(memory_space=pltpu.HBM)
PARAMS = pltpu.CompilerParams(vmem_limit_bytes=20 << 20)


def round_up(value, unit):
    return -(-value // unit) * unit


def iota(shape, dim):
    return lax.broadcasted_iota(I32, shape, dim)


def split_2(value):
    high = value.astype(BF)
    return high, (value - high.astype(F32)).astype(BF)


def split_3(value):
    high = value.astype(BF)
    rest = value - high.astype(F32)
    middle = rest.astype(BF)
    return high, middle, (rest - middle.astype(F32)).astype(BF)


def stacked(value):
    high, low = split_2(value)
    return jnp.concatenate([high, low], axis=0)


def folded(value):
    half = value.shape[0] // 2
    return value[:half] + value[half:]


def dot(left, right):
    return jnp.dot(left, right, preferred_element_type=F32)


def one_hot(mask):
    return jnp.where(mask, 1.0, 0.0).astype(BF)


def padded_index(nodes, width, padded):
    block = jnp.floor((nodes + 0.5) * (1.0 / width))
    return nodes + block * (padded - width)


class Sizes:
    def __init__(self, inverse_blocks, voltage, wave_init, line_node, conv_node):
        self.blocks, self.picks, self.width, _ = inverse_blocks.shape
        self.scen, self.nodes = voltage.shape
        self.delays = wave_init.shape[0]
        self.ends = line_node.shape[0]
        self.lines = self.ends // 2
        self.convs = conv_node.shape[0]
        self.regions = lax.axis_size("region")
        self.capacity = max(2, 12 * self.convs // (5 * self.regions))
        self.rows = round_up(self.capacity + 4, 8)
        self.slots = self.regions * self.rows
        self.slot_lanes = round_up(self.slots, LANES)
        self.padded = round_up(self.width, LANES)
        self.lanes = self.blocks * self.padded
        self.group = math.lcm(self.width, LANES) // self.width

    def vmem(self, shape, dtype=F32):
        return pltpu.VMEM(shape, dtype)


def pad_blocks(size, source, store):
    group_width = size.group * size.width
    for first in range(0, size.blocks, size.group):
        chunk = source[:, first * size.width : first * size.width + group_width]
        for j in range(size.group):
            part = chunk[:, j * size.width : (j + 1) * size.width]
            zeros = jnp.zeros((part.shape[0], size.padded - size.width), part.dtype)
            store(first + j, jnp.concatenate([part, zeros], axis=1))


def unpad_blocks(size, load, target):
    group_width = size.group * size.width
    for first in range(0, size.blocks, size.group):
        parts = [load(first + j)[:, : size.width] for j in range(size.group)]
        target[:, first * size.width : first * size.width + group_width] = jnp.concatenate(
            parts, axis=1
        )


def pack_kernel(size, region, node, power, gains, init, out, dst_out):
    convs, slots = size.convs, size.slots
    target = region[...]
    member = iota((round_up(size.regions, 16), convs), 0) == target
    before = one_hot(iota((convs, convs), 0) < iota((convs, convs), 1))
    earlier = dot(one_hot(member), before)
    rank = jnp.sum(jnp.where(member, earlier, 0.0), axis=0, keepdims=True)
    dst = target * size.rows + rank.astype(I32)
    dst_out[...] = dst
    select = one_hot(iota((slots, convs), 0) == dst)
    state = jnp.concatenate([init[0], init[1]], axis=0)
    settings = jnp.concatenate(
        [power[...], gains[...], node[...].astype(F32), jnp.zeros((LANES - 4, convs), F32)], axis=0
    )
    payload = jnp.concatenate([state.T, settings.T], axis=1)
    width = state.shape[0]
    rows = sum(dot(select, part) for part in split_3(payload))
    for r in range(size.regions):
        chunk = rows[r * size.rows : (r + 1) * size.rows]
        out[r] = chunk[:, :width]
        filler = jnp.zeros((LANES - size.rows, LANES), F32)
        turned = jnp.concatenate([chunk[:, width:], filler], axis=0).T
        out[r, size.capacity : size.capacity + 4, :] = turned[:4]


def converter_part(size, vb, cg, cs, prm, filt, amps, volt, branch, node_rows, peak, fault, base):
    measured = folded(dot(vb[...], cg[...]))
    filtered = filt[...]
    filtered = filtered + prm[2:3, :] * (measured - filtered)
    current = amps[...]
    target = prm[0:1, :] * filtered / (1.0 + filtered * filtered)
    current = current + prm[1:2, :] * (target - current)
    filt[...] = filtered
    amps[...] = current
    pair = stacked(current)
    site, level = fault
    lane = iota((size.scen, size.padded), 1)
    for b in range(size.blocks):
        injected = folded(dot(pair, cs[:, b * size.padded : (b + 1) * size.padded]))
        v = volt[b]
        history = node_rows[b, 1:2, :] * branch[b] + node_rows[b, 2:3, :] * v
        branch[b] = history
        hit = jnp.where(lane + b * size.padded == site, level, 0.0)
        base[b] = node_rows[b, 0:1, :] - history + injected - hit * v
        if peak is not None:
            size_of = jnp.abs(v)
            top = size_of[:8]
            for s in range(8, size.scen, 8):
                top = jnp.maximum(top, size_of[s : s + 8])
            peak[b] = jnp.maximum(peak[b], top)


def network_part(size, cols, history, delay, admittance, base, es, eg, wp, x, volt, vb):
    drive = jnp.zeros((size.scen, size.ends), F32)
    for d in range(size.delays):
        drive = jnp.where(delay == d + 1, history(d), drive)
    pair = stacked(drive)
    for b in range(size.blocks):
        added = folded(dot(pair, es[:, b * size.padded : (b + 1) * size.padded]))
        x[b] = stacked(base[b] + added)
    zeros = jnp.zeros((size.padded - size.width, 2 * size.padded), BF)

    def block_row(b, carry):
        left = jnp.concatenate([x[cols[k, b]] for k in range(size.picks)], axis=1)
        parts = []
        for k in range(size.picks):
            parts += [wp[b, k * size.width : (k + 1) * size.width, :], zeros]
        product = dot(left, jnp.concatenate(parts, axis=0))
        top, low = product[: size.scen], product[size.scen :]
        value = top[:, : size.padded] + top[:, size.padded :] + low[:, : size.padded]
        volt[b] = value
        vb[:, pl.ds(pl.multiple_of(b * size.padded, LANES), size.padded)] = stacked(value)
        return carry

    lax.fori_loop(0, size.blocks, block_row, 0, unroll=8)
    at_ends = folded(dot(vb[...], eg[...]))
    return 2.0 * admittance * at_ends - drive


def fault_terms(size, node, kind):
    first = lax.axis_index("region") * size.nodes
    local = (node[...] - first).astype(F32)
    inside = (local >= 0.0) & (local < size.nodes)
    site = jnp.where(inside, padded_index(local, size.width, size.padded), -1.0)
    level = 0.25 * jnp.left_shift(1, kind[...]).astype(F32)
    square = (size.scen, size.scen)
    diagonal = iota(square, 0) == iota(square, 1)

    def column(row):
        spread = jnp.where(diagonal, jnp.broadcast_to(row, square), 0.0)
        return jnp.broadcast_to(
            jnp.sum(spread, axis=1, keepdims=True), (size.scen, size.padded)
        )

    return column(site).astype(I32), column(level)


def turned_row(row):
    return jnp.broadcast_to(row, (LANES, row.shape[1])).T


def start_kernel(
    size,
    cols, received, inverse, source, decay, gain, voltage, branch_init, waves,
    line_node, delay, admittance, fault_node, fault_kind,
    wp, eg, es, cg, cs, prm, filt, amps, volt, vb, branch, node_rows, peak, fault_cols, up, down,
    raw, base, x, sems,
):
    stage = size.blocks // sems.shape[0]
    copies = []
    for i in range(sems.shape[0]):
        part = pl.ds(i * stage, stage)
        copies.append(pltpu.make_async_copy(inverse.at[part], raw.at[part], sems.at[i]))
        copies[-1].start()
    rows, capacity, slots = size.rows, size.capacity, size.slots
    regions, lanes = size.regions, size.lanes

    spare = size.slot_lanes - slots
    settings = [received[r * rows + capacity : r * rows + capacity + 4, :rows] for r in range(regions)]
    if spare:
        settings.append(jnp.zeros((4, spare), F32))
    prm[0:4, :] = jnp.concatenate(settings, axis=1)
    for c in range(0, size.slot_lanes, LANES):
        count = min(LANES, slots - c)
        within = lax.rem(iota((count, 2 * size.scen), 0) + c, rows)
        piece = jnp.where(within < capacity, received[c : c + count, :], 0.0)
        if count < LANES:
            piece = jnp.concatenate([piece, jnp.zeros((LANES - count, 2 * size.scen), F32)], axis=0)
        turned = piece.T
        filt[:, c : c + LANES] = turned[: size.scen]
        amps[:, c : c + LANES] = turned[size.scen :]

    def sites(row, gather, scatter):
        for c in range(0, row.shape[1], LANES):
            part = row[:, c : c + LANES]
            down_delta = part - iota((LANES, LANES), 0).astype(F32)
            across_delta = turned_row(part) - iota((LANES, LANES), 1).astype(F32)
            for n in range(0, lanes, LANES):
                gather[n : n + LANES, c : c + LANES] = one_hot(down_delta == float(n))
                scatter[c : c + LANES, n : n + LANES] = one_hot(across_delta == float(n))

    sites(padded_index(prm[3:4, :], size.width, size.padded), cg, cs)
    sites(padded_index(line_node[...].astype(F32), size.width, size.padded), eg, es)

    def put_voltage(b, value):
        volt[b] = value
        vb[:, b * size.padded : (b + 1) * size.padded] = stacked(value)

    def put_branch(b, value):
        branch[b] = value

    pad_blocks(size, voltage, put_voltage)
    pad_blocks(size, branch_init, put_branch)
    for i, vector in enumerate((source, decay, gain)):
        def put_row(b, value, i=i):
            node_rows[b, i : i + 1, :] = value

        pad_blocks(size, vector, put_row)
    site, level = fault_terms(size, fault_node, fault_kind)
    fault_cols[0] = site.astype(F32)
    fault_cols[1] = level
    converter_part(
        size, vb, cg, cs, prm, filt, amps, volt, branch, node_rows, None, (site, level), base
    )
    peak[...] = jnp.zeros(peak.shape, F32)

    for i, copy in enumerate(copies):
        copy.wait()

        def turn(b, carry):
            for k in range(size.picks):
                high, low = split_2(raw[b, k].T)
                zeros = jnp.zeros((size.width, size.padded - size.width), BF)
                wp[b, k * size.width : (k + 1) * size.width, :] = jnp.concatenate(
                    [high, zeros, low, zeros], axis=1
                )
            return carry

        lax.fori_loop(i * stage, (i + 1) * stage, turn, 0)

    launch = network_part(
        size, cols, lambda d: waves[d], delay[...], admittance[...], base, es, eg, wp, x, volt, vb
    )
    up[...] = launch[:, size.lines :]
    down[...] = launch[:, : size.lines]


def middle_kernel(size, last, vb, cg, cs, prm, volt, node_rows, fault_cols, *refs):
    refs = refs[4:]
    filt, amps, branch, peak, base = refs[:5]
    fault = (fault_cols[0].astype(I32), fault_cols[1])
    converter_part(size, vb, cg, cs, prm, filt, amps, volt, branch, node_rows, peak, fault, base)
    if last:
        back, branch_out = refs[5:]
        for c in range(0, size.slot_lanes, LANES):
            count = min(LANES, size.slots - c)
            part = jnp.concatenate([filt[:, c : c + LANES], amps[:, c : c + LANES]], axis=0)
            back[c : c + count, :] = part.T[:count]
        unpad_blocks(size, lambda b: branch[b], branch_out)


def step_kernel(size, last, done, cols, wp, eg, es, base, delay, admittance, waves, *refs):
    arrivals, refs = refs[: 2 * done], refs[2 * done :]

    def history(d):
        if d >= done:
            return waves[d - done]
        return jnp.concatenate([arrivals[2 * d][...], arrivals[2 * d + 1][...]], axis=1)

    if not last:
        volt, vb, up, down, x = refs
    else:
        peak, back, chunks, voltage_out, peak_out, volt, vb, x = refs
    launch = network_part(
        size, cols, history, delay[...], admittance[...], base, es, eg, wp, x, volt, vb
    )
    if not last:
        up[...] = launch[:, size.lines :]
        down[...] = launch[:, : size.lines]
        return
    rows = size.rows
    for r in range(size.regions):
        chunks[r, :rows, :] = back[r * rows : (r + 1) * rows, :]
    here = lax.axis_index("region")
    after = lax.rem(here + 1, size.regions)
    ahead = lax.rem(here + size.regions - 1, size.regions)
    chunks[after, rows : rows + size.scen, :] = launch[:, size.lines :]
    chunks[ahead, rows : rows + size.scen, :] = launch[:, : size.lines]
    unpad_blocks(size, lambda b: volt[b], voltage_out)

    def largest(b):
        top = jnp.max(jnp.abs(volt[b]), axis=0, keepdims=True)
        return jnp.maximum(top, jnp.max(peak[b], axis=0, keepdims=True))

    unpad_blocks(size, largest, peak_out)


def end_kernel(size, done, peaks, dst, received, waves, *refs):
    own, refs = refs[:peaks], refs[peaks:]
    arrivals, (state_out, waves_out, envelope_out) = refs[: 2 * done], refs[2 * done :]
    here = lax.axis_index("region")
    after = lax.rem(here + 1, size.regions)
    ahead = lax.rem(here + size.regions - 1, size.regions)
    rows, lines = size.rows, size.lines
    waves_out[0, :, :lines] = received[ahead, rows : rows + size.scen, :]
    waves_out[0, :, lines:] = received[after, rows : rows + size.scen, :]
    for d in range(1, size.delays):
        if d <= done:
            waves_out[d, :, :lines] = arrivals[2 * (d - 1)][...]
            waves_out[d, :, lines:] = arrivals[2 * (d - 1) + 1][...]
        else:
            waves_out[d] = waves[d - done - 1]
    top = own[0][...]
    for other in own[1:]:
        top = jnp.maximum(top, other[...])
    envelope_out[...] = top
    returned = jnp.concatenate([received[r, :rows, :] for r in range(size.regions)], axis=0)
    select = one_hot(iota((size.slots, size.convs), 0) == dst[...])
    parts = jnp.concatenate(split_3(returned.T), axis=0)
    state = dot(parts, select)
    width = 2 * size.scen
    state = state[:width] + state[width : 2 * width] + state[2 * width :]
    state_out[0] = state[: size.scen]
    state_out[1] = state[size.scen :]


def shape(dims, dtype=F32):
    return jax.ShapeDtypeStruct(dims, dtype)


def in_vmem(*values):
    return [pltpu.with_memory_space_constraint(v, pltpu.VMEM) for v in values]


def shards(
    inverse_blocks, block_cols, source_current, node_decay, node_gain, voltage_init, branch_init,
    wave_init, line_node, line_delay, line_admittance, conv_region, conv_node, conv_power,
    conv_gains, conv_init, fault_node, fault_kind,
):
    size = Sizes(inverse_blocks, voltage_init, wave_init, line_node, conv_node)
    regions, rows, scen = size.regions, size.rows, size.scen
    ring = [(i, (i + 1) % regions) for i in range(regions)]
    back_ring = [(j, i) for i, j in ring]

    def row(vector):
        return vector.reshape(1, -1)

    def call(kernel, name, outs, args, specs, scratch=(), aliases=None):
        return pl.pallas_call(
            kernel,
            name=name,
            out_shape=outs,
            in_specs=specs,
            out_specs=[VMEM] * len(outs),
            scratch_shapes=list(scratch),
            input_output_aliases=aliases or {},
            compiler_params=PARAMS,
        )(*args)

    packed, dst = call(
        functools.partial(pack_kernel, size),
        "pack",
        [shape((regions, rows, 2 * scen)), shape((1, size.convs), I32)],
        [row(conv_region), row(conv_node), row(conv_power), conv_gains, conv_init],
        [VMEM] * 5,
    )
    received = lax.all_to_all(packed, "region", split_axis=0, concat_axis=0, tiled=True)
    received = received.reshape(size.slots, 2 * scen)

    cols = block_cols.T
    delay, admittance = row(line_delay), row(line_admittance)
    state = (size.blocks, scen, size.padded)
    wide = (2 * scen, size.lanes)
    exchange = shape((scen, size.lines))
    x_scratch = pltpu.VMEM((size.blocks, 2 * scen, size.padded), BF)
    outs = [
        size.vmem((size.blocks, size.picks * size.width, 2 * size.padded), BF),
        size.vmem((size.lanes, size.ends), BF),
        size.vmem((size.ends, size.lanes), BF),
        size.vmem((size.lanes, size.slot_lanes), BF),
        size.vmem((size.slot_lanes, size.lanes), BF),
        size.vmem((8, size.slot_lanes)),
        size.vmem((scen, size.slot_lanes)),
        size.vmem((scen, size.slot_lanes)),
        size.vmem(state),
        size.vmem(wide, BF),
        size.vmem(state),
        size.vmem((size.blocks, 8, size.padded)),
        size.vmem((size.blocks, 8, size.padded)),
        size.vmem((2, scen, size.padded)),
        exchange,
        exchange,
    ]
    args = [
        cols, received, inverse_blocks, row(source_current), row(node_decay), row(node_gain),
        voltage_init, branch_init, wave_init, row(line_node), delay, admittance, row(fault_node),
        row(fault_kind),
    ]
    (
        wp, eg, es, cg, cs, prm, filt, amps, volt, vb, branch, node_rows, peak, fault_cols, up, down,
    ) = call(
        functools.partial(start_kernel, size),
        "start",
        outs,
        args,
        [SMEM, VMEM, HBM] + [VMEM] * 11,
        [
            pltpu.VMEM(inverse_blocks.shape, F32),
            pltpu.VMEM(state, F32),
            x_scratch,
            pltpu.SemaphoreType.DMA((4,)),
        ],
    )

    arrivals = []
    for step in range(1, STEPS):
        last = step == STEPS - 1
        from_ahead = lax.ppermute(up, "region", ring)
        from_after = lax.ppermute(down, "region", back_ring)
        outs = [
            size.vmem((scen, size.slot_lanes)),
            size.vmem((scen, size.slot_lanes)),
            size.vmem(state),
            size.vmem((size.blocks, 8, size.padded)),
            size.vmem(state),
        ]
        if last:
            outs += [size.vmem((size.slots, 2 * scen)), shape((scen, size.nodes))]
        result = call(
            functools.partial(middle_kernel, size, last),
            "middle",
            outs,
            in_vmem(vb, cg, cs, prm, volt, node_rows, fault_cols, filt, amps, branch, peak),
            [VMEM] * 11,
            aliases={7: 0, 8: 1, 9: 2, 10: 3},
        )
        filt, amps, branch, peak, base = result[:5]
        arrivals = [from_ahead, from_after] + arrivals
        args = [cols] + in_vmem(wp, eg, es, base) + [delay, admittance, wave_init] + arrivals
        specs = [SMEM] + [VMEM] * (len(args) - 1)
        if not last:
            volt, vb, up, down = call(
                functools.partial(step_kernel, size, False, step),
                "step",
                [size.vmem(state), size.vmem(wide, BF), exchange, exchange],
                args,
                specs,
                [x_scratch],
            )
            continue
        back, branch_out = result[5:]
        chunks, voltage_out, peak_out = call(
            functools.partial(step_kernel, size, True, step),
            "step",
            [
                shape((regions, rows + scen, 2 * scen)),
                shape((scen, size.nodes)),
                shape((1, size.nodes)),
            ],
            args + in_vmem(peak, back),
            specs + [VMEM] * 2,
            [pltpu.VMEM(state, F32), pltpu.VMEM(wide, BF), x_scratch],
        )

    others = lax.axis_size("scen")
    peaks = [peak_out] + [
        lax.ppermute(peak_out, "scen", [(i, (i + d) % others) for i in range(others)])
        for d in range(1, others)
    ]
    returned = lax.all_to_all(chunks, "region", split_axis=0, concat_axis=0, tiled=True)
    args = [dst, returned, wave_init] + peaks + arrivals
    conv_state, wave_history, envelope = call(
        functools.partial(end_kernel, size, STEPS - 1, len(peaks)),
        "end",
        [shape(conv_init.shape), shape(wave_init.shape), shape((1, size.nodes))],
        args,
        [VMEM] * len(args),
    )
    return voltage_out, branch_out, wave_history, conv_state, envelope.reshape(-1)


def solution(mesh):
    placed = (
        P("region", None, None, None),
        P("region", None),
        P("region"),
        P("region"),
        P("region"),
        P("scen", "region"),
        P("scen", "region"),
        P(None, "scen", "region"),
        P("region"),
        P("region"),
        P("region"),
        P("region", None),
        P("region"),
        P("region"),
        P(None, "region"),
        P(None, "scen", "region"),
        P("scen"),
        P("scen"),
    )
    return jax.shard_map(
        shards,
        mesh=mesh,
        in_specs=placed,
        out_specs=(
            P("scen", "region"),
            P("scen", "region"),
            P(None, "scen", "region"),
            P(None, "scen", "region"),
            P("region"),
        ),
        check_vma=False,
    )
```

```python
import functools
import math

import jax
import jax.numpy as jnp
from jax import lax
from jax.experimental import pallas as pl
from jax.experimental.pallas import tpu as pltpu
from jax.sharding import PartitionSpec as P

STEPS = 4
LANES = 128
BF = jnp.bfloat16
F32 = jnp.float32
I32 = jnp.int32
VMEM = pl.BlockSpec(memory_space=pltpu.VMEM)
SMEM = pl.BlockSpec(memory_space=pltpu.SMEM)
HBM = pl.BlockSpec(memory_space=pltpu.HBM)


def round_up(value, unit):
    return -(-value // unit) * unit


def iota(shape, dim):
    return lax.broadcasted_iota(I32, shape, dim)


def split_2(value):
    high = value.astype(BF)
    return high, (value - high.astype(F32)).astype(BF)


def split_3(value):
    high = value.astype(BF)
    rest = value - high.astype(F32)
    middle = rest.astype(BF)
    return high, middle, (rest - middle.astype(F32)).astype(BF)


def stacked(value):
    high, low = split_2(value)
    return jnp.concatenate([high, low], axis=0)


def folded(value):
    half = value.shape[0] // 2
    return value[:half] + value[half:]


def dot(left, right):
    return jnp.dot(left, right, preferred_element_type=F32)


def one_hot(mask):
    return jnp.where(mask, 1.0, 0.0).astype(BF)


def padded_index(nodes, width, padded):
    block = jnp.floor((nodes + 0.5) * (1.0 / width))
    return nodes + block * (padded - width)


class Sizes:
    def __init__(self, inverse_blocks, voltage, wave_init, line_node, conv_node):
        self.blocks, self.picks, self.width, _ = inverse_blocks.shape
        self.scen, self.nodes = voltage.shape
        self.delays = wave_init.shape[0]
        self.ends = line_node.shape[0]
        self.lines = self.ends // 2
        self.convs = conv_node.shape[0]
        self.regions = lax.axis_size("region")
        self.capacity = max(2, 12 * self.convs // (5 * self.regions))
        self.rows = round_up(self.capacity + 4, 8)
        self.slots = self.regions * self.rows
        self.slot_lanes = round_up(self.slots, LANES)
        self.padded = round_up(self.width, LANES)
        self.lanes = self.blocks * self.padded
        self.group = math.lcm(self.width, LANES) // self.width

        self.state = (self.blocks, self.scen, self.padded)
        self.wide = (2 * self.scen, self.lanes)
        self.weights = (self.blocks, self.picks * self.width, 2 * self.padded)
        self.site_rows = (self.lanes, self.ends)
        self.response = (self.blocks, self.ends, 2 * self.padded)
        self.coupling = (self.ends, 2 * self.ends)
        self.node_rows = (self.blocks, 8, self.padded)
        self.fault_cols = (2, self.scen, self.padded)
        self.drive = (self.scen, self.ends)
        self.exchange = (self.scen, self.lines)


class Copies:
    def __init__(self, sems):
        self.sems = sems
        self.count = 0

    def start(self, source, target):
        copy = pltpu.make_async_copy(source, target, self.sems.at[self.count])
        self.count += 1
        copy.start()
        return copy


def pad_blocks(size, source, store):
    group_width = size.group * size.width
    for first in range(0, size.blocks, size.group):
        chunk = source[:, first * size.width : first * size.width + group_width]
        for j in range(size.group):
            part = chunk[:, j * size.width : (j + 1) * size.width]
            zeros = jnp.zeros((part.shape[0], size.padded - size.width), part.dtype)
            store(first + j, jnp.concatenate([part, zeros], axis=1))


def unpad_blocks(size, load, target):
    group_width = size.group * size.width
    for first in range(0, size.blocks, size.group):
        parts = [load(first + j)[:, : size.width] for j in range(size.group)]
        target[:, first * size.width : first * size.width + group_width] = jnp.concatenate(
            parts, axis=1
        )


def block_lanes(size, b):
    return slice(b * size.padded, (b + 1) * size.padded)


def pack_kernel(size, table_hbm, init_hbm, out, dst_out, table, init, sems):
    convs, slots = size.convs, size.slots
    copies = Copies(sems)
    first = copies.start(table_hbm, table)
    second = copies.start(init_hbm, init)
    first.wait()
    target = table[0:1, :].astype(I32)
    member = iota((round_up(size.regions, 16), convs), 0) == target
    before = one_hot(iota((convs, convs), 0) < iota((convs, convs), 1))
    earlier = dot(one_hot(member), before)
    rank = jnp.sum(jnp.where(member, earlier, 0.0), axis=0, keepdims=True)
    dst = target * size.rows + rank.astype(I32)
    dst_out[...] = dst
    select = one_hot(iota((slots, convs), 0) == dst)
    settings = jnp.concatenate([table[1:5, :], jnp.zeros((LANES - 4, convs), F32)], axis=0)
    second.wait()
    state = jnp.concatenate([init[0], init[1]], axis=0)
    payload = jnp.concatenate([state.T, settings.T], axis=1)
    width = state.shape[0]
    rows = sum(dot(select, part) for part in split_3(payload))
    for r in range(size.regions):
        chunk = rows[r * size.rows : (r + 1) * size.rows]
        out[r] = chunk[:, :width]
        filler = jnp.zeros((LANES - size.rows, LANES), F32)
        turned = jnp.concatenate([chunk[:, width:], filler], axis=0).T
        out[r, size.capacity : size.capacity + 4, :] = turned[:4]


def fault_terms(size, node, kind):
    first = lax.axis_index("region") * size.nodes
    local = (node[...] - first).astype(F32)
    inside = (local >= 0.0) & (local < size.nodes)
    site = jnp.where(inside, padded_index(local, size.width, size.padded), -1.0)
    level = 0.25 * jnp.left_shift(1, kind[...]).astype(F32)
    square = (size.scen, size.scen)
    diagonal = iota(square, 0) == iota(square, 1)

    def column(row):
        spread = jnp.where(diagonal, jnp.broadcast_to(row, square), 0.0)
        return jnp.broadcast_to(jnp.sum(spread, axis=1, keepdims=True), (size.scen, size.padded))

    return column(site), column(level)


def turned_row(row):
    return jnp.broadcast_to(row, (LANES, row.shape[1])).T


def picked_product(size, cols, b, x, wp):
    zeros = jnp.zeros((size.padded - size.width, 2 * size.padded), BF)
    left = jnp.concatenate([x[cols[k, b]] for k in range(size.picks)], axis=1)
    parts = []
    for k in range(size.picks):
        parts += [wp[b, k * size.width : (k + 1) * size.width, :], zeros]
    return dot(left, jnp.concatenate(parts, axis=0))


def three_terms(product, rows, width):
    top, low = product[:rows], product[rows:]
    return top[:, :width] + top[:, width:] + low[:, :width]


def apply_inverse(size, cols, x, wp, volt, vb):
    def block_row(b, carry):
        value = three_terms(picked_product(size, cols, b, x, wp), size.scen, size.padded)
        volt[b] = value
        vb[:, pl.ds(pl.multiple_of(b * size.padded, LANES), size.padded)] = stacked(value)
        return carry

    lax.fori_loop(0, size.blocks, block_row, 0, unroll=8)


def prep_kernel(
    size,
    cols_hbm, inverse, source, decay, gain, voltage, branch_init, line_node, fault_node, fault_kind,
    wp_out, eg_out, mt_out, kk_out, vb_out, branch_out, rest_out, rows_out, fault_out,
    cols, raw, vectors, volt_in, branch_in, nodes, faults,
    wp, eg, es, mt, both, kk, vb, volt, branch, rest, node_rows, fault_cols,
    sems,
):
    copies = Copies(sems)
    cols_copy = copies.start(cols_hbm, cols)
    small = [
        copies.start(line_node, nodes),
        copies.start(fault_node, faults.at[0:1]),
        copies.start(fault_kind, faults.at[1:2]),
    ]
    small += [copies.start(v, vectors.at[i]) for i, v in enumerate((source, decay, gain))]
    large = [copies.start(voltage, volt_in), copies.start(branch_init, branch_in)]
    stages = 4
    stage = size.blocks // stages
    weight_copies = []
    for i in range(stages):
        part = pl.ds(i * stage, stage)
        weight_copies.append(copies.start(inverse.at[part], raw.at[part]))
    sent = []
    for copy in small:
        copy.wait()

    row = padded_index(nodes[...].astype(F32), size.width, size.padded)
    for c in range(0, size.ends, LANES):
        part = row[:, c : c + LANES]
        down_delta = part - iota((LANES, LANES), 0).astype(F32)
        across_delta = turned_row(part) - iota((LANES, LANES), 1).astype(F32)
        for n in range(0, size.lanes, LANES):
            eg[n : n + LANES, c : c + LANES] = one_hot(down_delta == float(n))
            b, lane = n // size.padded, n % size.padded
            es[b, c : c + LANES, lane : lane + LANES] = one_hot(across_delta == float(n))
    sent.append(copies.start(eg, eg_out))

    for i in range(3):
        def put_row(b, value, i=i):
            node_rows[b, i : i + 1, :] = value

        pad_blocks(size, vectors.at[i], put_row)
    sent.append(copies.start(node_rows, rows_out))
    site, level = fault_terms(size, faults.at[0:1], faults.at[1:2])
    fault_cols[0] = site
    fault_cols[1] = level
    sent.append(copies.start(fault_cols, fault_out))
    for copy in large:
        copy.wait()

    def put_voltage(b, value):
        volt[b] = value
        vb[:, block_lanes(size, b)] = stacked(value)

    def put_branch(b, value):
        history = node_rows[b, 1:2, :] * value + node_rows[b, 2:3, :] * volt[b]
        branch[b] = history
        rest[b] = rest_of(size, node_rows, b, history, volt[b], site, level)

    pad_blocks(size, volt_in, put_voltage)
    pad_blocks(size, branch_in, put_branch)
    sent.append(copies.start(vb, vb_out))
    sent.append(copies.start(branch, branch_out))
    sent.append(copies.start(rest, rest_out))

    cols_copy.wait()
    for i, copy in enumerate(weight_copies):
        copy.wait()

        def turn(b, carry):
            for k in range(size.picks):
                high, low = split_2(raw[b, k].T)
                zeros = jnp.zeros((size.width, size.padded - size.width), BF)
                wp[b, k * size.width : (k + 1) * size.width, :] = jnp.concatenate(
                    [high, zeros, low, zeros], axis=1
                )
            return carry

        lax.fori_loop(i * stage, (i + 1) * stage, turn, 0, unroll=2)
        part = pl.ds(i * stage, stage)
        sent.append(copies.start(wp.at[part], wp_out.at[part]))

    def respond(b, carry):
        product = picked_product(size, cols, b, es, wp)
        high, low = split_2(product[:, : size.padded] + product[:, size.padded :])
        mt[b] = jnp.concatenate([high, low], axis=1)
        both[:, pl.ds(pl.multiple_of(b * size.padded, LANES), size.padded)] = jnp.concatenate(
            [high, low], axis=0
        )
        return carry

    lax.fori_loop(0, size.blocks, respond, 0, unroll=4)
    sent.append(copies.start(mt, mt_out))
    high, low = split_2(folded(dot(both[...], eg[...])))
    kk[...] = jnp.concatenate([high, low], axis=1)
    sent.append(copies.start(kk, kk_out))
    for copy in sent:
        copy.wait()


def rest_of(size, node_rows, b, history, v, site, level):
    lane = iota((size.scen, size.padded), 1).astype(F32)
    hit = jnp.where(lane + float(b * size.padded) == site, level, 0.0)
    return node_rows[b, 0:1, :] - history - hit * v


def converter_update(size, vb, cg, prm, filt, amps):
    measured = folded(dot(vb[...], cg[...]))
    filtered = filt[...]
    filtered = filtered + prm[2:3, :] * (measured - filtered)
    current = amps[...]
    target = prm[0:1, :] * filtered / (1.0 + filtered * filtered)
    current = current + prm[1:2, :] * (target - current)
    filt[...] = filtered
    amps[...] = current
    return stacked(current)


def launch_part(size, history, ends, at_ends, kk, drive_out, up, down):
    drive = jnp.zeros(size.drive, F32)
    for d in range(size.delays):
        drive = jnp.where(ends[0:1, :] == float(d + 1), history(d), drive)
    drive_out[...] = drive
    answer = three_terms(dot(stacked(drive), kk[...]), size.scen, size.ends)
    launch = 2.0 * ends[1:2, :] * (at_ends + answer) - drive
    up[...] = launch[:, size.lines :]
    down[...] = launch[:, : size.lines]


def start_kernel(
    size,
    cols_hbm, received_hbm, waves_hbm, delay_hbm, admittance_hbm,
    wp_hbm, eg_hbm, mt_hbm, kk_hbm, vb_hbm, branch_hbm, rest_hbm, rows_hbm, fault_hbm,
    wp, eg, mt, kk, waves, ends, node_rows, fault_cols, branch, cg, cs, prm, filt, amps, volt,
    peak, drive, up, down,
    cols, received, line_rows, rest, x, vb, sems,
):
    copies = Copies(sems)
    received_copy = copies.start(received_hbm, received)
    vb_copy = copies.start(vb_hbm, vb)
    rest_copy = copies.start(rest_hbm, rest)
    cols_copy = copies.start(cols_hbm, cols)
    wp_copy = copies.start(wp_hbm, wp)
    later = [
        copies.start(eg_hbm, eg),
        copies.start(delay_hbm, line_rows.at[0]),
        copies.start(admittance_hbm, line_rows.at[1]),
        copies.start(waves_hbm, waves),
        copies.start(kk_hbm, kk),
        copies.start(mt_hbm, mt),
        copies.start(branch_hbm, branch),
        copies.start(rows_hbm, node_rows),
        copies.start(fault_hbm, fault_cols),
    ]
    rows, capacity, slots, regions = size.rows, size.capacity, size.slots, size.regions
    received_copy.wait()
    settings = [
        received[r * rows + capacity : r * rows + capacity + 4, :rows] for r in range(regions)
    ]
    spare = size.slot_lanes - slots
    if spare:
        settings.append(jnp.zeros((4, spare), F32))
    prm[0:4, :] = jnp.concatenate(settings, axis=1)
    for c in range(0, size.slot_lanes, LANES):
        count = min(LANES, slots - c)
        within = lax.rem(iota((count, 2 * size.scen), 0) + c, rows)
        piece = jnp.where(within < capacity, received[c : c + count, :], 0.0)
        if count < LANES:
            piece = jnp.concatenate([piece, jnp.zeros((LANES - count, 2 * size.scen), F32)], axis=0)
        turned = piece.T
        filt[:, c : c + LANES] = turned[: size.scen]
        amps[:, c : c + LANES] = turned[size.scen :]
    row = padded_index(prm[3:4, :], size.width, size.padded)
    for c in range(0, size.slot_lanes, LANES):
        part = row[:, c : c + LANES]
        down_delta = part - iota((LANES, LANES), 0).astype(F32)
        across_delta = turned_row(part) - iota((LANES, LANES), 1).astype(F32)
        for n in range(0, size.lanes, LANES):
            cg[n : n + LANES, c : c + LANES] = one_hot(down_delta == float(n))
            cs[c : c + LANES, n : n + LANES] = one_hot(across_delta == float(n))
    peak[...] = jnp.zeros(peak.shape, F32)

    vb_copy.wait()
    pair = converter_update(size, vb, cg, prm, filt, amps)
    rest_copy.wait()
    for b in range(size.blocks):
        injected = folded(dot(pair, cs[:, block_lanes(size, b)]))
        x[b] = stacked(rest[b] + injected)
    cols_copy.wait()
    wp_copy.wait()
    apply_inverse(size, cols, x, wp, volt, vb)
    for copy in later:
        copy.wait()
    ends[0:1, :] = line_rows[0].astype(F32)
    ends[1:2, :] = line_rows[1]
    at_ends = folded(dot(vb[...], eg[...]))
    launch_part(size, lambda d: waves[d], ends, at_ends, kk, drive, up, down)


def middle_kernel(
    size, last,
    cols_hbm, drive, wp, eg, mt, node_rows, fault_cols, cg, cs, prm,
    branch_in, filt_in, amps_in, volt_in, peak_in,
    branch, filt, amps, volt, peak, at_ends, *refs,
):
    if last:
        back, branch_out = refs[:2]
    cols, x, vb, sem = refs[-4:]
    cols_copy = pltpu.make_async_copy(cols_hbm, cols, sem)
    cols_copy.start()
    pair = stacked(drive[...])
    for b in range(size.blocks):
        added = three_terms(dot(pair, mt[b]), size.scen, size.padded)
        v = volt[b] + added
        volt[b] = v
        vb[:, block_lanes(size, b)] = stacked(v)
        magnitude = jnp.abs(v)
        top = magnitude[:8]
        for s in range(8, size.scen, 8):
            top = jnp.maximum(top, magnitude[s : s + 8])
        peak[b] = jnp.maximum(peak[b], top)
    pair = converter_update(size, vb, cg, prm, filt, amps)
    site, level = fault_cols[0], fault_cols[1]
    for b in range(size.blocks):
        injected = folded(dot(pair, cs[:, block_lanes(size, b)]))
        history = node_rows[b, 1:2, :] * branch[b] + node_rows[b, 2:3, :] * volt[b]
        branch[b] = history
        x[b] = stacked(rest_of(size, node_rows, b, history, volt[b], site, level) + injected)
    cols_copy.wait()
    apply_inverse(size, cols, x, wp, volt, vb)
    at_ends[...] = folded(dot(vb[...], eg[...]))
    if last:
        for c in range(0, size.slot_lanes, LANES):
            count = min(LANES, size.slots - c)
            part = jnp.concatenate([filt[:, c : c + LANES], amps[:, c : c + LANES]], axis=0)
            back[c : c + count, :] = part.T[:count]
        unpad_blocks(size, lambda b: branch[b], branch_out)


def launch_kernel(size, done, last, at_ends, kk, ends, waves, *refs):
    arrivals, refs = refs[: 2 * done], refs[2 * done :]

    def history(d):
        if d >= done:
            return waves[d - done]
        return jnp.concatenate([arrivals[2 * d][...], arrivals[2 * d + 1][...]], axis=1)

    if last:
        back, refs = refs[0], refs[1:]
    drive, up, down = refs[:3]
    if last:
        chunks, waves_out, recent, sems = refs[3:]
        copies = Copies(sems)
        sent = [copies.start(back, chunks)]
        for d in range(done):
            recent[d] = history(d)
        sent.append(copies.start(recent, waves_out.at[pl.ds(1, done)]))
        kept = size.delays - 1 - done
        sent.append(copies.start(waves.at[pl.ds(0, kept)], waves_out.at[pl.ds(1 + done, kept)]))
    launch_part(size, history, ends, at_ends[...], kk, drive, up, down)
    if last:
        for copy in sent:
            copy.wait()


def final_kernel(size, drive, volt_hbm, mt_hbm, peak_hbm, voltage_out, peak_out, volt, mt, peak, sems):
    copies = Copies(sems)
    half = size.blocks // 2
    parts = []
    for i in range(2):
        part = pl.ds(i * half, half)
        parts.append(
            [copies.start(volt_hbm.at[part], volt.at[part]), copies.start(mt_hbm.at[part], mt.at[part])]
        )
    peak_copy = copies.start(peak_hbm, peak)
    pair = stacked(drive[...])
    for b in range(size.blocks):
        if b % half == 0:
            for copy in parts[b // half]:
                copy.wait()
        volt[b] = volt[b] + three_terms(dot(pair, mt[b]), size.scen, size.padded)
    unpad_blocks(size, lambda b: volt[b], voltage_out)
    peak_copy.wait()

    def largest(b):
        top = jnp.max(jnp.abs(volt[b]), axis=0, keepdims=True)
        return jnp.maximum(top, jnp.max(peak[b], axis=0, keepdims=True))

    unpad_blocks(size, largest, peak_out)


def end_kernel(size, peaks, dst_hbm, received_hbm, ahead, after, waves_in, *refs):
    own, refs = refs[:peaks], refs[peaks:]
    state_out, waves_out, envelope_out, dst, received, newest, tops, sems = refs
    copies = Copies(sems)
    received_copy = copies.start(received_hbm, received)
    dst_copy = copies.start(dst_hbm, dst)
    top_copies = [copies.start(ref, tops.at[i]) for i, ref in enumerate(own)]
    lines = size.lines
    newest[0, :, :lines] = ahead[...]
    newest[0, :, lines:] = after[...]
    newest_copy = copies.start(newest, waves_out.at[pl.ds(0, 1)])
    for copy in top_copies:
        copy.wait()
    top = tops[0]
    for i in range(1, peaks):
        top = jnp.maximum(top, tops[i])
    envelope_out[...] = top
    dst_copy.wait()
    select = one_hot(iota((size.slots, size.convs), 0) == dst[...])
    received_copy.wait()
    parts = jnp.concatenate(split_3(received[...].T), axis=0)
    state = dot(parts, select)
    width = 2 * size.scen
    state = state[:width] + state[width : 2 * width] + state[2 * width :]
    state_out[0] = state[: size.scen]
    state_out[1] = state[size.scen :]
    newest_copy.wait()


def shape(dims, dtype=F32):
    return jax.ShapeDtypeStruct(dims, dtype)


def in_vmem(*values):
    return [pltpu.with_memory_space_constraint(v, pltpu.VMEM) for v in values]


def call(kernel, name, outs, out_specs, args, specs, scratch, limit, aliases=None):
    return pl.pallas_call(
        kernel,
        name=name,
        out_shape=outs,
        in_specs=specs,
        out_specs=out_specs,
        scratch_shapes=list(scratch),
        input_output_aliases=aliases or {},
        compiler_params=pltpu.CompilerParams(vmem_limit_bytes=limit << 20),
    )(*args)


def shards(
    inverse_blocks, block_cols, source_current, node_decay, node_gain, voltage_init, branch_init,
    wave_init, line_node, line_delay, line_admittance, conv_region, conv_node, conv_power,
    conv_gains, conv_init, fault_node, fault_kind,
):
    size = Sizes(inverse_blocks, voltage_init, wave_init, line_node, conv_node)
    regions, rows, scen = size.regions, size.rows, size.scen
    ring = [(i, (i + 1) % regions) for i in range(regions)]
    back_ring = [(j, i) for i, j in ring]
    dma = pltpu.SemaphoreType.DMA
    vmem = pltpu.VMEM

    def row(vector):
        return vector.reshape(1, -1)

    table = jnp.stack(
        [
            conv_region[:, 0].astype(F32),
            conv_power,
            conv_gains[0],
            conv_gains[1],
            conv_node.astype(F32),
        ]
    )
    table = jnp.concatenate([table, jnp.zeros((3, size.convs), F32)], axis=0)
    packed, dst = call(
        functools.partial(pack_kernel, size),
        "pack",
        [shape((regions, rows, 2 * scen)), shape((1, size.convs), I32)],
        [VMEM] * 2,
        [table, conv_init],
        [HBM] * 2,
        [vmem(table.shape, F32), vmem(conv_init.shape, F32), dma((2,))],
        16,
    )
    received = lax.all_to_all(packed, "region", split_axis=0, concat_axis=0, tiled=True)
    received = received.reshape(size.slots, 2 * scen)

    cols = block_cols.T
    cols_scratch = pltpu.SMEM(cols.shape, I32)
    x_scratch = vmem((size.blocks, 2 * scen, size.padded), BF)
    wide_scratch = vmem(size.wide, BF)
    kept = [
        (size.weights, BF),
        (size.site_rows, BF),
        (size.response, BF),
        (size.coupling, BF),
        (size.wide, BF),
        (size.state, F32),
        (size.state, F32),
        (size.node_rows, F32),
        (size.fault_cols, F32),
    ]
    vectors = (3, 1, size.nodes)
    args = [
        cols, inverse_blocks, row(source_current), row(node_decay), row(node_gain), voltage_init,
        branch_init, row(line_node), row(fault_node), row(fault_kind),
    ]
    wp_hbm, eg_hbm, mt_hbm, kk_hbm, vb_hbm, branch_hbm, rest_hbm, rows_hbm, fault_hbm = call(
        functools.partial(prep_kernel, size),
        "prep",
        [shape(*item) for item in kept],
        [HBM] * len(kept),
        args,
        [HBM] * len(args),
        [
            cols_scratch,
            vmem(inverse_blocks.shape, F32),
            vmem(vectors, F32),
            vmem(voltage_init.shape, F32),
            vmem(voltage_init.shape, F32),
            vmem((1, size.ends), I32),
            vmem((2, scen), I32),
            vmem(size.weights, BF),
            vmem(size.site_rows, BF),
            vmem((size.blocks, size.ends, size.padded), BF),
            vmem(size.response, BF),
            vmem((2 * size.ends, size.lanes), BF),
            vmem(size.coupling, BF),
            wide_scratch,
            vmem(size.state, F32),
            vmem(size.state, F32),
            vmem(size.state, F32),
            vmem(size.node_rows, F32),
            vmem(size.fault_cols, F32),
            dma((40,)),
        ],
        48,
    )

    slot_state = vmem((scen, size.slot_lanes), F32)
    outs = [
        vmem(size.weights, BF),
        vmem(size.site_rows, BF),
        vmem(size.response, BF),
        vmem(size.coupling, BF),
        vmem(wave_init.shape, F32),
        vmem((8, size.ends), F32),
        vmem(size.node_rows, F32),
        vmem(size.fault_cols, F32),
        vmem(size.state, F32),
        vmem((size.lanes, size.slot_lanes), BF),
        vmem((size.slot_lanes, size.lanes), BF),
        vmem((8, size.slot_lanes), F32),
        slot_state,
        slot_state,
        vmem(size.state, F32),
        vmem(size.node_rows, F32),
        vmem(size.drive, F32),
        shape(size.exchange),
        shape(size.exchange),
    ]
    args = [
        cols, received, wave_init, row(line_delay.astype(F32)), row(line_admittance), wp_hbm, eg_hbm,
        mt_hbm, kk_hbm, vb_hbm, branch_hbm, rest_hbm, rows_hbm, fault_hbm,
    ]
    (
        wp, eg, mt, kk, waves, ends, node_rows, fault_cols, branch, cg, cs, prm, filt, amps, volt,
        peak, drive, up, down,
    ) = call(
        functools.partial(start_kernel, size),
        "start",
        outs,
        [VMEM] * len(outs),
        args,
        [HBM] * len(args),
        [
            cols_scratch,
            vmem((size.slots, 2 * scen), F32),
            vmem((2, 1, size.ends), F32),
            vmem(size.state, F32),
            x_scratch,
            wide_scratch,
            dma((16,)),
        ],
        10,
    )

    arrivals = []
    for step in range(1, STEPS):
        last = step == STEPS - 1
        from_ahead = lax.ppermute(up, "region", ring)
        from_after = lax.ppermute(down, "region", back_ring)
        outs = [
            vmem(size.state, F32),
            slot_state,
            slot_state,
            vmem(size.state, F32),
            vmem(size.node_rows, F32),
            vmem(size.drive, F32),
        ]
        if last:
            outs += [vmem((size.slots, 2 * scen), F32), shape((scen, size.nodes))]
        result = call(
            functools.partial(middle_kernel, size, last),
            "middle",
            outs,
            [VMEM] * len(outs),
            [cols]
            + in_vmem(
                drive, wp, eg, mt, node_rows, fault_cols, cg, cs, prm, branch, filt, amps, volt, peak
            ),
            [HBM] + [VMEM] * 14,
            [cols_scratch, x_scratch, wide_scratch, dma],
            8,
            {10: 0, 11: 1, 12: 2, 13: 3, 14: 4},
        )
        branch, filt, amps, volt, peak, at_ends = result[:6]
        arrivals = [from_ahead, from_after] + arrivals
        args = in_vmem(at_ends, kk, ends, waves) + arrivals
        outs = [vmem(size.drive, F32), shape(size.exchange), shape(size.exchange)]
        specs, scratch = [VMEM] * 3, []
        if last:
            back, branch_out = result[6:]
            args += in_vmem(back)
            outs[0] = shape(size.drive)
            outs += [shape((size.slots, 2 * scen)), shape(wave_init.shape)]
            specs += [HBM, HBM]
            scratch = [vmem((step, *size.drive), F32), dma((3,))]
        drive, up, down, *rest = call(
            functools.partial(launch_kernel, size, step, last),
            "launch",
            outs,
            specs,
            args,
            [VMEM] * len(args),
            scratch,
            4,
        )
    chunks, waves_out = rest
    from_ahead = lax.ppermute(up, "region", ring)
    from_after = lax.ppermute(down, "region", back_ring)
    chunks = chunks.reshape(regions, rows, 2 * scen)
    returned = lax.all_to_all(chunks, "region", split_axis=0, concat_axis=0, tiled=True)
    voltage_out, peak_out = call(
        functools.partial(final_kernel, size),
        "final",
        [shape((scen, size.nodes)), shape((1, size.nodes))],
        [VMEM] * 2,
        [drive, volt, mt_hbm, peak],
        [VMEM, HBM, HBM, HBM],
        [
            vmem(size.state, F32),
            vmem(size.response, BF),
            vmem(size.node_rows, F32),
            dma((5,)),
        ],
        12,
    )
    others = lax.axis_size("scen")
    peaks = [peak_out] + [
        lax.ppermute(peak_out, "scen", [(i, (i + d) % others) for i in range(others)])
        for d in range(1, others)
    ]
    returned = returned.reshape(size.slots, 2 * scen)
    args = [dst, returned, from_ahead, from_after, waves_out] + peaks
    conv_state, wave_history, envelope = call(
        functools.partial(end_kernel, size, len(peaks)),
        "end",
        [shape(conv_init.shape), shape(wave_init.shape), shape((1, size.nodes))],
        [VMEM, HBM, VMEM],
        args,
        [HBM, HBM, VMEM, VMEM] + [HBM] * (len(args) - 4),
        [
            vmem(dst.shape, I32),
            vmem(returned.shape, F32),
            vmem((1, *size.drive), F32),
            vmem((others, 1, size.nodes), F32),
            dma((3 + others,)),
        ],
        16,
        {4: 1},
    )
    return voltage_out, branch_out, wave_history, conv_state, envelope.reshape(-1)


def solution(mesh):
    placed = (
        P("region", None, None, None),
        P("region", None),
        P("region"),
        P("region"),
        P("region"),
        P("scen", "region"),
        P("scen", "region"),
        P(None, "scen", "region"),
        P("region"),
        P("region"),
        P("region"),
        P("region", None),
        P("region"),
        P("region"),
        P(None, "region"),
        P(None, "scen", "region"),
        P("scen"),
        P("scen"),
    )
    return jax.shard_map(
        shards,
        mesh=mesh,
        in_specs=placed,
        out_specs=(
            P("scen", "region"),
            P("scen", "region"),
            P(None, "scen", "region"),
            P(None, "scen", "region"),
            P("region"),
        ),
        check_vma=False,
    )
```

```python
import functools
import math

import jax
import jax.numpy as jnp
from jax import lax
from jax.experimental import pallas as pl
from jax.experimental.pallas import tpu as pltpu
from jax.sharding import PartitionSpec as P

STEPS = 4
LANES = 128
BF = jnp.bfloat16
F32 = jnp.float32
I32 = jnp.int32
VMEM = pl.BlockSpec(memory_space=pltpu.VMEM)
SMEM = pl.BlockSpec(memory_space=pltpu.SMEM)
HBM = pl.BlockSpec(memory_space=pltpu.HBM)


def round_up(value, unit):
    return -(-value // unit) * unit


def iota(shape, dim):
    return lax.broadcasted_iota(I32, shape, dim)


def split_2(value):
    high = value.astype(BF)
    return high, (value - high.astype(F32)).astype(BF)


def split_3(value):
    high = value.astype(BF)
    rest = value - high.astype(F32)
    middle = rest.astype(BF)
    return high, middle, (rest - middle.astype(F32)).astype(BF)


def stacked(value):
    high, low = split_2(value)
    return jnp.concatenate([high, low], axis=0)


def folded(value):
    half = value.shape[0] // 2
    return value[:half] + value[half:]


def dot(left, right):
    return jnp.dot(left, right, preferred_element_type=F32)


def one_hot(mask):
    return jnp.where(mask, 1.0, 0.0).astype(BF)


def padded_index(nodes, width, padded):
    block = jnp.floor((nodes + 0.5) * (1.0 / width))
    return nodes + block * (padded - width)


class Sizes:
    def __init__(self, inverse_blocks, voltage, wave_init, line_node, conv_node):
        self.blocks, self.picks, self.width, _ = inverse_blocks.shape
        self.scen, self.nodes = voltage.shape
        self.delays = wave_init.shape[0]
        self.ends = line_node.shape[0]
        self.lines = self.ends // 2
        self.convs = conv_node.shape[0]
        self.regions = lax.axis_size("region")
        self.capacity = max(2, 12 * self.convs // (5 * self.regions))
        self.rows = round_up(self.capacity + 4, 8)
        self.slots = self.regions * self.rows
        self.slot_lanes = round_up(self.slots, LANES)
        self.padded = round_up(self.width, LANES)
        self.lanes = self.blocks * self.padded
        self.group = math.lcm(self.width, LANES) // self.width

        self.state = (self.blocks, self.scen, self.padded)
        self.wide = (2 * self.scen, self.lanes)
        self.weights = (self.blocks, self.picks * self.width, 2 * self.padded)
        self.site_rows = (self.lanes, self.ends)
        self.response = (self.blocks, self.ends, 2 * self.padded)
        self.coupling = (self.ends, 2 * self.ends)
        self.node_rows = (self.blocks, 8, self.padded)
        self.fault_cols = (2, self.scen, self.padded)
        self.drive = (self.scen, self.ends)
        self.exchange = (self.scen, self.lines)


class Copies:
    def __init__(self, sems):
        self.sems = sems
        self.count = 0

    def start(self, source, target):
        copy = pltpu.make_async_copy(source, target, self.sems.at[self.count])
        self.count += 1
        copy.start()
        return copy


def pad_blocks(size, source, store):
    group_width = size.group * size.width
    for first in range(0, size.blocks, size.group):
        chunk = source[:, first * size.width : first * size.width + group_width]
        for j in range(size.group):
            part = chunk[:, j * size.width : (j + 1) * size.width]
            zeros = jnp.zeros((part.shape[0], size.padded - size.width), part.dtype)
            store(first + j, jnp.concatenate([part, zeros], axis=1))


def unpad_blocks(size, load, target):
    group_width = size.group * size.width
    for first in range(0, size.blocks, size.group):
        parts = [load(first + j)[:, : size.width] for j in range(size.group)]
        target[:, first * size.width : first * size.width + group_width] = jnp.concatenate(
            parts, axis=1
        )


def block_lanes(size, b):
    return slice(b * size.padded, (b + 1) * size.padded)


def pack_kernel(
    size, region_hbm, table_hbm, gains_hbm, init_hbm, out_hbm, dst_hbm,
    region, table, gains, init, out, dst_out, sems,
):
    convs, slots = size.convs, size.slots
    copies = Copies(sems)
    first = copies.start(region_hbm, region)
    second = copies.start(init_hbm, init)
    others = [copies.start(table_hbm, table), copies.start(gains_hbm, gains)]
    first.wait()
    target = region[...]
    member = iota((round_up(size.regions, 16), convs), 0) == target
    before = one_hot(iota((convs, convs), 0) < iota((convs, convs), 1))
    earlier = dot(one_hot(member), before)
    rank = jnp.sum(jnp.where(member, earlier, 0.0), axis=0, keepdims=True)
    dst = target * size.rows + rank.astype(I32)
    dst_out[...] = dst
    select = one_hot(iota((slots, convs), 0) == dst)
    sent = [copies.start(dst_out, dst_hbm)]
    for copy in others:
        copy.wait()
    settings = jnp.concatenate(
        [table[0:1, :], gains[...], table[1:2, :], jnp.zeros((LANES - 4, convs), F32)], axis=0
    )
    second.wait()
    state = jnp.concatenate([init[0], init[1]], axis=0)
    payload = jnp.concatenate([state.T, settings.T], axis=1)
    width = state.shape[0]
    rows = sum(dot(select, part) for part in split_3(payload))
    for r in range(size.regions):
        chunk = rows[r * size.rows : (r + 1) * size.rows]
        out[r] = chunk[:, :width]
        filler = jnp.zeros((LANES - size.rows, LANES), F32)
        turned = jnp.concatenate([chunk[:, width:], filler], axis=0).T
        out[r, size.capacity : size.capacity + 4, :] = turned[:4]
    sent.append(copies.start(out, out_hbm))
    for copy in sent:
        copy.wait()


def fault_terms(size, node, kind):
    first = lax.axis_index("region") * size.nodes
    local = (node[...] - first).astype(F32)
    inside = (local >= 0.0) & (local < size.nodes)
    site = jnp.where(inside, padded_index(local, size.width, size.padded), -1.0)
    level = 0.25 * jnp.left_shift(1, kind[...]).astype(F32)
    square = (size.scen, size.scen)
    diagonal = iota(square, 0) == iota(square, 1)

    def column(row):
        spread = jnp.where(diagonal, jnp.broadcast_to(row, square), 0.0)
        return jnp.broadcast_to(jnp.sum(spread, axis=1, keepdims=True), (size.scen, size.padded))

    return column(site), column(level)


def site_products(size, row, chunk, gather, scatter):
    part = row[:, chunk : chunk + LANES]
    block = jnp.floor((part + 0.5) * (1.0 / LANES))
    lane = part - block * LANES
    square = (LANES, LANES)
    down_block = jnp.broadcast_to(block, square).astype(BF)
    across_block = turned_row(block).astype(BF)
    down_lane = one_hot(lane == iota(square, 0).astype(F32))
    across_lane = one_hot(turned_row(lane) == iota(square, 1).astype(F32))
    zeros = jnp.zeros(square, BF)
    for n in range(size.lanes // LANES):
        here = jnp.asarray(n, BF)
        gather(n, jnp.where(down_block == here, down_lane, zeros))
        scatter(n, jnp.where(across_block == here, across_lane, zeros))


def turned_row(row):
    return jnp.broadcast_to(row, (LANES, row.shape[1])).T


def picked_product(size, cols, b, x, wp):
    zeros = jnp.zeros((size.padded - size.width, 2 * size.padded), BF)
    left = jnp.concatenate([x[cols[k, b]] for k in range(size.picks)], axis=1)
    parts = []
    for k in range(size.picks):
        parts += [wp[b, k * size.width : (k + 1) * size.width, :], zeros]
    return dot(left, jnp.concatenate(parts, axis=0))


def three_terms(product, rows, width):
    top, low = product[:rows], product[rows:]
    return top[:, :width] + top[:, width:] + low[:, :width]


def apply_inverse(size, cols, x, wp, volt, vb):
    def block_row(b, carry):
        value = three_terms(picked_product(size, cols, b, x, wp), size.scen, size.padded)
        volt[b] = value
        vb[:, pl.ds(pl.multiple_of(b * size.padded, LANES), size.padded)] = stacked(value)
        return carry

    lax.fori_loop(0, size.blocks, block_row, 0, unroll=8)


def prep_kernel(
    size,
    cols_hbm, inverse, source, decay, gain, voltage, branch_init, line_node, fault_node, fault_kind,
    wp_out, eg_out, mt_out, kk_out, vb_out, branch_out, rest_out, rows_out, fault_out,
    cols, raw, vectors, volt_in, branch_in, nodes, faults,
    wp, eg, es, mt, both, kk, vb, volt, branch, rest, node_rows, fault_cols,
    sems,
):
    copies = Copies(sems)
    cols_copy = copies.start(cols_hbm, cols)
    small = [
        copies.start(line_node, nodes),
        copies.start(fault_node, faults.at[0:1]),
        copies.start(fault_kind, faults.at[1:2]),
    ]
    small += [copies.start(v, vectors.at[i]) for i, v in enumerate((source, decay, gain))]
    large = [copies.start(voltage, volt_in), copies.start(branch_init, branch_in)]
    stages = 4
    stage = size.blocks // stages
    weight_copies = []
    for i in range(stages):
        part = pl.ds(i * stage, stage)
        weight_copies.append(copies.start(inverse.at[part], raw.at[part]))
    sent = []
    for copy in small:
        copy.wait()

    row = padded_index(nodes[...].astype(F32), size.width, size.padded)
    for c in range(0, size.ends, LANES):
        def put_gather(n, value, c=c):
            eg[n * LANES : (n + 1) * LANES, c : c + LANES] = value

        def put_scatter(n, value, c=c):
            b, lane = n * LANES // size.padded, n * LANES % size.padded
            es[b, c : c + LANES, lane : lane + LANES] = value

        site_products(size, row, c, put_gather, put_scatter)
    sent.append(copies.start(eg, eg_out))

    for i in range(3):
        def put_row(b, value, i=i):
            node_rows[b, i : i + 1, :] = value

        pad_blocks(size, vectors.at[i], put_row)
    sent.append(copies.start(node_rows, rows_out))
    site, level = fault_terms(size, faults.at[0:1], faults.at[1:2])
    fault_cols[0] = site
    fault_cols[1] = level
    sent.append(copies.start(fault_cols, fault_out))
    for copy in large:
        copy.wait()

    def put_voltage(b, value):
        volt[b] = value
        vb[:, block_lanes(size, b)] = stacked(value)

    def put_branch(b, value):
        history = node_rows[b, 1:2, :] * value + node_rows[b, 2:3, :] * volt[b]
        branch[b] = history
        rest[b] = rest_of(size, node_rows, b, history, volt[b], site, level)

    pad_blocks(size, volt_in, put_voltage)
    pad_blocks(size, branch_in, put_branch)
    sent.append(copies.start(vb, vb_out))
    sent.append(copies.start(branch, branch_out))
    sent.append(copies.start(rest, rest_out))

    cols_copy.wait()
    for i, copy in enumerate(weight_copies):
        copy.wait()

        def turn(b, carry):
            for k in range(size.picks):
                high, low = split_2(raw[b, k].T)
                zeros = jnp.zeros((size.width, size.padded - size.width), BF)
                wp[b, k * size.width : (k + 1) * size.width, :] = jnp.concatenate(
                    [high, zeros, low, zeros], axis=1
                )
            return carry

        lax.fori_loop(i * stage, (i + 1) * stage, turn, 0, unroll=2)
        part = pl.ds(i * stage, stage)
        sent.append(copies.start(wp.at[part], wp_out.at[part]))

    def respond(b, carry):
        product = picked_product(size, cols, b, es, wp)
        high, low = split_2(product[:, : size.padded] + product[:, size.padded :])
        mt[b] = jnp.concatenate([high, low], axis=1)
        both[:, pl.ds(pl.multiple_of(b * size.padded, LANES), size.padded)] = jnp.concatenate(
            [high, low], axis=0
        )
        return carry

    lax.fori_loop(0, size.blocks, respond, 0, unroll=4)
    sent.append(copies.start(mt, mt_out))
    high, low = split_2(folded(dot(both[...], eg[...])))
    kk[...] = jnp.concatenate([high, low], axis=1)
    sent.append(copies.start(kk, kk_out))
    for copy in sent:
        copy.wait()


def rest_of(size, node_rows, b, history, v, site, level):
    lane = iota((size.scen, size.padded), 1).astype(F32)
    hit = jnp.where(lane + float(b * size.padded) == site, level, 0.0)
    return node_rows[b, 0:1, :] - history - hit * v


def converter_update(size, vb, cg, prm, filt, amps):
    measured = folded(dot(vb[...], cg[...]))
    filtered = filt[...]
    filtered = filtered + prm[2:3, :] * (measured - filtered)
    current = amps[...]
    target = prm[0:1, :] * filtered / (1.0 + filtered * filtered)
    current = current + prm[1:2, :] * (target - current)
    filt[...] = filtered
    amps[...] = current
    return stacked(current)


def launch_part(size, history, ends, at_ends, kk, drive_out, up, down):
    drive = jnp.zeros(size.drive, F32)
    for d in range(size.delays):
        drive = jnp.where(ends[0:1, :] == float(d + 1), history(d), drive)
    drive_out[...] = drive
    answer = three_terms(dot(stacked(drive), kk[...]), size.scen, size.ends)
    launch = 2.0 * ends[1:2, :] * (at_ends + answer) - drive
    up[...] = launch[:, size.lines :]
    down[...] = launch[:, : size.lines]


def start_kernel(
    size,
    cols_hbm, received_hbm, waves_hbm, delay_hbm, admittance_hbm,
    wp_hbm, eg_hbm, mt_hbm, kk_hbm, vb_hbm, branch_hbm, rest_hbm, rows_hbm, fault_hbm,
    wp, eg, mt, kk, waves, ends, node_rows, fault_cols, branch, cg, cs, prm, filt, amps, volt,
    peak, drive, up, down,
    cols, received, delays, admittances, rest, x, vb, sems,
):
    copies = Copies(sems)
    received_copy = copies.start(received_hbm, received)
    vb_copy = copies.start(vb_hbm, vb)
    rest_copy = copies.start(rest_hbm, rest)
    cols_copy = copies.start(cols_hbm, cols)
    wp_copy = copies.start(wp_hbm, wp)
    later = [
        copies.start(eg_hbm, eg),
        copies.start(delay_hbm, delays),
        copies.start(admittance_hbm, admittances),
        copies.start(waves_hbm, waves),
        copies.start(kk_hbm, kk),
        copies.start(mt_hbm, mt),
        copies.start(branch_hbm, branch),
        copies.start(rows_hbm, node_rows),
        copies.start(fault_hbm, fault_cols),
    ]
    rows, capacity, slots, regions = size.rows, size.capacity, size.slots, size.regions
    received_copy.wait()
    settings = [
        received[r * rows + capacity : r * rows + capacity + 4, :rows] for r in range(regions)
    ]
    spare = size.slot_lanes - slots
    if spare:
        settings.append(jnp.zeros((4, spare), F32))
    prm[0:4, :] = jnp.concatenate(settings, axis=1)
    for c in range(0, size.slot_lanes, LANES):
        count = min(LANES, slots - c)
        within = lax.rem(iota((count, 2 * size.scen), 0) + c, rows)
        piece = jnp.where(within < capacity, received[c : c + count, :], 0.0)
        if count < LANES:
            piece = jnp.concatenate([piece, jnp.zeros((LANES - count, 2 * size.scen), F32)], axis=0)
        turned = piece.T
        filt[:, c : c + LANES] = turned[: size.scen]
        amps[:, c : c + LANES] = turned[size.scen :]
    row = padded_index(prm[3:4, :], size.width, size.padded)
    for c in range(0, size.slot_lanes, LANES):
        def put_gather(n, value, c=c):
            cg[n * LANES : (n + 1) * LANES, c : c + LANES] = value

        def put_scatter(n, value, c=c):
            cs[c : c + LANES, n * LANES : (n + 1) * LANES] = value

        site_products(size, row, c, put_gather, put_scatter)
    peak[...] = jnp.zeros(peak.shape, F32)

    vb_copy.wait()
    pair = converter_update(size, vb, cg, prm, filt, amps)
    rest_copy.wait()
    for b in range(size.blocks):
        injected = folded(dot(pair, cs[:, block_lanes(size, b)]))
        x[b] = stacked(rest[b] + injected)
    cols_copy.wait()
    wp_copy.wait()
    apply_inverse(size, cols, x, wp, volt, vb)
    for copy in later:
        copy.wait()
    ends[0:1, :] = delays[...].astype(F32)
    ends[1:2, :] = admittances[...]
    at_ends = folded(dot(vb[...], eg[...]))
    launch_part(size, lambda d: waves[d], ends, at_ends, kk, drive, up, down)


def middle_kernel(
    size, last,
    cols_hbm, drive, wp, eg, mt, node_rows, fault_cols, cg, cs, prm,
    branch_in, filt_in, amps_in, volt_in, peak_in,
    branch, filt, amps, volt, peak, at_ends, *refs,
):
    if last:
        back, branch_hbm, volt_hbm, peak_hbm, branch_out = *refs[:4], refs[-1]
        refs = refs[4:-1]
    cols, x, vb, sems = refs
    copies = Copies(sems)
    cols_copy = copies.start(cols_hbm, cols)
    pair = stacked(drive[...])
    for b in range(size.blocks):
        added = three_terms(dot(pair, mt[b]), size.scen, size.padded)
        v = volt[b] + added
        volt[b] = v
        vb[:, block_lanes(size, b)] = stacked(v)
        magnitude = jnp.abs(v)
        top = magnitude[:8]
        for s in range(8, size.scen, 8):
            top = jnp.maximum(top, magnitude[s : s + 8])
        peak[b] = jnp.maximum(peak[b], top)
    pair = converter_update(size, vb, cg, prm, filt, amps)
    site, level = fault_cols[0], fault_cols[1]
    for b in range(size.blocks):
        injected = folded(dot(pair, cs[:, block_lanes(size, b)]))
        history = node_rows[b, 1:2, :] * branch[b] + node_rows[b, 2:3, :] * volt[b]
        branch[b] = history
        x[b] = stacked(rest_of(size, node_rows, b, history, volt[b], site, level) + injected)
    cols_copy.wait()
    if last:
        unpad_blocks(size, lambda b: branch[b], branch_out)
        sent = [copies.start(branch_out, branch_hbm), copies.start(peak, peak_hbm)]
    apply_inverse(size, cols, x, wp, volt, vb)
    if last:
        sent.append(copies.start(volt, volt_hbm))
    at_ends[...] = folded(dot(vb[...], eg[...]))
    if last:
        for c in range(0, size.slot_lanes, LANES):
            count = min(LANES, size.slots - c)
            part = jnp.concatenate([filt[:, c : c + LANES], amps[:, c : c + LANES]], axis=0)
            back[c : c + count, :] = part.T[:count]
        for copy in sent:
            copy.wait()


def launch_kernel(size, done, last, at_ends, kk, ends, waves, *refs):
    arrivals, refs = refs[: 2 * done], refs[2 * done :]

    def history(d):
        if d >= done:
            return waves[d - done]
        return jnp.concatenate([arrivals[2 * d][...], arrivals[2 * d + 1][...]], axis=1)

    if last:
        back, refs = refs[0], refs[1:]
    drive, up, down = refs[:3]
    if last:
        drive_hbm = drive
        chunks, waves_out, recent, drive, sems = refs[3:]
        copies = Copies(sems)
        sent = [copies.start(back, chunks)]
        for d in range(done):
            recent[d] = history(d)
        sent.append(copies.start(recent, waves_out.at[pl.ds(1, done)]))
        kept = size.delays - 1 - done
        sent.append(copies.start(waves.at[pl.ds(0, kept)], waves_out.at[pl.ds(1 + done, kept)]))
    launch_part(size, history, ends, at_ends[...], kk, drive, up, down)
    if last:
        sent.append(copies.start(drive, drive_hbm))
        for copy in sent:
            copy.wait()


def final_kernel(
    size, drive_hbm, volt_hbm, mt_hbm, peak_hbm, voltage_hbm, top_hbm,
    drive, volt, mt, peak, voltage_out, peak_out, sems,
):
    copies = Copies(sems)
    drive_copy = copies.start(drive_hbm, drive)
    half = size.blocks // 2
    parts = []
    for i in range(2):
        part = pl.ds(i * half, half)
        parts.append(
            [copies.start(volt_hbm.at[part], volt.at[part]), copies.start(mt_hbm.at[part], mt.at[part])]
        )
    peak_copy = copies.start(peak_hbm, peak)
    drive_copy.wait()
    pair = stacked(drive[...])
    for b in range(size.blocks):
        if b % half == 0:
            for copy in parts[b // half]:
                copy.wait()
        volt[b] = volt[b] + three_terms(dot(pair, mt[b]), size.scen, size.padded)
    peak_copy.wait()

    def largest(b):
        top = jnp.max(jnp.abs(volt[b]), axis=0, keepdims=True)
        return jnp.maximum(top, jnp.max(peak[b], axis=0, keepdims=True))

    unpad_blocks(size, largest, peak_out)
    sent = [copies.start(peak_out, top_hbm)]
    unpad_blocks(size, lambda b: volt[b], voltage_out)
    sent.append(copies.start(voltage_out, voltage_hbm))
    for copy in sent:
        copy.wait()


def end_kernel(size, peaks, dst_hbm, received_hbm, ahead, after, waves_in, *refs):
    own, refs = refs[:peaks], refs[peaks:]
    (
        state_hbm, waves_out, envelope_hbm,
        dst, received, newest, arrived, tops, state_out, envelope_out, sems,
    ) = refs
    copies = Copies(sems)
    received_copy = copies.start(received_hbm, received)
    dst_copy = copies.start(dst_hbm, dst)
    top_copies = [copies.start(ref, tops.at[i]) for i, ref in enumerate(own)]
    lines = size.lines
    arrived_copies = [copies.start(ahead, arrived.at[0]), copies.start(after, arrived.at[1])]
    for copy in arrived_copies:
        copy.wait()
    newest[0, :, :lines] = arrived[0]
    newest[0, :, lines:] = arrived[1]
    sent = [copies.start(newest, waves_out.at[pl.ds(0, 1)])]
    for copy in top_copies:
        copy.wait()
    top = tops[0]
    for i in range(1, peaks):
        top = jnp.maximum(top, tops[i])
    envelope_out[...] = top
    sent.append(copies.start(envelope_out, envelope_hbm))
    dst_copy.wait()
    select = one_hot(iota((size.slots, size.convs), 0) == dst[...])
    received_copy.wait()
    parts = jnp.concatenate(split_3(received[...].T), axis=0)
    state = dot(parts, select)
    width = 2 * size.scen
    state = state[:width] + state[width : 2 * width] + state[2 * width :]
    state_out[0] = state[: size.scen]
    state_out[1] = state[size.scen :]
    sent.append(copies.start(state_out, state_hbm))
    for copy in sent:
        copy.wait()


def shape(dims, dtype=F32):
    return jax.ShapeDtypeStruct(dims, dtype)


def in_vmem(*values):
    return [pltpu.with_memory_space_constraint(v, pltpu.VMEM) for v in values]


def in_hbm(*values):
    return [pltpu.with_memory_space_constraint(v, pltpu.HBM) for v in values]


def call(kernel, name, outs, out_specs, args, specs, scratch, limit, aliases=None):
    return pl.pallas_call(
        kernel,
        name=name,
        out_shape=outs,
        in_specs=specs,
        out_specs=out_specs,
        scratch_shapes=list(scratch),
        input_output_aliases=aliases or {},
        compiler_params=pltpu.CompilerParams(vmem_limit_bytes=limit << 20),
    )(*args)


def shards(
    inverse_blocks, block_cols, source_current, node_decay, node_gain, voltage_init, branch_init,
    wave_init, line_node, line_delay, line_admittance, conv_region, conv_node, conv_power,
    conv_gains, conv_init, fault_node, fault_kind,
):
    size = Sizes(inverse_blocks, voltage_init, wave_init, line_node, conv_node)
    regions, rows, scen = size.regions, size.rows, size.scen
    ring = [(i, (i + 1) % regions) for i in range(regions)]
    back_ring = [(j, i) for i, j in ring]
    dma = pltpu.SemaphoreType.DMA
    vmem, hbm = pltpu.VMEM, pltpu.HBM

    def row(vector):
        return vector.reshape(1, -1)

    first_row = jnp.arange(2, dtype=I32)[:, None] == 0
    table = jnp.where(first_row, conv_power[None, :], conv_node.astype(F32)[None, :])
    chunk = (regions, rows, 2 * scen)
    packed, dst = call(
        functools.partial(pack_kernel, size),
        "pack",
        [hbm(chunk, F32), hbm((1, size.convs), I32)],
        [HBM] * 2,
        in_hbm(row(conv_region), table, conv_gains, conv_init),
        [HBM] * 4,
        [
            vmem((1, size.convs), I32),
            vmem(table.shape, F32),
            vmem(conv_gains.shape, F32),
            vmem(conv_init.shape, F32),
            vmem(chunk, F32),
            vmem((1, size.convs), I32),
            dma((6,)),
        ],
        16,
    )
    received = lax.all_to_all(packed, "region", split_axis=0, concat_axis=0, tiled=True)
    received = received.reshape(size.slots, 2 * scen)

    cols = block_cols.T
    cols_scratch = pltpu.SMEM(cols.shape, I32)
    x_scratch = vmem((size.blocks, 2 * scen, size.padded), BF)
    wide_scratch = vmem(size.wide, BF)
    kept = [
        (size.weights, BF),
        (size.site_rows, BF),
        (size.response, BF),
        (size.coupling, BF),
        (size.wide, BF),
        (size.state, F32),
        (size.state, F32),
        (size.node_rows, F32),
        (size.fault_cols, F32),
    ]
    vectors = (3, 1, size.nodes)
    args = [
        cols, inverse_blocks, row(source_current), row(node_decay), row(node_gain), voltage_init,
        branch_init, row(line_node), row(fault_node), row(fault_kind),
    ]
    wp_hbm, eg_hbm, mt_hbm, kk_hbm, vb_hbm, branch_hbm, rest_hbm, rows_hbm, fault_hbm = call(
        functools.partial(prep_kernel, size),
        "prep",
        [hbm(*item) for item in kept],
        [HBM] * len(kept),
        in_hbm(*args),
        [HBM] * len(args),
        [
            cols_scratch,
            vmem(inverse_blocks.shape, F32),
            vmem(vectors, F32),
            vmem(voltage_init.shape, F32),
            vmem(voltage_init.shape, F32),
            vmem((1, size.ends), I32),
            vmem((2, scen), I32),
            vmem(size.weights, BF),
            vmem(size.site_rows, BF),
            vmem((size.blocks, size.ends, size.padded), BF),
            vmem(size.response, BF),
            vmem((2 * size.ends, size.lanes), BF),
            vmem(size.coupling, BF),
            wide_scratch,
            vmem(size.state, F32),
            vmem(size.state, F32),
            vmem(size.state, F32),
            vmem(size.node_rows, F32),
            vmem(size.fault_cols, F32),
            dma((40,)),
        ],
        48,
    )

    slot_state = vmem((scen, size.slot_lanes), F32)
    outs = [
        vmem(size.weights, BF),
        vmem(size.site_rows, BF),
        vmem(size.response, BF),
        vmem(size.coupling, BF),
        vmem(wave_init.shape, F32),
        vmem((8, size.ends), F32),
        vmem(size.node_rows, F32),
        vmem(size.fault_cols, F32),
        vmem(size.state, F32),
        vmem((size.lanes, size.slot_lanes), BF),
        vmem((size.slot_lanes, size.lanes), BF),
        vmem((8, size.slot_lanes), F32),
        slot_state,
        slot_state,
        vmem(size.state, F32),
        vmem(size.node_rows, F32),
        vmem(size.drive, F32),
        shape(size.exchange),
        shape(size.exchange),
    ]
    args = [
        cols, received, wave_init, row(line_delay), row(line_admittance), wp_hbm, eg_hbm,
        mt_hbm, kk_hbm, vb_hbm, branch_hbm, rest_hbm, rows_hbm, fault_hbm,
    ]
    (
        wp, eg, mt, kk, waves, ends, node_rows, fault_cols, branch, cg, cs, prm, filt, amps, volt,
        peak, drive, up, down,
    ) = call(
        functools.partial(start_kernel, size),
        "start",
        outs,
        [VMEM] * len(outs),
        in_hbm(*args),
        [HBM] * len(args),
        [
            cols_scratch,
            vmem((size.slots, 2 * scen), F32),
            vmem((1, size.ends), I32),
            vmem((1, size.ends), F32),
            vmem(size.state, F32),
            x_scratch,
            wide_scratch,
            dma((16,)),
        ],
        10,
    )

    arrivals = []
    for step in range(1, STEPS):
        last = step == STEPS - 1
        from_ahead = lax.ppermute(up, "region", ring)
        from_after = lax.ppermute(down, "region", back_ring)
        outs = [
            vmem(size.state, F32),
            slot_state,
            slot_state,
            vmem(size.state, F32),
            vmem(size.node_rows, F32),
            vmem(size.drive, F32),
        ]
        specs = [VMEM] * len(outs)
        scratch = [cols_scratch, x_scratch, wide_scratch, dma((4,))]
        if last:
            outs += [
                vmem((size.slots, 2 * scen), F32),
                hbm((scen, size.nodes), F32),
                hbm(size.state, F32),
                hbm(size.node_rows, F32),
            ]
            specs += [VMEM, HBM, HBM, HBM]
            scratch.append(vmem((scen, size.nodes), F32))
        result = call(
            functools.partial(middle_kernel, size, last),
            "middle",
            outs,
            specs,
            in_hbm(cols)
            + in_vmem(
                drive, wp, eg, mt, node_rows, fault_cols, cg, cs, prm, branch, filt, amps, volt, peak
            ),
            [HBM] + [VMEM] * 14,
            scratch,
            8,
            {10: 0, 11: 1, 12: 2, 13: 3, 14: 4},
        )
        branch, filt, amps, volt, peak, at_ends = result[:6]
        arrivals = [from_ahead, from_after] + arrivals
        args = in_vmem(at_ends, kk, ends, waves) + arrivals
        outs = [vmem(size.drive, F32), shape(size.exchange), shape(size.exchange)]
        specs, scratch = [VMEM] * 3, []
        if last:
            back, branch_out, volt, peak = result[6:]
            args += in_vmem(back)
            outs[0] = hbm(size.drive, F32)
            outs += [hbm((size.slots, 2 * scen), F32), hbm(wave_init.shape, F32)]
            specs[0] = HBM
            specs += [HBM, HBM]
            scratch = [vmem((step, *size.drive), F32), vmem(size.drive, F32), dma((4,))]
        drive, up, down, *rest = call(
            functools.partial(launch_kernel, size, step, last),
            "launch",
            outs,
            specs,
            args,
            [VMEM] * len(args),
            scratch,
            4,
        )
    chunks, waves_out = rest
    from_ahead = lax.ppermute(up, "region", ring)
    from_after = lax.ppermute(down, "region", back_ring)
    chunks = chunks.reshape(regions, rows, 2 * scen)
    returned = lax.all_to_all(chunks, "region", split_axis=0, concat_axis=0, tiled=True)
    voltage_out, peak_out = call(
        functools.partial(final_kernel, size),
        "final",
        [hbm((scen, size.nodes), F32), hbm((1, size.nodes), F32)],
        [HBM] * 2,
        in_hbm(drive, volt, mt_hbm, peak),
        [HBM] * 4,
        [
            vmem(size.drive, F32),
            vmem(size.state, F32),
            vmem(size.response, BF),
            vmem(size.node_rows, F32),
            vmem((scen, size.nodes), F32),
            vmem((1, size.nodes), F32),
            dma((8,)),
        ],
        12,
    )
    others = lax.axis_size("scen")
    peaks = [peak_out] + [
        lax.ppermute(peak_out, "scen", [(i, (i + d) % others) for i in range(others)])
        for d in range(1, others)
    ]
    returned = returned.reshape(size.slots, 2 * scen)
    args = [dst, returned, from_ahead, from_after, waves_out] + peaks
    conv_state, wave_history, envelope = call(
        functools.partial(end_kernel, size, len(peaks)),
        "end",
        [hbm(conv_init.shape, F32), hbm(wave_init.shape, F32), hbm((1, size.nodes), F32)],
        [HBM] * 3,
        in_hbm(*args),
        [HBM] * len(args),
        [
            vmem(dst.shape, I32),
            vmem(returned.shape, F32),
            vmem((1, *size.drive), F32),
            vmem((2, *size.exchange), F32),
            vmem((others, 1, size.nodes), F32),
            vmem(conv_init.shape, F32),
            vmem((1, size.nodes), F32),
            dma((7 + others,)),
        ],
        16,
        {4: 1},
    )
    return voltage_out, branch_out, wave_history, conv_state, envelope.reshape(-1)


def solution(mesh):
    placed = (
        P("region", None, None, None),
        P("region", None),
        P("region"),
        P("region"),
        P("region"),
        P("scen", "region"),
        P("scen", "region"),
        P(None, "scen", "region"),
        P("region"),
        P("region"),
        P("region"),
        P("region", None),
        P("region"),
        P("region"),
        P(None, "region"),
        P(None, "scen", "region"),
        P("scen"),
        P("scen"),
    )
    return jax.shard_map(
        shards,
        mesh=mesh,
        in_specs=placed,
        out_specs=(
            P("scen", "region"),
            P("scen", "region"),
            P(None, "scen", "region"),
            P(None, "scen", "region"),
            P("region"),
        ),
        check_vma=False,
    )
```

```python
import functools
import math

import jax
import jax.numpy as jnp
from jax import lax
from jax.experimental import pallas as pl
from jax.experimental.pallas import tpu as pltpu
from jax.sharding import PartitionSpec as P

STEPS = 4
LANES = 128
BF = jnp.bfloat16
F32 = jnp.float32
I32 = jnp.int32
VMEM = pl.BlockSpec(memory_space=pltpu.VMEM)
SMEM = pl.BlockSpec(memory_space=pltpu.SMEM)
HBM = pl.BlockSpec(memory_space=pltpu.HBM)


def round_up(value, unit):
    return -(-value // unit) * unit


def iota(shape, dim):
    return lax.broadcasted_iota(I32, shape, dim)


def split_2(value):
    high = value.astype(BF)
    return high, (value - high.astype(F32)).astype(BF)


def split_3(value):
    high = value.astype(BF)
    rest = value - high.astype(F32)
    middle = rest.astype(BF)
    return high, middle, (rest - middle.astype(F32)).astype(BF)


def stacked(value):
    high, low = split_2(value)
    return jnp.concatenate([high, low], axis=0)


def folded(value):
    half = value.shape[0] // 2
    return value[:half] + value[half:]


def dot(left, right):
    return jnp.dot(left, right, preferred_element_type=F32)


def one_hot(mask):
    return jnp.where(mask, 1.0, 0.0).astype(BF)


def padded_index(nodes, width, padded):
    block = jnp.floor((nodes + 0.5) * (1.0 / width))
    return nodes + block * (padded - width)


class Sizes:
    def __init__(self, inverse_blocks, voltage, wave_init, line_node, conv_node):
        self.blocks, self.picks, self.width, _ = inverse_blocks.shape
        self.scen, self.nodes = voltage.shape
        self.delays = wave_init.shape[0]
        self.ends = line_node.shape[0]
        self.lines = self.ends // 2
        self.convs = conv_node.shape[0]
        self.regions = lax.axis_size("region")
        self.capacity = max(2, 12 * self.convs // (5 * self.regions))
        self.rows = round_up(self.capacity + 4, 8)
        self.slots = self.regions * self.rows
        self.slot_lanes = round_up(self.slots, LANES)
        self.padded = round_up(self.width, LANES)
        self.lanes = self.blocks * self.padded
        self.group = math.lcm(self.width, LANES) // self.width

        self.state = (self.blocks, self.scen, self.padded)
        self.wide = (2 * self.scen, self.lanes)
        self.weights = (self.blocks, self.picks * self.width, 2 * self.padded)
        self.site_rows = (self.lanes, self.ends)
        self.response = (self.blocks, self.ends, 2 * self.padded)
        self.coupling = (self.ends, 2 * self.ends)
        self.node_rows = (self.blocks, 8, self.padded)
        self.fault_cols = (2, self.scen, self.padded)
        self.drive = (self.scen, self.ends)
        self.exchange = (self.scen, self.lines)


class Copies:
    def __init__(self, sems):
        self.sems = sems
        self.count = 0

    def start(self, source, target):
        copy = pltpu.make_async_copy(source, target, self.sems.at[self.count])
        self.count += 1
        copy.start()
        return copy


def pad_blocks(size, source, store):
    group_width = size.group * size.width
    for first in range(0, size.blocks, size.group):
        chunk = source[:, first * size.width : first * size.width + group_width]
        for j in range(size.group):
            part = chunk[:, j * size.width : (j + 1) * size.width]
            zeros = jnp.zeros((part.shape[0], size.padded - size.width), part.dtype)
            store(first + j, jnp.concatenate([part, zeros], axis=1))


def unpad_blocks(size, load, target):
    group_width = size.group * size.width
    for first in range(0, size.blocks, size.group):
        parts = [load(first + j)[:, : size.width] for j in range(size.group)]
        target[:, first * size.width : first * size.width + group_width] = jnp.concatenate(
            parts, axis=1
        )


def block_lanes(size, b):
    return slice(b * size.padded, (b + 1) * size.padded)


def pack_kernel(
    size, region_hbm, power_hbm, node_hbm, gains_hbm, init_hbm, out_hbm, dst_hbm,
    region, power, node, gains, init, out, dst_out, sems,
):
    convs, slots = size.convs, size.slots
    copies = Copies(sems)
    first = copies.start(region_hbm, region)
    second = copies.start(init_hbm, init)
    others = [
        copies.start(power_hbm, power),
        copies.start(node_hbm, node),
        copies.start(gains_hbm, gains),
    ]
    first.wait()
    target = region[...]
    member = iota((round_up(size.regions, 16), convs), 0) == target
    before = one_hot(iota((convs, convs), 0) < iota((convs, convs), 1))
    earlier = dot(one_hot(member), before)
    rank = jnp.sum(jnp.where(member, earlier, 0.0), axis=0, keepdims=True)
    dst = target * size.rows + rank.astype(I32)
    dst_out[...] = dst
    select = one_hot(iota((slots, convs), 0) == dst)
    sent = [copies.start(dst_out, dst_hbm)]
    for copy in others:
        copy.wait()
    rows = [
        power[...].reshape(1, convs),
        gains[...],
        node[...].astype(F32).reshape(1, convs),
        jnp.zeros((LANES - 4, convs), F32),
    ]
    settings = jnp.concatenate(rows, axis=0)
    second.wait()
    state = jnp.concatenate([init[0], init[1]], axis=0)
    payload = jnp.concatenate([state.T, settings.T], axis=1)
    width = state.shape[0]
    rows = sum(dot(select, part) for part in split_3(payload))
    for r in range(size.regions):
        chunk = rows[r * size.rows : (r + 1) * size.rows]
        out[r] = chunk[:, :width]
        filler = jnp.zeros((LANES - size.rows, LANES), F32)
        turned = jnp.concatenate([chunk[:, width:], filler], axis=0).T
        out[r, size.capacity : size.capacity + 4, :] = turned[:4]
    sent.append(copies.start(out, out_hbm))
    for copy in sent:
        copy.wait()


def fault_terms(size, node, kind):
    first = lax.axis_index("region") * size.nodes
    local = (node[...] - first).astype(F32)
    inside = (local >= 0.0) & (local < size.nodes)
    site = jnp.where(inside, padded_index(local, size.width, size.padded), -1.0)
    level = 0.25 * jnp.left_shift(1, kind[...]).astype(F32)
    square = (size.scen, size.scen)
    diagonal = iota(square, 0) == iota(square, 1)

    def column(row):
        spread = jnp.where(diagonal, jnp.broadcast_to(row, square), 0.0)
        return jnp.broadcast_to(jnp.sum(spread, axis=1, keepdims=True), (size.scen, size.padded))

    return column(site), column(level)


def site_products(size, row, chunk, gather, scatter):
    part = row[:, chunk : chunk + LANES]
    block = jnp.floor((part + 0.5) * (1.0 / LANES))
    lane = part - block * LANES
    square = (LANES, LANES)
    down_block = jnp.broadcast_to(block, square).astype(BF)
    across_block = turned_row(block).astype(BF)
    down_lane = one_hot(lane == iota(square, 0).astype(F32))
    across_lane = one_hot(turned_row(lane) == iota(square, 1).astype(F32))
    zeros = jnp.zeros(square, BF)
    for n in range(size.lanes // LANES):
        here = jnp.asarray(n, BF)
        gather(n, jnp.where(down_block == here, down_lane, zeros))
        scatter(n, jnp.where(across_block == here, across_lane, zeros))


def turned_row(row):
    return jnp.broadcast_to(row, (LANES, row.shape[1])).T


def picked_product(size, cols, b, x, wp):
    zeros = jnp.zeros((size.padded - size.width, 2 * size.padded), BF)
    left = jnp.concatenate([x[cols[k, b]] for k in range(size.picks)], axis=1)
    parts = []
    for k in range(size.picks):
        parts += [wp[b, k * size.width : (k + 1) * size.width, :], zeros]
    return dot(left, jnp.concatenate(parts, axis=0))


def three_terms(product, rows, width):
    top, low = product[:rows], product[rows:]
    return top[:, :width] + top[:, width:] + low[:, :width]


def apply_inverse(size, cols, x, wp, volt, vb):
    def block_row(b, carry):
        value = three_terms(picked_product(size, cols, b, x, wp), size.scen, size.padded)
        volt[b] = value
        vb[:, pl.ds(pl.multiple_of(b * size.padded, LANES), size.padded)] = stacked(value)
        return carry

    lax.fori_loop(0, size.blocks, block_row, 0, unroll=8)


def prep_kernel(
    size,
    cols_hbm, inverse, source, decay, gain, voltage, branch_init, line_node, fault_node, fault_kind,
    wp_out, eg_out, mt_out, kk_out, vb_out, branch_out, rest_out, rows_out, fault_out,
    cols, raw, vectors, volt_in, branch_in, nodes, faults,
    wp, eg, es, mt, both, kk, vb, volt, branch, rest, node_rows, fault_cols,
    sems,
):
    copies = Copies(sems)
    cols_copy = copies.start(cols_hbm, cols)
    small = [
        copies.start(line_node, nodes),
        copies.start(fault_node, faults.at[0:1]),
        copies.start(fault_kind, faults.at[1:2]),
    ]
    small += [copies.start(v, vectors.at[i]) for i, v in enumerate((source, decay, gain))]
    large = [copies.start(voltage, volt_in), copies.start(branch_init, branch_in)]
    stages = 4
    stage = size.blocks // stages
    weight_copies = []
    for i in range(stages):
        part = pl.ds(i * stage, stage)
        weight_copies.append(copies.start(inverse.at[part], raw.at[part]))
    sent = []
    for copy in small:
        copy.wait()

    row = padded_index(nodes[...].astype(F32), size.width, size.padded)
    for c in range(0, size.ends, LANES):
        def put_gather(n, value, c=c):
            eg[n * LANES : (n + 1) * LANES, c : c + LANES] = value

        def put_scatter(n, value, c=c):
            b, lane = n * LANES // size.padded, n * LANES % size.padded
            es[b, c : c + LANES, lane : lane + LANES] = value

        site_products(size, row, c, put_gather, put_scatter)
    sent.append(copies.start(eg, eg_out))

    for i in range(3):
        def put_row(b, value, i=i):
            node_rows[b, i : i + 1, :] = value

        pad_blocks(size, vectors.at[i], put_row)
    sent.append(copies.start(node_rows, rows_out))
    site, level = fault_terms(size, faults.at[0:1], faults.at[1:2])
    fault_cols[0] = site
    fault_cols[1] = level
    sent.append(copies.start(fault_cols, fault_out))
    for copy in large:
        copy.wait()

    def put_voltage(b, value):
        volt[b] = value
        vb[:, block_lanes(size, b)] = stacked(value)

    def put_branch(b, value):
        history = node_rows[b, 1:2, :] * value + node_rows[b, 2:3, :] * volt[b]
        branch[b] = history
        rest[b] = rest_of(size, node_rows, b, history, volt[b], site, level)

    pad_blocks(size, volt_in, put_voltage)
    pad_blocks(size, branch_in, put_branch)
    sent.append(copies.start(vb, vb_out))
    sent.append(copies.start(branch, branch_out))
    sent.append(copies.start(rest, rest_out))

    cols_copy.wait()
    zeros = jnp.zeros((size.width, size.padded - size.width), BF)
    zero_rows = jnp.zeros((size.padded - size.width, 2 * size.padded), BF)
    for i, copy in enumerate(weight_copies):
        copy.wait()

        def turn(b, carry):
            parts = []
            for k in range(size.picks):
                high, low = split_2(raw[b, k].T)
                part = jnp.concatenate([high, zeros, low, zeros], axis=1)
                wp[b, k * size.width : (k + 1) * size.width, :] = part
                parts += [part, zero_rows]
            left = jnp.concatenate([es[cols[k, b]] for k in range(size.picks)], axis=1)
            product = dot(left, jnp.concatenate(parts, axis=0))
            high, low = split_2(product[:, : size.padded] + product[:, size.padded :])
            mt[b] = jnp.concatenate([high, low], axis=1)
            both[:, pl.ds(pl.multiple_of(b * size.padded, LANES), size.padded)] = jnp.concatenate(
                [high, low], axis=0
            )
            return carry

        lax.fori_loop(i * stage, (i + 1) * stage, turn, 0, unroll=4)
        part = pl.ds(i * stage, stage)
        sent.append(copies.start(wp.at[part], wp_out.at[part]))
        sent.append(copies.start(mt.at[part], mt_out.at[part]))

    high, low = split_2(folded(dot(both[...], eg[...])))
    kk[...] = jnp.concatenate([high, low], axis=1)
    sent.append(copies.start(kk, kk_out))
    for copy in sent:
        copy.wait()


def rest_of(size, node_rows, b, history, v, site, level):
    lane = iota((size.scen, size.padded), 1).astype(F32)
    hit = jnp.where(lane + float(b * size.padded) == site, level, 0.0)
    return node_rows[b, 0:1, :] - history - hit * v


def injections(size, pair, cs):
    step = 2 if size.blocks % 2 == 0 else 1
    for first in range(0, size.blocks, step):
        lanes = slice(first * size.padded, (first + step) * size.padded)
        both = folded(dot(pair, cs[:, lanes]))
        for j in range(step):
            yield first + j, both[:, block_lanes(size, j)]


def converter_update(size, vb, cg, prm, filt, amps):
    measured = folded(dot(vb[...], cg[...]))
    filtered = filt[...]
    filtered = filtered + prm[2:3, :] * (measured - filtered)
    current = amps[...]
    target = prm[0:1, :] * filtered / (1.0 + filtered * filtered)
    current = current + prm[1:2, :] * (target - current)
    filt[...] = filtered
    amps[...] = current
    return stacked(current)


def launch_part(size, history, ends, at_ends, kk, drive_out, up, down):
    drive = jnp.zeros(size.drive, F32)
    for d in range(size.delays):
        drive = jnp.where(ends[0:1, :] == float(d + 1), history(d), drive)
    drive_out[...] = drive
    answer = three_terms(dot(stacked(drive), kk[...]), size.scen, size.ends)
    launch = 2.0 * ends[1:2, :] * (at_ends + answer) - drive
    up[...] = launch[:, size.lines :]
    down[...] = launch[:, : size.lines]


def start_kernel(
    size,
    cols_hbm, received, waves_hbm, delay_hbm, admittance_hbm,
    wp_hbm, eg_hbm, mt_hbm, kk_hbm, vb_hbm, branch_hbm, rest_hbm, rows_hbm, fault_hbm,
    wp, eg, mt, kk, waves, ends, node_rows, fault_cols, branch, cg, cs, prm, filt, amps, volt,
    peak, drive, up, down,
    cols, delays, admittances, rest, x, vb, sems,
):
    copies = Copies(sems)
    vb_copy = copies.start(vb_hbm, vb)
    rest_copy = copies.start(rest_hbm, rest)
    cols_copy = copies.start(cols_hbm, cols)
    wp_copy = copies.start(wp_hbm, wp)
    later = [
        copies.start(eg_hbm, eg),
        copies.start(delay_hbm, delays),
        copies.start(admittance_hbm, admittances),
        copies.start(waves_hbm, waves),
        copies.start(kk_hbm, kk),
        copies.start(mt_hbm, mt),
        copies.start(branch_hbm, branch),
        copies.start(rows_hbm, node_rows),
        copies.start(fault_hbm, fault_cols),
    ]
    rows, capacity, slots, regions = size.rows, size.capacity, size.slots, size.regions
    settings = [
        received[r * rows + capacity : r * rows + capacity + 4, :rows] for r in range(regions)
    ]
    spare = size.slot_lanes - slots
    if spare:
        settings.append(jnp.zeros((4, spare), F32))
    prm[0:4, :] = jnp.concatenate(settings, axis=1)
    for c in range(0, size.slot_lanes, LANES):
        count = min(LANES, slots - c)
        within = lax.rem(iota((count, 2 * size.scen), 0) + c, rows)
        piece = jnp.where(within < capacity, received[c : c + count, :], 0.0)
        if count < LANES:
            piece = jnp.concatenate([piece, jnp.zeros((LANES - count, 2 * size.scen), F32)], axis=0)
        turned = piece.T
        filt[:, c : c + LANES] = turned[: size.scen]
        amps[:, c : c + LANES] = turned[size.scen :]
    row = padded_index(prm[3:4, :], size.width, size.padded)
    for c in range(0, size.slot_lanes, LANES):
        def put_gather(n, value, c=c):
            cg[n * LANES : (n + 1) * LANES, c : c + LANES] = value

        def put_scatter(n, value, c=c):
            cs[c : c + LANES, n * LANES : (n + 1) * LANES] = value

        site_products(size, row, c, put_gather, put_scatter)
    peak[...] = jnp.zeros(peak.shape, F32)

    vb_copy.wait()
    pair = converter_update(size, vb, cg, prm, filt, amps)
    rest_copy.wait()
    for b, injected in injections(size, pair, cs):
        x[b] = stacked(rest[b] + injected)
    cols_copy.wait()
    wp_copy.wait()
    apply_inverse(size, cols, x, wp, volt, vb)
    for copy in later:
        copy.wait()
    ends[0:1, :] = delays[...].astype(F32)
    ends[1:2, :] = admittances[...]
    at_ends = folded(dot(vb[...], eg[...]))
    launch_part(size, lambda d: waves[d], ends, at_ends, kk, drive, up, down)


def middle_kernel(
    size, last,
    cols_hbm, drive, wp, eg, mt, node_rows, fault_cols, cg, cs, prm,
    branch_in, filt_in, amps_in, volt_in, peak_in,
    branch, filt, amps, volt, peak, at_ends, *refs,
):
    if last:
        back, branch_hbm, volt_hbm, peak_hbm, branch_out = *refs[:4], refs[-1]
        refs = refs[4:-1]
    cols, x, vb, sems = refs
    copies = Copies(sems)
    cols_copy = copies.start(cols_hbm, cols)
    pair = stacked(drive[...])
    for b in range(size.blocks):
        added = three_terms(dot(pair, mt[b]), size.scen, size.padded)
        v = volt[b] + added
        volt[b] = v
        vb[:, block_lanes(size, b)] = stacked(v)
        magnitude = jnp.abs(v)
        top = magnitude[:8]
        for s in range(8, size.scen, 8):
            top = jnp.maximum(top, magnitude[s : s + 8])
        peak[b] = jnp.maximum(peak[b], top)
    pair = converter_update(size, vb, cg, prm, filt, amps)
    site, level = fault_cols[0], fault_cols[1]
    for b, injected in injections(size, pair, cs):
        history = node_rows[b, 1:2, :] * branch[b] + node_rows[b, 2:3, :] * volt[b]
        branch[b] = history
        x[b] = stacked(rest_of(size, node_rows, b, history, volt[b], site, level) + injected)
    cols_copy.wait()
    if last:
        unpad_blocks(size, lambda b: branch[b], branch_out)
        sent = [copies.start(branch_out, branch_hbm), copies.start(peak, peak_hbm)]
    apply_inverse(size, cols, x, wp, volt, vb)
    if last:
        sent.append(copies.start(volt, volt_hbm))
    at_ends[...] = folded(dot(vb[...], eg[...]))
    if last:
        for c in range(0, size.slot_lanes, LANES):
            count = min(LANES, size.slots - c)
            part = jnp.concatenate([filt[:, c : c + LANES], amps[:, c : c + LANES]], axis=0)
            back[c : c + count, :] = part.T[:count]
        for copy in sent:
            copy.wait()


def launch_kernel(size, done, last, at_ends, kk, ends, waves, *refs):
    arrivals, refs = refs[: 2 * done], refs[2 * done :]

    def history(d):
        if d >= done:
            return waves[d - done]
        return jnp.concatenate([arrivals[2 * d][...], arrivals[2 * d + 1][...]], axis=1)

    if last:
        back, refs = refs[0], refs[1:]
    drive, up, down = refs[:3]
    if last:
        drive_hbm = drive
        chunks, waves_out, recent, drive, sems = refs[3:]
        copies = Copies(sems)
        sent = [copies.start(back, chunks)]
        for d in range(done):
            recent[d] = history(d)
        sent.append(copies.start(recent, waves_out.at[pl.ds(1, done)]))
        kept = size.delays - 1 - done
        sent.append(copies.start(waves.at[pl.ds(0, kept)], waves_out.at[pl.ds(1 + done, kept)]))
    launch_part(size, history, ends, at_ends[...], kk, drive, up, down)
    if last:
        sent.append(copies.start(drive, drive_hbm))
        for copy in sent:
            copy.wait()


def final_kernel(
    size, drive_hbm, volt_hbm, mt_hbm, peak_hbm, voltage_hbm, top_hbm,
    drive, volt, mt, peak, voltage_out, peak_out, sems,
):
    copies = Copies(sems)
    drive_copy = copies.start(drive_hbm, drive)
    half = size.blocks // 2
    parts = []
    for i in range(2):
        part = pl.ds(i * half, half)
        parts.append(
            [copies.start(volt_hbm.at[part], volt.at[part]), copies.start(mt_hbm.at[part], mt.at[part])]
        )
    peak_copy = copies.start(peak_hbm, peak)
    drive_copy.wait()
    pair = stacked(drive[...])
    for b in range(size.blocks):
        if b % half == 0:
            for copy in parts[b // half]:
                copy.wait()
        volt[b] = volt[b] + three_terms(dot(pair, mt[b]), size.scen, size.padded)
    peak_copy.wait()

    def largest(b):
        top = jnp.max(jnp.abs(volt[b]), axis=0, keepdims=True)
        return jnp.maximum(top, jnp.max(peak[b], axis=0, keepdims=True))

    unpad_blocks(size, largest, peak_out)
    sent = [copies.start(peak_out, top_hbm)]
    unpad_blocks(size, lambda b: volt[b], voltage_out)
    sent.append(copies.start(voltage_out, voltage_hbm))
    for copy in sent:
        copy.wait()


def end_kernel(
    size, dst_hbm, received, ahead, after, waves_in, state_hbm, waves_out,
    dst, newest, state_out, sems,
):
    copies = Copies(sems)
    dst_copy = copies.start(dst_hbm, dst)
    newest[0, :, : size.lines] = ahead[...]
    newest[0, :, size.lines :] = after[...]
    sent = [copies.start(newest, waves_out.at[pl.ds(0, 1)])]
    parts = jnp.concatenate(split_3(received[...].T), axis=0)
    dst_copy.wait()
    select = one_hot(iota((size.slots, size.convs), 0) == dst[...])
    state = dot(parts, select)
    width = 2 * size.scen
    state = state[:width] + state[width : 2 * width] + state[2 * width :]
    state_out[0] = state[: size.scen]
    state_out[1] = state[size.scen :]
    sent.append(copies.start(state_out, state_hbm))
    for copy in sent:
        copy.wait()


def shape(dims, dtype=F32):
    return jax.ShapeDtypeStruct(dims, dtype)


def in_vmem(*values):
    return [pltpu.with_memory_space_constraint(v, pltpu.VMEM) for v in values]


def in_hbm(*values):
    return [pltpu.with_memory_space_constraint(v, pltpu.HBM) for v in values]


def call(kernel, name, outs, out_specs, args, specs, scratch, limit, aliases=None):
    return pl.pallas_call(
        kernel,
        name=name,
        out_shape=outs,
        in_specs=specs,
        out_specs=out_specs,
        scratch_shapes=list(scratch),
        input_output_aliases=aliases or {},
        compiler_params=pltpu.CompilerParams(vmem_limit_bytes=limit << 20),
    )(*args)


def shards(
    inverse_blocks, block_cols, source_current, node_decay, node_gain, voltage_init, branch_init,
    wave_init, line_node, line_delay, line_admittance, conv_region, conv_node, conv_power,
    conv_gains, conv_init, fault_node, fault_kind,
):
    size = Sizes(inverse_blocks, voltage_init, wave_init, line_node, conv_node)
    regions, rows, scen = size.regions, size.rows, size.scen
    ring = [(i, (i + 1) % regions) for i in range(regions)]
    back_ring = [(j, i) for i, j in ring]
    dma = pltpu.SemaphoreType.DMA
    vmem, hbm = pltpu.VMEM, pltpu.HBM

    def row(vector):
        return vector.reshape(1, -1)

    chunk = (regions, rows, 2 * scen)
    packed, dst = call(
        functools.partial(pack_kernel, size),
        "pack",
        [hbm(chunk, F32), hbm((1, size.convs), I32)],
        [HBM] * 2,
        in_hbm(row(conv_region), conv_power, conv_node, conv_gains, conv_init),
        [HBM] * 5,
        [
            vmem((1, size.convs), I32),
            vmem(conv_power.shape, F32),
            vmem(conv_node.shape, I32),
            vmem(conv_gains.shape, F32),
            vmem(conv_init.shape, F32),
            vmem(chunk, F32),
            vmem((1, size.convs), I32),
            dma((8,)),
        ],
        16,
    )
    received = lax.all_to_all(packed, "region", split_axis=0, concat_axis=0, tiled=True)
    received = received.reshape(size.slots, 2 * scen)

    cols = block_cols.T
    cols_scratch = pltpu.SMEM(cols.shape, I32)
    x_scratch = vmem((size.blocks, 2 * scen, size.padded), BF)
    wide_scratch = vmem(size.wide, BF)
    kept = [
        (size.weights, BF),
        (size.site_rows, BF),
        (size.response, BF),
        (size.coupling, BF),
        (size.wide, BF),
        (size.state, F32),
        (size.state, F32),
        (size.node_rows, F32),
        (size.fault_cols, F32),
    ]
    vectors = (3, 1, size.nodes)
    args = [
        cols, inverse_blocks, row(source_current), row(node_decay), row(node_gain), voltage_init,
        branch_init, row(line_node), row(fault_node), row(fault_kind),
    ]
    wp_hbm, eg_hbm, mt_hbm, kk_hbm, vb_hbm, branch_hbm, rest_hbm, rows_hbm, fault_hbm = call(
        functools.partial(prep_kernel, size),
        "prep",
        [hbm(*item) for item in kept],
        [HBM] * len(kept),
        in_hbm(*args),
        [HBM] * len(args),
        [
            cols_scratch,
            vmem(inverse_blocks.shape, F32),
            vmem(vectors, F32),
            vmem(voltage_init.shape, F32),
            vmem(voltage_init.shape, F32),
            vmem((1, size.ends), I32),
            vmem((2, scen), I32),
            vmem(size.weights, BF),
            vmem(size.site_rows, BF),
            vmem((size.blocks, size.ends, size.padded), BF),
            vmem(size.response, BF),
            vmem((2 * size.ends, size.lanes), BF),
            vmem(size.coupling, BF),
            wide_scratch,
            vmem(size.state, F32),
            vmem(size.state, F32),
            vmem(size.state, F32),
            vmem(size.node_rows, F32),
            vmem(size.fault_cols, F32),
            dma((40,)),
        ],
        48,
    )

    slot_state = vmem((scen, size.slot_lanes), F32)
    outs = [
        vmem(size.weights, BF),
        vmem(size.site_rows, BF),
        vmem(size.response, BF),
        vmem(size.coupling, BF),
        vmem(wave_init.shape, F32),
        vmem((8, size.ends), F32),
        vmem(size.node_rows, F32),
        vmem(size.fault_cols, F32),
        vmem(size.state, F32),
        vmem((size.lanes, size.slot_lanes), BF),
        vmem((size.slot_lanes, size.lanes), BF),
        vmem((8, size.slot_lanes), F32),
        slot_state,
        slot_state,
        vmem(size.state, F32),
        vmem(size.node_rows, F32),
        vmem(size.drive, F32),
        shape(size.exchange),
        shape(size.exchange),
    ]
    args = [
        cols, received, wave_init, row(line_delay), row(line_admittance), wp_hbm, eg_hbm,
        mt_hbm, kk_hbm, vb_hbm, branch_hbm, rest_hbm, rows_hbm, fault_hbm,
    ]
    (
        wp, eg, mt, kk, waves, ends, node_rows, fault_cols, branch, cg, cs, prm, filt, amps, volt,
        peak, drive, up, down,
    ) = call(
        functools.partial(start_kernel, size),
        "start",
        outs,
        [VMEM] * len(outs),
        in_hbm(cols) + in_vmem(received) + in_hbm(*args[2:]),
        [HBM, VMEM] + [HBM] * (len(args) - 2),
        [
            cols_scratch,
            vmem((1, size.ends), I32),
            vmem((1, size.ends), F32),
            vmem(size.state, F32),
            x_scratch,
            wide_scratch,
            dma((16,)),
        ],
        10,
    )

    arrivals = []
    for step in range(1, STEPS):
        last = step == STEPS - 1
        from_ahead = lax.ppermute(up, "region", ring)
        from_after = lax.ppermute(down, "region", back_ring)
        outs = [
            vmem(size.state, F32),
            slot_state,
            slot_state,
            vmem(size.state, F32),
            vmem(size.node_rows, F32),
            vmem(size.drive, F32),
        ]
        specs = [VMEM] * len(outs)
        scratch = [cols_scratch, x_scratch, wide_scratch, dma((4,))]
        if last:
            outs += [
                vmem((size.slots, 2 * scen), F32),
                hbm((scen, size.nodes), F32),
                hbm(size.state, F32),
                hbm(size.node_rows, F32),
            ]
            specs += [VMEM, HBM, HBM, HBM]
            scratch.append(vmem((scen, size.nodes), F32))
        result = call(
            functools.partial(middle_kernel, size, last),
            "middle",
            outs,
            specs,
            in_hbm(cols)
            + in_vmem(
                drive, wp, eg, mt, node_rows, fault_cols, cg, cs, prm, branch, filt, amps, volt, peak
            ),
            [HBM] + [VMEM] * 14,
            scratch,
            8,
            {10: 0, 11: 1, 12: 2, 13: 3, 14: 4},
        )
        branch, filt, amps, volt, peak, at_ends = result[:6]
        arrivals = [from_ahead, from_after] + arrivals
        args = in_vmem(at_ends, kk, ends, waves) + arrivals
        outs = [vmem(size.drive, F32), shape(size.exchange), shape(size.exchange)]
        specs, scratch = [VMEM] * 3, []
        if last:
            back, branch_out, volt, peak = result[6:]
            args += in_vmem(back)
            outs[0] = hbm(size.drive, F32)
            outs += [hbm((size.slots, 2 * scen), F32), hbm(wave_init.shape, F32)]
            specs[0] = HBM
            specs += [HBM, HBM]
            scratch = [vmem((step, *size.drive), F32), vmem(size.drive, F32), dma((4,))]
        drive, up, down, *rest = call(
            functools.partial(launch_kernel, size, step, last),
            "launch",
            outs,
            specs,
            args,
            [VMEM] * len(args),
            scratch,
            4,
        )
    chunks, waves_out = rest
    from_ahead = lax.ppermute(up, "region", ring)
    from_after = lax.ppermute(down, "region", back_ring)
    chunks = chunks.reshape(regions, rows, 2 * scen)
    returned = lax.all_to_all(chunks, "region", split_axis=0, concat_axis=0, tiled=True)
    voltage_out, peak_out = call(
        functools.partial(final_kernel, size),
        "final",
        [hbm((scen, size.nodes), F32), hbm((1, size.nodes), F32)],
        [HBM] * 2,
        in_hbm(drive, volt, mt_hbm, peak),
        [HBM] * 4,
        [
            vmem(size.drive, F32),
            vmem(size.state, F32),
            vmem(size.response, BF),
            vmem(size.node_rows, F32),
            vmem((scen, size.nodes), F32),
            vmem((1, size.nodes), F32),
            dma((8,)),
        ],
        12,
    )
    others = lax.axis_size("scen")
    peaks = []
    for d in range(1, others):
        shift = [(i, (i + d) % others) for i in range(others)]
        peaks.append(lax.ppermute(peak_out, "scen", shift))
    returned = returned.reshape(size.slots, 2 * scen)
    conv_state, wave_history = call(
        functools.partial(end_kernel, size),
        "end",
        [hbm(conv_init.shape, F32), hbm(wave_init.shape, F32)],
        [HBM] * 2,
        in_hbm(dst) + in_vmem(returned, from_ahead, from_after) + in_hbm(waves_out),
        [HBM, VMEM, VMEM, VMEM, HBM],
        [
            vmem(dst.shape, I32),
            vmem((1, *size.drive), F32),
            vmem(conv_init.shape, F32),
            dma((3,)),
        ],
        16,
        {4: 1},
    )
    envelope, conv_state = lax.optimization_barrier((peak_out, conv_state))
    for peak in peaks:
        envelope = jnp.maximum(envelope, peak)
    return voltage_out, branch_out, wave_history, conv_state, envelope.reshape(-1)


def solution(mesh):
    placed = (
        P("region", None, None, None),
        P("region", None),
        P("region"),
        P("region"),
        P("region"),
        P("scen", "region"),
        P("scen", "region"),
        P(None, "scen", "region"),
        P("region"),
        P("region"),
        P("region"),
        P("region", None),
        P("region"),
        P("region"),
        P(None, "region"),
        P(None, "scen", "region"),
        P("scen"),
        P("scen"),
    )
    return jax.shard_map(
        shards,
        mesh=mesh,
        in_specs=placed,
        out_specs=(
            P("scen", "region"),
            P("scen", "region"),
            P(None, "scen", "region"),
            P(None, "scen", "region"),
            P("region"),
        ),
        check_vma=False,
    )
```

```python
import functools
import math

import jax
import jax.numpy as jnp
from jax import lax
from jax.experimental import pallas as pl
from jax.experimental.pallas import tpu as pltpu
from jax.sharding import PartitionSpec as P

STEPS = 4
LANES = 128
BF = jnp.bfloat16
F32 = jnp.float32
I32 = jnp.int32
VMEM = pl.BlockSpec(memory_space=pltpu.VMEM)
SMEM = pl.BlockSpec(memory_space=pltpu.SMEM)
HBM = pl.BlockSpec(memory_space=pltpu.HBM)


def round_up(value, unit):
    return -(-value // unit) * unit


def iota(shape, dim):
    return lax.broadcasted_iota(I32, shape, dim)


def split_2(value):
    high = value.astype(BF)
    return high, (value - high.astype(F32)).astype(BF)


def split_3(value):
    high = value.astype(BF)
    rest = value - high.astype(F32)
    middle = rest.astype(BF)
    return high, middle, (rest - middle.astype(F32)).astype(BF)


def stacked(value):
    high, low = split_2(value)
    return jnp.concatenate([high, low], axis=0)


def folded(value):
    half = value.shape[0] // 2
    return value[:half] + value[half:]


def dot(left, right):
    return jnp.dot(left, right, preferred_element_type=F32)


def one_hot(mask):
    return jnp.where(mask, 1.0, 0.0).astype(BF)


def padded_index(nodes, width, padded):
    block = jnp.floor((nodes + 0.5) * (1.0 / width))
    return nodes + block * (padded - width)


class Sizes:
    def __init__(self, inverse_blocks, voltage, wave_init, line_node, conv_node):
        self.blocks, self.picks, self.width, _ = inverse_blocks.shape
        self.scen, self.nodes = voltage.shape
        self.delays = wave_init.shape[0]
        self.ends = line_node.shape[0]
        self.lines = self.ends // 2
        self.convs = conv_node.shape[0]
        self.regions = lax.axis_size("region")
        self.capacity = max(2, 12 * self.convs // (5 * self.regions))
        self.rows = round_up(self.capacity + 4, 8)
        self.slots = self.regions * self.rows
        self.slot_lanes = round_up(self.slots, 2 * LANES)
        self.padded = round_up(self.width, LANES)
        self.lanes = self.blocks * self.padded
        self.group = math.lcm(self.width, LANES) // self.width

        self.state = (self.blocks, self.scen, self.padded)
        starts = [k * self.width for k in range(self.picks)]
        self.starts = starts
        self.shifts = sorted({start % LANES for start in starts})
        self.depth = round_up(self.picks * self.width, LANES)
        self.turned = (len(self.shifts), self.blocks, 2 * self.scen, self.padded)
        self.chunk = min(2 * LANES, self.slot_lanes)
        self.chunks = self.slot_lanes // self.chunk
        self.wide = (2 * self.scen, self.lanes)
        self.weights = (self.blocks, self.picks * self.width, 2 * self.padded)
        self.site_rows = (self.lanes, self.ends)
        self.response = (self.blocks, self.ends, 2 * self.padded)
        self.coupling = (self.ends, 2 * self.ends)
        self.node_rows = (self.blocks, 8, self.padded)
        self.fault_cols = (2, self.scen, self.padded)
        self.drive = (self.scen, self.ends)
        self.exchange = (self.scen, self.lines)


class Copies:
    def __init__(self, sems):
        self.sems = sems
        self.count = 0

    def start(self, source, target):
        copy = pltpu.make_async_copy(source, target, self.sems.at[self.count])
        self.count += 1
        copy.start()
        return copy


def pad_blocks(size, source, store):
    group_width = size.group * size.width
    for first in range(0, size.blocks, size.group):
        chunk = source[:, first * size.width : first * size.width + group_width]
        for j in range(size.group):
            part = chunk[:, j * size.width : (j + 1) * size.width]
            zeros = jnp.zeros((part.shape[0], size.padded - size.width), part.dtype)
            store(first + j, jnp.concatenate([part, zeros], axis=1))


def unpad_blocks(size, load, target):
    group_width = size.group * size.width
    for first in range(0, size.blocks, size.group):
        parts = [load(first + j)[:, : size.width] for j in range(size.group)]
        target[:, first * size.width : first * size.width + group_width] = jnp.concatenate(
            parts, axis=1
        )


def block_lanes(size, b):
    return slice(b * size.padded, (b + 1) * size.padded)


def pack_kernel(
    size, region_hbm, power_hbm, node_hbm, gains_hbm, init_hbm, out_hbm, dst_hbm,
    region, power, node, gains, init, out, dst_out, sems,
):
    convs, slots = size.convs, size.slots
    copies = Copies(sems)
    first = copies.start(region_hbm, region)
    second = copies.start(init_hbm, init)
    others = [
        copies.start(power_hbm, power),
        copies.start(node_hbm, node),
        copies.start(gains_hbm, gains),
    ]
    first.wait()
    target = region[...]
    member = iota((round_up(size.regions, 16), convs), 0) == target
    before = one_hot(iota((convs, convs), 0) < iota((convs, convs), 1))
    earlier = dot(one_hot(member), before)
    rank = jnp.sum(jnp.where(member, earlier, 0.0), axis=0, keepdims=True)
    dst = target * size.rows + rank.astype(I32)
    dst_out[...] = dst
    select = one_hot(iota((slots, convs), 0) == dst)
    sent = [copies.start(dst_out, dst_hbm)]
    for copy in others:
        copy.wait()
    rows = [
        power[...].reshape(1, convs),
        gains[...],
        node[...].astype(F32).reshape(1, convs) + 1.0,
        jnp.zeros((LANES - 4, convs), F32),
    ]
    settings = jnp.concatenate(rows, axis=0)
    second.wait()
    state = jnp.concatenate([init[0], init[1]], axis=0)
    payload = jnp.concatenate([state.T, settings.T], axis=1)
    width = state.shape[0]
    rows = sum(dot(select, part) for part in split_3(payload))
    for r in range(size.regions):
        chunk = rows[r * size.rows : (r + 1) * size.rows]
        out[r] = chunk[:, :width]
        filler = jnp.zeros((LANES - size.rows, LANES), F32)
        turned = jnp.concatenate([chunk[:, width:], filler], axis=0).T
        out[r, size.capacity : size.capacity + 4, :] = turned[:4]
    sent.append(copies.start(out, out_hbm))
    for copy in sent:
        copy.wait()


def fault_terms(size, node, kind):
    first = lax.axis_index("region") * size.nodes
    local = (node[...] - first).astype(F32)
    inside = (local >= 0.0) & (local < size.nodes)
    site = jnp.where(inside, padded_index(local, size.width, size.padded), -1.0)
    level = 0.25 * jnp.left_shift(1, kind[...]).astype(F32)
    square = (size.scen, size.scen)
    diagonal = iota(square, 0) == iota(square, 1)

    def column(row):
        spread = jnp.where(diagonal, jnp.broadcast_to(row, square), 0.0)
        return jnp.broadcast_to(jnp.sum(spread, axis=1, keepdims=True), (size.scen, size.padded))

    return column(site), column(level)


def site_products(size, row, chunk, gather, scatter):
    part = row[:, chunk : chunk + LANES]
    block = jnp.floor((part + 0.5) * (1.0 / LANES))
    lane = part - block * LANES
    square = (LANES, LANES)
    down_block = jnp.broadcast_to(block, square).astype(BF)
    across_block = turned_row(block).astype(BF)
    down_lane = one_hot(lane == iota(square, 0).astype(F32))
    across_lane = one_hot(turned_row(lane) == iota(square, 1).astype(F32))
    zeros = jnp.zeros(square, BF)
    for n in range(size.lanes // LANES):
        here = jnp.asarray(n, BF)
        gather(n, jnp.where(down_block == here, down_lane, zeros))
        scatter(n, jnp.where(across_block == here, across_lane, zeros))


def turned_row(row):
    return jnp.broadcast_to(row, (LANES, row.shape[1])).T


def put_turned(size, x, b, value):
    pair = stacked(value)
    for i, shift in enumerate(size.shifts):
        x[i, b] = pltpu.roll(pair, shift, 1) if shift else pair


def picked_product(size, cols, b, x, wp):
    lane = iota((2 * size.scen, LANES), 1)
    tiles = []
    for first in range(0, size.depth, LANES):
        tile = None
        for k, start in enumerate(size.starts):
            if start + size.width <= first or start >= first + LANES:
                continue
            piece = x[size.shifts.index(start % LANES), cols[k, b]]
            tile = piece if tile is None else jnp.where(lane < start - first, tile, piece)
        tiles.append(tile)
    spare = size.depth - size.picks * size.width
    weights = wp[b]
    if spare:
        weights = jnp.concatenate([weights, jnp.zeros((spare, weights.shape[1]), BF)], axis=0)
    return dot(jnp.concatenate(tiles, axis=1), weights)


def three_terms(product, rows, width):
    top, low = product[:rows], product[rows:]
    return top[:, :width] + top[:, width:] + low[:, :width]


def apply_inverse(size, cols, x, wp, volt, vb):
    def block_row(b, carry):
        value = three_terms(picked_product(size, cols, b, x, wp), size.scen, size.padded)
        volt[b] = value
        vb[:, pl.ds(pl.multiple_of(b * size.padded, LANES), size.padded)] = stacked(value)
        return carry

    lax.fori_loop(0, size.blocks, block_row, 0, unroll=True)


def prep_kernel(
    size,
    cols_hbm, inverse, source, decay, gain, voltage, branch_init, line_node, fault_node, fault_kind,
    wp_out, eg_out, mt_out, kk_out, vb_out, branch_out, rest_out, rows_out, fault_out,
    cols, raw, vectors, volt_in, branch_in, nodes, faults,
    wp, eg, es, mt, both, kk, vb, volt, branch, rest, node_rows, fault_cols,
    sems,
):
    copies = Copies(sems)
    cols_copy = copies.start(cols_hbm, cols)
    small = [
        copies.start(line_node, nodes),
        copies.start(fault_node, faults.at[0:1]),
        copies.start(fault_kind, faults.at[1:2]),
    ]
    small += [copies.start(v, vectors.at[i]) for i, v in enumerate((source, decay, gain))]
    large = [copies.start(voltage, volt_in), copies.start(branch_init, branch_in)]
    stages = 4
    stage = size.blocks // stages
    weight_copies = []
    for i in range(stages):
        part = pl.ds(i * stage, stage)
        weight_copies.append(copies.start(inverse.at[part], raw.at[part]))
    sent = []
    for copy in small:
        copy.wait()

    row = padded_index(nodes[...].astype(F32), size.width, size.padded)
    for c in range(0, size.ends, LANES):
        def put_gather(n, value, c=c):
            eg[n * LANES : (n + 1) * LANES, c : c + LANES] = value

        def put_scatter(n, value, c=c):
            b, lane = n * LANES // size.padded, n * LANES % size.padded
            es[b, c : c + LANES, lane : lane + LANES] = value

        site_products(size, row, c, put_gather, put_scatter)
    sent.append(copies.start(eg, eg_out))

    for i in range(3):
        def put_row(b, value, i=i):
            node_rows[b, i : i + 1, :] = value

        pad_blocks(size, vectors.at[i], put_row)
    sent.append(copies.start(node_rows, rows_out))
    site, level = fault_terms(size, faults.at[0:1], faults.at[1:2])
    fault_cols[0] = site
    fault_cols[1] = level
    sent.append(copies.start(fault_cols, fault_out))
    for copy in large:
        copy.wait()

    def put_voltage(b, value):
        volt[b] = value
        vb[:, block_lanes(size, b)] = stacked(value)

    def put_branch(b, value):
        history = node_rows[b, 1:2, :] * value + node_rows[b, 2:3, :] * volt[b]
        branch[b] = history
        rest[b] = rest_of(size, node_rows, b, history, volt[b], site, level)

    pad_blocks(size, volt_in, put_voltage)
    pad_blocks(size, branch_in, put_branch)
    sent.append(copies.start(vb, vb_out))
    sent.append(copies.start(branch, branch_out))
    sent.append(copies.start(rest, rest_out))

    cols_copy.wait()
    zeros = jnp.zeros((size.width, size.padded - size.width), BF)
    zero_rows = jnp.zeros((size.padded - size.width, 2 * size.padded), BF)
    for i, copy in enumerate(weight_copies):
        copy.wait()

        def turn(b, carry):
            parts = []
            for k in range(size.picks):
                high, low = split_2(raw[b, k].T)
                part = jnp.concatenate([high, zeros, low, zeros], axis=1)
                wp[b, k * size.width : (k + 1) * size.width, :] = part
                parts += [part, zero_rows]
            left = jnp.concatenate([es[cols[k, b]] for k in range(size.picks)], axis=1)
            product = dot(left, jnp.concatenate(parts, axis=0))
            high, low = split_2(product[:, : size.padded] + product[:, size.padded :])
            mt[b] = jnp.concatenate([high, low], axis=1)
            both[:, pl.ds(pl.multiple_of(b * size.padded, LANES), size.padded)] = jnp.concatenate(
                [high, low], axis=0
            )
            return carry

        lax.fori_loop(i * stage, (i + 1) * stage, turn, 0, unroll=4)
        part = pl.ds(i * stage, stage)
        sent.append(copies.start(wp.at[part], wp_out.at[part]))
        sent.append(copies.start(mt.at[part], mt_out.at[part]))

    high, low = split_2(folded(dot(both[...], eg[...])))
    kk[...] = jnp.concatenate([high, low], axis=1)
    sent.append(copies.start(kk, kk_out))
    for copy in sent:
        copy.wait()


def rest_of(size, node_rows, b, history, v, site, level):
    lane = iota((size.scen, size.padded), 1).astype(F32)
    first = jnp.asarray(b * size.padded, I32).astype(F32)
    hit = jnp.where(lane + first == site, level, 0.0)
    return node_rows[b, 0:1, :] - history - hit * v


def for_chunks(size, count, work):
    for c in range(size.chunks):
        if c < 2:
            work(c * size.chunk)
        else:
            pl.when(count > c)(functools.partial(work, c * size.chunk))


def inject(size, count, pair, cs, put):
    step = 2 if size.blocks % 2 == 0 else 1
    width = step * size.padded
    least = min(2, size.chunks)

    def inject_from(used):
        left = pair[:, : used * size.chunk]

        def some_blocks(i, carry):
            lanes = pl.ds(pl.multiple_of(i * width, LANES), width)
            both = folded(dot(left, cs[: used * size.chunk, lanes]))
            for j in range(step):
                put(i * step + j, both[:, block_lanes(size, j)])
            return carry

        lax.fori_loop(0, size.blocks // step, some_blocks, 0, unroll=4)

    for used in range(least, size.chunks + 1):
        if used == least:
            chosen = count <= used
        else:
            chosen = count == used
        pl.when(chosen)(functools.partial(inject_from, used))


def converter_update(size, count, vb, cg, prm, filt, amps, pair):
    def update(first):
        lanes = slice(first, first + size.chunk)
        measured = folded(dot(vb[...], cg[:, lanes]))
        filtered = filt[:, lanes]
        filtered = filtered + prm[2:3, lanes] * (measured - filtered)
        current = amps[:, lanes]
        target = prm[0:1, lanes] * filtered / (1.0 + filtered * filtered)
        current = current + prm[1:2, lanes] * (target - current)
        filt[:, lanes] = filtered
        amps[:, lanes] = current
        pair[:, lanes] = stacked(current)

    for_chunks(size, count, update)


def launch_part(size, history, ends, at_ends, kk, drive_out, up, down):
    drive = jnp.zeros(size.drive, F32)
    for d in range(size.delays):
        drive = jnp.where(ends[0:1, :] == float(d + 1), history(d), drive)
    drive_out[...] = drive
    answer = three_terms(dot(stacked(drive), kk[...]), size.scen, size.ends)
    launch = 2.0 * ends[1:2, :] * (at_ends + answer) - drive
    up[...] = launch[:, size.lines :]
    down[...] = launch[:, : size.lines]


def start_kernel(
    size,
    cols_hbm, received, waves_hbm, delay_hbm, admittance_hbm,
    wp_hbm, eg_hbm, mt_hbm, kk_hbm, vb_hbm, branch_hbm, rest_hbm, rows_hbm, fault_hbm,
    wp, eg, mt, kk, waves, ends, node_rows, fault_cols, branch, cg, cs, prm, filt, amps, volt,
    peak, drive, up, down, place_hbm,
    cols, place, delays, admittances, rest, x, vb, pair, moved, moved_settings, sems,
):
    copies = Copies(sems)
    vb_copy = copies.start(vb_hbm, vb)
    rest_copy = copies.start(rest_hbm, rest)
    cols_copy = copies.start(cols_hbm, cols)
    wp_copy = copies.start(wp_hbm, wp)
    later = [
        copies.start(eg_hbm, eg),
        copies.start(delay_hbm, delays),
        copies.start(admittance_hbm, admittances),
        copies.start(waves_hbm, waves),
        copies.start(kk_hbm, kk),
        copies.start(mt_hbm, mt),
        copies.start(branch_hbm, branch),
        copies.start(rows_hbm, node_rows),
        copies.start(fault_hbm, fault_cols),
    ]
    rows, capacity, slots, regions = size.rows, size.capacity, size.slots, size.regions
    total = 0
    for r in range(regions):
        settings = received[r * rows + capacity : r * rows + capacity + 4, :]
        filler = jnp.zeros((LANES - 4, LANES), F32)
        turned = jnp.concatenate([settings[:, :LANES], filler], axis=0).T
        place[r] = total
        moved[pl.ds(total, rows), :] = received[r * rows : (r + 1) * rows, :]
        moved_settings[pl.ds(total, rows), :] = turned[:rows]
        total = total + jnp.sum(jnp.where(settings[3:4, :] > 0.0, 1.0, 0.0)).astype(I32)
    count = lax.div(total + (size.chunk - 1), size.chunk)
    place[regions] = count
    place_copy = copies.start(place, place_hbm)
    for c in range(0, size.slot_lanes, LANES):
        valid = iota((LANES, LANES), 0) + c < total
        turned = jnp.where(valid, moved[c : c + LANES, :], 0.0).T
        filt[:, c : c + LANES] = turned[: size.scen]
        amps[:, c : c + LANES] = turned[size.scen :]
        turned = jnp.where(valid, moved_settings[c : c + LANES, :], 0.0).T
        prm[:, c : c + LANES] = turned[:8]
    row = padded_index(prm[3:4, :] - 1.0, size.width, size.padded)

    def put_products(first):
        for c in range(first, first + size.chunk, LANES):
            def put_gather(n, value, c=c):
                cg[n * LANES : (n + 1) * LANES, c : c + LANES] = value

            def put_scatter(n, value, c=c):
                cs[c : c + LANES, n * LANES : (n + 1) * LANES] = value

            site_products(size, row, c, put_gather, put_scatter)

    for_chunks(size, count, put_products)
    peak[...] = jnp.zeros(peak.shape, F32)

    vb_copy.wait()
    converter_update(size, count, vb, cg, prm, filt, amps, pair)
    rest_copy.wait()

    def put_start(b, injected):
        put_turned(size, x, b, rest[b] + injected)

    inject(size, count, pair, cs, put_start)
    cols_copy.wait()
    wp_copy.wait()
    apply_inverse(size, cols, x, wp, volt, vb)
    for copy in later:
        copy.wait()
    ends[0:1, :] = delays[...].astype(F32)
    ends[1:2, :] = admittances[...]
    at_ends = folded(dot(vb[...], eg[...]))
    launch_part(size, lambda d: waves[d], ends, at_ends, kk, drive, up, down)
    place_copy.wait()


def middle_kernel(
    size, last,
    cols_hbm, place_hbm, drive, wp, eg, mt, node_rows, fault_cols, cg, cs, prm,
    branch_in, filt_in, amps_in, volt_in, peak_in,
    branch, filt, amps, volt, peak, at_ends, *refs,
):
    if last:
        back, branch_hbm, volt_hbm, peak_hbm, branch_out, moved = *refs[:4], *refs[-2:]
        refs = refs[4:-2]
    cols, place, x, vb, pair, sems = refs
    copies = Copies(sems)
    place_copy = copies.start(place_hbm, place)
    cols_copy = copies.start(cols_hbm, cols)
    drives = stacked(drive[...])
    for b in range(size.blocks):
        added = three_terms(dot(drives, mt[b]), size.scen, size.padded)
        v = volt[b] + added
        volt[b] = v
        vb[:, block_lanes(size, b)] = stacked(v)
        magnitude = jnp.abs(v)
        top = magnitude[:8]
        for s in range(8, size.scen, 8):
            top = jnp.maximum(top, magnitude[s : s + 8])
        peak[b] = jnp.maximum(peak[b], top)
    place_copy.wait()
    count = place[size.regions]
    converter_update(size, count, vb, cg, prm, filt, amps, pair)

    def put_next(b, injected):
        history = node_rows[b, 1:2, :] * branch[b] + node_rows[b, 2:3, :] * volt[b]
        branch[b] = history
        site, level = fault_cols[0], fault_cols[1]
        rest = rest_of(size, node_rows, b, history, volt[b], site, level)
        put_turned(size, x, b, rest + injected)

    inject(size, count, pair, cs, put_next)
    cols_copy.wait()
    if last:
        unpad_blocks(size, lambda b: branch[b], branch_out)
        sent = [copies.start(branch_out, branch_hbm), copies.start(peak, peak_hbm)]
    apply_inverse(size, cols, x, wp, volt, vb)
    if last:
        sent.append(copies.start(volt, volt_hbm))
    at_ends[...] = folded(dot(vb[...], eg[...]))
    if last:
        for c in range(0, size.slot_lanes, LANES):
            part = jnp.concatenate([filt[:, c : c + LANES], amps[:, c : c + LANES]], axis=0)
            moved[c : c + LANES, :] = part.T
        moved[size.slot_lanes :, :] = jnp.zeros((size.rows, 2 * size.scen), F32)
        for r in range(size.regions):
            back[r * size.rows : (r + 1) * size.rows, :] = moved[pl.ds(place[r], size.rows), :]
        for copy in sent:
            copy.wait()


def launch_kernel(size, done, last, at_ends, kk, ends, waves, *refs):
    arrivals, refs = refs[: 2 * done], refs[2 * done :]

    def history(d):
        if d >= done:
            return waves[d - done]
        return jnp.concatenate([arrivals[2 * d][...], arrivals[2 * d + 1][...]], axis=1)

    if last:
        back, refs = refs[0], refs[1:]
    drive, up, down = refs[:3]
    if last:
        drive_hbm = drive
        chunks, waves_out, recent, drive, sems = refs[3:]
        copies = Copies(sems)
        sent = [copies.start(back, chunks)]
        for d in range(done):
            recent[d] = history(d)
        sent.append(copies.start(recent, waves_out.at[pl.ds(1, done)]))
        kept = size.delays - 1 - done
        sent.append(copies.start(waves.at[pl.ds(0, kept)], waves_out.at[pl.ds(1 + done, kept)]))
    launch_part(size, history, ends, at_ends[...], kk, drive, up, down)
    if last:
        sent.append(copies.start(drive, drive_hbm))
        for copy in sent:
            copy.wait()


def final_kernel(
    size, drive_hbm, volt_hbm, mt_hbm, peak_hbm, voltage_hbm, top_hbm,
    drive, volt, mt, peak, voltage_out, peak_out, sems,
):
    copies = Copies(sems)
    drive_copy = copies.start(drive_hbm, drive)
    half = size.blocks // 2
    parts = []
    for i in range(2):
        part = pl.ds(i * half, half)
        parts.append(
            [copies.start(volt_hbm.at[part], volt.at[part]), copies.start(mt_hbm.at[part], mt.at[part])]
        )
    peak_copy = copies.start(peak_hbm, peak)
    drive_copy.wait()
    pair = stacked(drive[...])
    for b in range(size.blocks):
        if b % half == 0:
            for copy in parts[b // half]:
                copy.wait()
        volt[b] = volt[b] + three_terms(dot(pair, mt[b]), size.scen, size.padded)
    peak_copy.wait()

    def largest(b):
        top = jnp.max(jnp.abs(volt[b]), axis=0, keepdims=True)
        return jnp.maximum(top, jnp.max(peak[b], axis=0, keepdims=True))

    unpad_blocks(size, largest, peak_out)
    sent = [copies.start(peak_out, top_hbm)]
    unpad_blocks(size, lambda b: volt[b], voltage_out)
    sent.append(copies.start(voltage_out, voltage_hbm))
    for copy in sent:
        copy.wait()


def end_kernel(
    size, dst_hbm, received, ahead, after, waves_in, state_hbm, waves_out,
    dst, newest, state_out, sems,
):
    copies = Copies(sems)
    dst_copy = copies.start(dst_hbm, dst)
    newest[0, :, : size.lines] = ahead[...]
    newest[0, :, size.lines :] = after[...]
    sent = [copies.start(newest, waves_out.at[pl.ds(0, 1)])]
    parts = jnp.concatenate(split_3(received[...].T), axis=0)
    dst_copy.wait()
    select = one_hot(iota((size.slots, size.convs), 0) == dst[...])
    state = dot(parts, select)
    width = 2 * size.scen
    state = state[:width] + state[width : 2 * width] + state[2 * width :]
    state_out[0] = state[: size.scen]
    state_out[1] = state[size.scen :]
    sent.append(copies.start(state_out, state_hbm))
    for copy in sent:
        copy.wait()


def shape(dims, dtype=F32):
    return jax.ShapeDtypeStruct(dims, dtype)


def in_vmem(*values):
    return [pltpu.with_memory_space_constraint(v, pltpu.VMEM) for v in values]


def in_hbm(*values):
    return [pltpu.with_memory_space_constraint(v, pltpu.HBM) for v in values]


def call(kernel, name, outs, out_specs, args, specs, scratch, limit, aliases=None):
    return pl.pallas_call(
        kernel,
        name=name,
        out_shape=outs,
        in_specs=specs,
        out_specs=out_specs,
        scratch_shapes=list(scratch),
        input_output_aliases=aliases or {},
        compiler_params=pltpu.CompilerParams(vmem_limit_bytes=limit << 20),
    )(*args)


def shards(
    inverse_blocks, block_cols, source_current, node_decay, node_gain, voltage_init, branch_init,
    wave_init, line_node, line_delay, line_admittance, conv_region, conv_node, conv_power,
    conv_gains, conv_init, fault_node, fault_kind,
):
    size = Sizes(inverse_blocks, voltage_init, wave_init, line_node, conv_node)
    regions, rows, scen = size.regions, size.rows, size.scen
    ring = [(i, (i + 1) % regions) for i in range(regions)]
    back_ring = [(j, i) for i, j in ring]
    dma = pltpu.SemaphoreType.DMA
    vmem, hbm = pltpu.VMEM, pltpu.HBM

    def row(vector):
        return vector.reshape(1, -1)

    chunk = (regions, rows, 2 * scen)
    packed, dst = call(
        functools.partial(pack_kernel, size),
        "pack",
        [hbm(chunk, F32), hbm((1, size.convs), I32)],
        [HBM] * 2,
        in_hbm(row(conv_region), conv_power, conv_node, conv_gains, conv_init),
        [HBM] * 5,
        [
            vmem((1, size.convs), I32),
            vmem(conv_power.shape, F32),
            vmem(conv_node.shape, I32),
            vmem(conv_gains.shape, F32),
            vmem(conv_init.shape, F32),
            vmem(chunk, F32),
            vmem((1, size.convs), I32),
            dma((8,)),
        ],
        16,
    )
    received = lax.all_to_all(packed, "region", split_axis=0, concat_axis=0, tiled=True)
    received = received.reshape(size.slots, 2 * scen)

    cols = block_cols.T
    cols_scratch = pltpu.SMEM(cols.shape, I32)
    x_scratch = vmem(size.turned, BF)
    wide_scratch = vmem(size.wide, BF)
    place_scratch = pltpu.SMEM((LANES,), I32)
    pair_scratch = vmem((2 * scen, size.slot_lanes), BF)
    moved_scratch = vmem((size.slot_lanes + rows, 2 * scen), F32)
    kept = [
        (size.weights, BF),
        (size.site_rows, BF),
        (size.response, BF),
        (size.coupling, BF),
        (size.wide, BF),
        (size.state, F32),
        (size.state, F32),
        (size.node_rows, F32),
        (size.fault_cols, F32),
    ]
    vectors = (3, 1, size.nodes)
    args = [
        cols, inverse_blocks, row(source_current), row(node_decay), row(node_gain), voltage_init,
        branch_init, row(line_node), row(fault_node), row(fault_kind),
    ]
    wp_hbm, eg_hbm, mt_hbm, kk_hbm, vb_hbm, branch_hbm, rest_hbm, rows_hbm, fault_hbm = call(
        functools.partial(prep_kernel, size),
        "prep",
        [hbm(*item) for item in kept],
        [HBM] * len(kept),
        in_hbm(*args),
        [HBM] * len(args),
        [
            cols_scratch,
            vmem(inverse_blocks.shape, F32),
            vmem(vectors, F32),
            vmem(voltage_init.shape, F32),
            vmem(voltage_init.shape, F32),
            vmem((1, size.ends), I32),
            vmem((2, scen), I32),
            vmem(size.weights, BF),
            vmem(size.site_rows, BF),
            vmem((size.blocks, size.ends, size.padded), BF),
            vmem(size.response, BF),
            vmem((2 * size.ends, size.lanes), BF),
            vmem(size.coupling, BF),
            wide_scratch,
            vmem(size.state, F32),
            vmem(size.state, F32),
            vmem(size.state, F32),
            vmem(size.node_rows, F32),
            vmem(size.fault_cols, F32),
            dma((40,)),
        ],
        48,
    )

    slot_state = vmem((scen, size.slot_lanes), F32)
    outs = [
        vmem(size.weights, BF),
        vmem(size.site_rows, BF),
        vmem(size.response, BF),
        vmem(size.coupling, BF),
        vmem(wave_init.shape, F32),
        vmem((8, size.ends), F32),
        vmem(size.node_rows, F32),
        vmem(size.fault_cols, F32),
        vmem(size.state, F32),
        vmem((size.lanes, size.slot_lanes), BF),
        vmem((size.slot_lanes, size.lanes), BF),
        vmem((8, size.slot_lanes), F32),
        slot_state,
        slot_state,
        vmem(size.state, F32),
        vmem(size.node_rows, F32),
        vmem(size.drive, F32),
        shape(size.exchange),
        shape(size.exchange),
        hbm((LANES,), I32),
    ]
    args = [
        cols, received, wave_init, row(line_delay), row(line_admittance), wp_hbm, eg_hbm,
        mt_hbm, kk_hbm, vb_hbm, branch_hbm, rest_hbm, rows_hbm, fault_hbm,
    ]
    (
        wp, eg, mt, kk, waves, ends, node_rows, fault_cols, branch, cg, cs, prm, filt, amps, volt,
        peak, drive, up, down, place,
    ) = call(
        functools.partial(start_kernel, size),
        "start",
        outs,
        [VMEM] * (len(outs) - 1) + [HBM],
        in_hbm(cols) + in_vmem(received) + in_hbm(*args[2:]),
        [HBM, VMEM] + [HBM] * (len(args) - 2),
        [
            cols_scratch,
            place_scratch,
            vmem((1, size.ends), I32),
            vmem((1, size.ends), F32),
            vmem(size.state, F32),
            x_scratch,
            wide_scratch,
            pair_scratch,
            moved_scratch,
            moved_scratch,
            dma((16,)),
        ],
        14,
    )

    arrivals = []
    for step in range(1, STEPS):
        last = step == STEPS - 1
        from_ahead = lax.ppermute(up, "region", ring)
        from_after = lax.ppermute(down, "region", back_ring)
        outs = [
            vmem(size.state, F32),
            slot_state,
            slot_state,
            vmem(size.state, F32),
            vmem(size.node_rows, F32),
            vmem(size.drive, F32),
        ]
        specs = [VMEM] * len(outs)
        scratch = [cols_scratch, place_scratch, x_scratch, wide_scratch, pair_scratch, dma((5,))]
        if last:
            outs += [
                vmem((size.slots, 2 * scen), F32),
                hbm((scen, size.nodes), F32),
                hbm(size.state, F32),
                hbm(size.node_rows, F32),
            ]
            specs += [VMEM, HBM, HBM, HBM]
            scratch += [vmem((scen, size.nodes), F32), moved_scratch]
        result = call(
            functools.partial(middle_kernel, size, last),
            "middle",
            outs,
            specs,
            in_hbm(cols, place)
            + in_vmem(
                drive, wp, eg, mt, node_rows, fault_cols, cg, cs, prm, branch, filt, amps, volt, peak
            ),
            [HBM] * 2 + [VMEM] * 14,
            scratch,
            12,
            {11: 0, 12: 1, 13: 2, 14: 3, 15: 4},
        )
        branch, filt, amps, volt, peak, at_ends = result[:6]
        arrivals = [from_ahead, from_after] + arrivals
        args = in_vmem(at_ends, kk, ends, waves) + arrivals
        outs = [vmem(size.drive, F32), shape(size.exchange), shape(size.exchange)]
        specs, scratch = [VMEM] * 3, []
        if last:
            back, branch_out, volt, peak = result[6:]
            args += in_vmem(back)
            outs[0] = hbm(size.drive, F32)
            outs += [hbm((size.slots, 2 * scen), F32), hbm(wave_init.shape, F32)]
            specs[0] = HBM
            specs += [HBM, HBM]
            scratch = [vmem((step, *size.drive), F32), vmem(size.drive, F32), dma((4,))]
        drive, up, down, *rest = call(
            functools.partial(launch_kernel, size, step, last),
            "launch",
            outs,
            specs,
            args,
            [VMEM] * len(args),
            scratch,
            4,
        )
    chunks, waves_out = rest
    from_ahead = lax.ppermute(up, "region", ring)
    from_after = lax.ppermute(down, "region", back_ring)
    chunks = chunks.reshape(regions, rows, 2 * scen)
    returned = lax.all_to_all(chunks, "region", split_axis=0, concat_axis=0, tiled=True)
    voltage_out, peak_out = call(
        functools.partial(final_kernel, size),
        "final",
        [hbm((scen, size.nodes), F32), hbm((1, size.nodes), F32)],
        [HBM] * 2,
        in_hbm(drive, volt, mt_hbm, peak),
        [HBM] * 4,
        [
            vmem(size.drive, F32),
            vmem(size.state, F32),
            vmem(size.response, BF),
            vmem(size.node_rows, F32),
            vmem((scen, size.nodes), F32),
            vmem((1, size.nodes), F32),
            dma((8,)),
        ],
        12,
    )
    others = lax.axis_size("scen")
    peaks = []
    for d in range(1, others):
        shift = [(i, (i + d) % others) for i in range(others)]
        peaks.append(lax.ppermute(peak_out, "scen", shift))
    returned = returned.reshape(size.slots, 2 * scen)
    conv_state, wave_history = call(
        functools.partial(end_kernel, size),
        "end",
        [hbm(conv_init.shape, F32), hbm(wave_init.shape, F32)],
        [HBM] * 2,
        in_hbm(dst) + in_vmem(returned, from_ahead, from_after) + in_hbm(waves_out),
        [HBM, VMEM, VMEM, VMEM, HBM],
        [
            vmem(dst.shape, I32),
            vmem((1, *size.drive), F32),
            vmem(conv_init.shape, F32),
            dma((3,)),
        ],
        16,
        {4: 1},
    )
    envelope, conv_state = lax.optimization_barrier((peak_out, conv_state))
    for peak in peaks:
        envelope = jnp.maximum(envelope, peak)
    return voltage_out, branch_out, wave_history, conv_state, envelope.reshape(-1)


def solution(mesh):
    placed = (
        P("region", None, None, None),
        P("region", None),
        P("region"),
        P("region"),
        P("region"),
        P("scen", "region"),
        P("scen", "region"),
        P(None, "scen", "region"),
        P("region"),
        P("region"),
        P("region"),
        P("region", None),
        P("region"),
        P("region"),
        P(None, "region"),
        P(None, "scen", "region"),
        P("scen"),
        P("scen"),
    )
    return jax.shard_map(
        shards,
        mesh=mesh,
        in_specs=placed,
        out_specs=(
            P("scen", "region"),
            P("scen", "region"),
            P(None, "scen", "region"),
            P(None, "scen", "region"),
            P("region"),
        ),
        check_vma=False,
    )
```

```python
import functools
import math

import jax
import jax.numpy as jnp
from jax import lax
from jax.experimental import pallas as pl
from jax.experimental.pallas import tpu as pltpu
from jax.sharding import PartitionSpec as P

STEPS = 4
LANES = 128
BF = jnp.bfloat16
F32 = jnp.float32
I32 = jnp.int32
VMEM = pl.BlockSpec(memory_space=pltpu.VMEM)
SMEM = pl.BlockSpec(memory_space=pltpu.SMEM)
HBM = pl.BlockSpec(memory_space=pltpu.HBM)


def round_up(value, unit):
    return -(-value // unit) * unit


def iota(shape, dim):
    return lax.broadcasted_iota(I32, shape, dim)


def split_2(value):
    high = value.astype(BF)
    return high, (value - high.astype(F32)).astype(BF)


def split_3(value):
    high = value.astype(BF)
    rest = value - high.astype(F32)
    middle = rest.astype(BF)
    return high, middle, (rest - middle.astype(F32)).astype(BF)


def stacked(value):
    high, low = split_2(value)
    return jnp.concatenate([high, low], axis=0)


def folded(value):
    half = value.shape[0] // 2
    return value[:half] + value[half:]


def dot(left, right):
    return jnp.dot(left, right, preferred_element_type=F32)


def one_hot(mask):
    return jnp.where(mask, 1.0, 0.0).astype(BF)


def padded_index(nodes, width, padded):
    block = jnp.floor((nodes + 0.5) * (1.0 / width))
    return nodes + block * (padded - width)


class Sizes:
    def __init__(self, inverse_blocks, voltage, wave_init, line_node, conv_node):
        self.blocks, self.picks, self.width, _ = inverse_blocks.shape
        self.scen, self.nodes = voltage.shape
        self.delays = wave_init.shape[0]
        self.ends = line_node.shape[0]
        self.lines = self.ends // 2
        self.convs = conv_node.shape[0]
        self.regions = lax.axis_size("region")
        self.capacity = max(2, 12 * self.convs // (5 * self.regions))
        self.rows = round_up(self.capacity + 4, 8)
        self.slots = self.regions * self.rows
        self.slot_lanes = round_up(self.slots, 2 * LANES)
        self.padded = round_up(self.width, LANES)
        self.lanes = self.blocks * self.padded
        self.group = math.lcm(self.width, LANES) // self.width

        self.state = (self.blocks, self.scen, self.padded)
        starts = [k * self.width for k in range(self.picks)]
        self.starts = starts
        self.shifts = sorted({start % LANES for start in starts})
        self.depth = round_up(self.picks * self.width, LANES)
        self.turned = (len(self.shifts), self.blocks, 2 * self.scen, self.padded)
        self.chunk = min(2 * LANES, self.slot_lanes)
        self.chunks = self.slot_lanes // self.chunk
        self.wide = (2 * self.scen, self.lanes)
        self.weights = (self.blocks, self.picks * self.width, 2 * self.padded)
        self.site_rows = (self.lanes, self.ends)
        self.response = (self.blocks, self.ends, 2 * self.padded)
        self.coupling = (self.ends, 2 * self.ends)
        self.node_rows = (self.blocks, 8, self.padded)
        self.fault_cols = (2, self.scen, self.padded)
        self.drive = (self.scen, self.ends)
        self.exchange = (self.scen, self.lines)


class Copies:
    def __init__(self, sems):
        self.sems = sems
        self.count = 0

    def start(self, source, target):
        copy = pltpu.make_async_copy(source, target, self.sems.at[self.count])
        self.count += 1
        copy.start()
        return copy


def pad_blocks(size, source, store):
    group_width = size.group * size.width
    for first in range(0, size.blocks, size.group):
        chunk = source[:, first * size.width : first * size.width + group_width]
        for j in range(size.group):
            part = chunk[:, j * size.width : (j + 1) * size.width]
            zeros = jnp.zeros((part.shape[0], size.padded - size.width), part.dtype)
            store(first + j, jnp.concatenate([part, zeros], axis=1))


def unpad_blocks(size, load, target):
    group_width = size.group * size.width
    for first in range(0, size.blocks, size.group):
        parts = [load(first + j)[:, : size.width] for j in range(size.group)]
        target[:, first * size.width : first * size.width + group_width] = jnp.concatenate(
            parts, axis=1
        )


def block_lanes(size, b):
    return slice(b * size.padded, (b + 1) * size.padded)


def pack_kernel(
    size, region_hbm, power_hbm, node_hbm, gains_hbm, init_hbm, out_hbm, dst_hbm,
    region, power, node, gains, init, out, dst_out, sems,
):
    convs, slots = size.convs, size.slots
    copies = Copies(sems)
    first = copies.start(region_hbm, region)
    second = copies.start(init_hbm, init)
    others = [
        copies.start(power_hbm, power),
        copies.start(node_hbm, node),
        copies.start(gains_hbm, gains),
    ]
    first.wait()
    target = region[...]
    member = iota((round_up(size.regions, 16), convs), 0) == target
    before = one_hot(iota((convs, convs), 0) < iota((convs, convs), 1))
    earlier = dot(one_hot(member), before)
    rank = jnp.sum(jnp.where(member, earlier, 0.0), axis=0, keepdims=True)
    dst = target * size.rows + rank.astype(I32)
    dst_out[...] = dst
    select = one_hot(iota((slots, convs), 0) == dst)
    sent = [copies.start(dst_out, dst_hbm)]
    for copy in others:
        copy.wait()
    rows = [
        power[...].reshape(1, convs),
        gains[...],
        node[...].astype(F32).reshape(1, convs) + 1.0,
        jnp.zeros((LANES - 4, convs), F32),
    ]
    settings = jnp.concatenate(rows, axis=0)
    second.wait()
    state = jnp.concatenate([init[0], init[1]], axis=0)
    payload = jnp.concatenate([state.T, settings.T], axis=1)
    width = state.shape[0]
    rows = sum(dot(select, part) for part in split_3(payload))
    for r in range(size.regions):
        chunk = rows[r * size.rows : (r + 1) * size.rows]
        out[r] = chunk[:, :width]
        filler = jnp.zeros((LANES - size.rows, LANES), F32)
        turned = jnp.concatenate([chunk[:, width:], filler], axis=0).T
        out[r, size.capacity : size.capacity + 4, :] = turned[:4]
    sent.append(copies.start(out, out_hbm))
    for copy in sent:
        copy.wait()


def fault_terms(size, node, kind):
    first = lax.axis_index("region") * size.nodes
    local = (node[...] - first).astype(F32)
    inside = (local >= 0.0) & (local < size.nodes)
    site = jnp.where(inside, padded_index(local, size.width, size.padded), -1.0)
    level = 0.25 * jnp.left_shift(1, kind[...]).astype(F32)
    square = (size.scen, size.scen)
    diagonal = iota(square, 0) == iota(square, 1)

    def column(row):
        spread = jnp.where(diagonal, jnp.broadcast_to(row, square), 0.0)
        return jnp.broadcast_to(jnp.sum(spread, axis=1, keepdims=True), (size.scen, size.padded))

    return column(site), column(level)


def site_products(size, row, chunk, gather, scatter):
    part = row[:, chunk : chunk + LANES]
    block = jnp.floor((part + 0.5) * (1.0 / LANES))
    lane = part - block * LANES
    square = (LANES, LANES)
    down_block = jnp.broadcast_to(block, square).astype(BF)
    across_block = turned_row(block).astype(BF)
    down_lane = one_hot(lane == iota(square, 0).astype(F32))
    across_lane = one_hot(turned_row(lane) == iota(square, 1).astype(F32))
    zeros = jnp.zeros(square, BF)
    for n in range(size.lanes // LANES):
        here = jnp.asarray(n, BF)
        gather(n, jnp.where(down_block == here, down_lane, zeros))
        scatter(n, jnp.where(across_block == here, across_lane, zeros))


def turned_row(row):
    return jnp.broadcast_to(row, (LANES, row.shape[1])).T


def put_turned(size, x, b, value):
    pair = stacked(value)
    for i, shift in enumerate(size.shifts):
        x[i, b] = pltpu.roll(pair, shift, 1) if shift else pair


def picked_product(size, cols, b, x, wp):
    lane = iota((2 * size.scen, LANES), 1)
    tiles = []
    for first in range(0, size.depth, LANES):
        tile = None
        for k, start in enumerate(size.starts):
            if start + size.width <= first or start >= first + LANES:
                continue
            piece = x[size.shifts.index(start % LANES), cols[k, b]]
            tile = piece if tile is None else jnp.where(lane < start - first, tile, piece)
        tiles.append(tile)
    spare = size.depth - size.picks * size.width
    weights = wp[b]
    if spare:
        weights = jnp.concatenate([weights, jnp.zeros((spare, weights.shape[1]), BF)], axis=0)
    return dot(jnp.concatenate(tiles, axis=1), weights)


def three_terms(product, rows, width):
    top, low = product[:rows], product[rows:]
    return top[:, :width] + top[:, width:] + low[:, :width]


def apply_inverse(size, cols, x, wp, volt, vb):
    def block_row(b, carry):
        value = three_terms(picked_product(size, cols, b, x, wp), size.scen, size.padded)
        volt[b] = value
        vb[:, pl.ds(pl.multiple_of(b * size.padded, LANES), size.padded)] = stacked(value)
        return carry

    lax.fori_loop(0, size.blocks, block_row, 0, unroll=True)


def prep_kernel(
    size,
    cols_hbm, inverse, source, decay, gain, voltage, branch_init, line_node, fault_node, fault_kind,
    wp_out, eg_out, mt_out, kk_out, vb_out, branch_out, rest_out, rows_out, fault_out,
    cols, raw, vectors, volt_in, branch_in, nodes, faults,
    wp, eg, es, mt, both, kk, vb, volt, branch, rest, node_rows, fault_cols,
    sems,
):
    copies = Copies(sems)
    cols_copy = copies.start(cols_hbm, cols)
    small = [
        copies.start(line_node, nodes),
        copies.start(fault_node, faults.at[0:1]),
        copies.start(fault_kind, faults.at[1:2]),
    ]
    small += [copies.start(v, vectors.at[i]) for i, v in enumerate((source, decay, gain))]
    large = [copies.start(voltage, volt_in), copies.start(branch_init, branch_in)]
    stages = 4
    stage = size.blocks // stages
    weight_copies = []
    for i in range(stages):
        part = pl.ds(i * stage, stage)
        weight_copies.append(copies.start(inverse.at[part], raw.at[part]))
    sent = []
    for copy in small:
        copy.wait()

    row = padded_index(nodes[...].astype(F32), size.width, size.padded)
    for c in range(0, size.ends, LANES):
        def put_gather(n, value, c=c):
            eg[n * LANES : (n + 1) * LANES, c : c + LANES] = value

        def put_scatter(n, value, c=c):
            b, lane = n * LANES // size.padded, n * LANES % size.padded
            es[b, c : c + LANES, lane : lane + LANES] = value

        site_products(size, row, c, put_gather, put_scatter)
    sent.append(copies.start(eg, eg_out))

    for i in range(3):
        def put_row(b, value, i=i):
            node_rows[b, i : i + 1, :] = value

        pad_blocks(size, vectors.at[i], put_row)
    sent.append(copies.start(node_rows, rows_out))
    site, level = fault_terms(size, faults.at[0:1], faults.at[1:2])
    fault_cols[0] = site
    fault_cols[1] = level
    sent.append(copies.start(fault_cols, fault_out))
    for copy in large:
        copy.wait()

    def put_voltage(b, value):
        volt[b] = value
        vb[:, block_lanes(size, b)] = stacked(value)

    def put_branch(b, value):
        history = node_rows[b, 1:2, :] * value + node_rows[b, 2:3, :] * volt[b]
        branch[b] = history
        rest[b] = rest_of(size, node_rows, b, history, volt[b], site, level)

    pad_blocks(size, volt_in, put_voltage)
    pad_blocks(size, branch_in, put_branch)
    sent.append(copies.start(vb, vb_out))
    sent.append(copies.start(branch, branch_out))
    sent.append(copies.start(rest, rest_out))

    cols_copy.wait()
    zeros = jnp.zeros((size.width, size.padded - size.width), BF)
    zero_rows = jnp.zeros((size.padded - size.width, 2 * size.padded), BF)
    for i, copy in enumerate(weight_copies):
        copy.wait()

        def turn(b, carry):
            parts = []
            for k in range(size.picks):
                high, low = split_2(raw[b, k].T)
                part = jnp.concatenate([high, zeros, low, zeros], axis=1)
                wp[b, k * size.width : (k + 1) * size.width, :] = part
                parts += [part, zero_rows]
            left = jnp.concatenate([es[cols[k, b]] for k in range(size.picks)], axis=1)
            product = dot(left, jnp.concatenate(parts, axis=0))
            high, low = split_2(product[:, : size.padded] + product[:, size.padded :])
            mt[b] = jnp.concatenate([high, low], axis=1)
            both[:, pl.ds(pl.multiple_of(b * size.padded, LANES), size.padded)] = jnp.concatenate(
                [high, low], axis=0
            )
            return carry

        lax.fori_loop(i * stage, (i + 1) * stage, turn, 0, unroll=4)
        part = pl.ds(i * stage, stage)
        sent.append(copies.start(wp.at[part], wp_out.at[part]))
        sent.append(copies.start(mt.at[part], mt_out.at[part]))

    high, low = split_2(folded(dot(both[...], eg[...])))
    kk[...] = jnp.concatenate([high, low], axis=1)
    sent.append(copies.start(kk, kk_out))
    for copy in sent:
        copy.wait()


def rest_of(size, node_rows, b, history, v, site, level):
    lane = iota((size.scen, size.padded), 1).astype(F32)
    first = jnp.asarray(b * size.padded, I32).astype(F32)
    hit = jnp.where(lane + first == site, level, 0.0)
    return node_rows[b, 0:1, :] - history - hit * v


def for_chunks(size, count, work):
    for c in range(size.chunks):
        if c < 2:
            work(c * size.chunk)
        else:
            pl.when(count > c)(functools.partial(work, c * size.chunk))


def inject(size, count, pair, cs, put):
    step = 2 if size.blocks % 2 == 0 else 1
    width = step * size.padded
    least = min(2, size.chunks)

    def inject_from(used):
        left = pair[:, : used * size.chunk]

        def some_blocks(i, carry):
            lanes = pl.ds(pl.multiple_of(i * width, LANES), width)
            both = folded(dot(left, cs[: used * size.chunk, lanes]))
            for j in range(step):
                put(i * step + j, both[:, block_lanes(size, j)])
            return carry

        lax.fori_loop(0, size.blocks // step, some_blocks, 0, unroll=True)

    for used in range(least, size.chunks + 1):
        if used == least:
            chosen = count <= used
        else:
            chosen = count == used
        pl.when(chosen)(functools.partial(inject_from, used))


def converter_update(size, count, vb, cg, prm, filt, amps, pair):
    def update(first):
        lanes = slice(first, first + size.chunk)
        measured = folded(dot(vb[...], cg[:, lanes]))
        filtered = filt[:, lanes]
        filtered = filtered + prm[2:3, lanes] * (measured - filtered)
        current = amps[:, lanes]
        target = prm[0:1, lanes] * filtered / (1.0 + filtered * filtered)
        current = current + prm[1:2, lanes] * (target - current)
        filt[:, lanes] = filtered
        amps[:, lanes] = current
        pair[:, lanes] = stacked(current)

    for_chunks(size, count, update)


def launch_part(size, history, ends, at_ends, kk, drive_out, far, near):
    drive = jnp.zeros(size.drive, F32)
    for d in range(size.delays):
        drive = jnp.where(ends[0:1, :] == float(d + 1), history(d), drive)
    drive_out[...] = drive
    answer = three_terms(dot(stacked(drive), kk[...]), size.scen, size.ends)
    launch = 2.0 * ends[1:2, :] * (at_ends + answer) - drive
    even = lax.rem(lax.axis_index("region"), 2) == 0
    up, down = launch[:, size.lines :], launch[:, : size.lines]
    far[...] = jnp.where(even, down, up)
    near[...] = jnp.where(even, up, down)


def arrived(size, far, near):
    even = lax.rem(lax.axis_index("region"), 2) == 0
    ahead = jnp.where(even, far[...], near[...])
    after = jnp.where(even, near[...], far[...])
    return jnp.concatenate([ahead, after], axis=1)


def start_kernel(
    size,
    cols_hbm, received, waves_hbm, delay_hbm, admittance_hbm,
    wp_hbm, eg_hbm, mt_hbm, kk_hbm, vb_hbm, branch_hbm, rest_hbm, rows_hbm, fault_hbm,
    wp, eg, mt, kk, waves, ends, node_rows, fault_cols, branch, cg, cs, prm, filt, amps, volt,
    peak, drive, far, near, place_hbm,
    cols, place, delays, admittances, rest, x, vb, pair, moved, moved_settings, sems,
):
    copies = Copies(sems)
    vb_copy = copies.start(vb_hbm, vb)
    rest_copy = copies.start(rest_hbm, rest)
    cols_copy = copies.start(cols_hbm, cols)
    wp_copy = copies.start(wp_hbm, wp)
    later = [
        copies.start(eg_hbm, eg),
        copies.start(delay_hbm, delays),
        copies.start(admittance_hbm, admittances),
        copies.start(waves_hbm, waves),
        copies.start(kk_hbm, kk),
        copies.start(mt_hbm, mt),
        copies.start(branch_hbm, branch),
        copies.start(rows_hbm, node_rows),
        copies.start(fault_hbm, fault_cols),
    ]
    rows, capacity, slots, regions = size.rows, size.capacity, size.slots, size.regions
    total = 0
    for r in range(regions):
        settings = received[r * rows + capacity : r * rows + capacity + 4, :]
        filler = jnp.zeros((LANES - 4, LANES), F32)
        turned = jnp.concatenate([settings[:, :LANES], filler], axis=0).T
        place[r] = total
        moved[pl.ds(total, rows), :] = received[r * rows : (r + 1) * rows, :]
        moved_settings[pl.ds(total, rows), :] = turned[:rows]
        total = total + jnp.sum(jnp.where(settings[3:4, :] > 0.0, 1.0, 0.0)).astype(I32)
    count = lax.div(total + (size.chunk - 1), size.chunk)
    place[regions] = count
    place_copy = copies.start(place, place_hbm)
    for c in range(0, size.slot_lanes, LANES):
        valid = iota((LANES, LANES), 0) + c < total
        turned = jnp.where(valid, moved[c : c + LANES, :], 0.0).T
        filt[:, c : c + LANES] = turned[: size.scen]
        amps[:, c : c + LANES] = turned[size.scen :]
        turned = jnp.where(valid, moved_settings[c : c + LANES, :], 0.0).T
        prm[:, c : c + LANES] = turned[:8]
    row = padded_index(prm[3:4, :] - 1.0, size.width, size.padded)

    def put_products(first):
        for c in range(first, first + size.chunk, LANES):
            def put_gather(n, value, c=c):
                cg[n * LANES : (n + 1) * LANES, c : c + LANES] = value

            def put_scatter(n, value, c=c):
                cs[c : c + LANES, n * LANES : (n + 1) * LANES] = value

            site_products(size, row, c, put_gather, put_scatter)

    for_chunks(size, count, put_products)
    peak[...] = jnp.zeros(peak.shape, F32)

    vb_copy.wait()
    converter_update(size, count, vb, cg, prm, filt, amps, pair)
    rest_copy.wait()

    def put_start(b, injected):
        put_turned(size, x, b, rest[b] + injected)

    inject(size, count, pair, cs, put_start)
    cols_copy.wait()
    wp_copy.wait()
    apply_inverse(size, cols, x, wp, volt, vb)
    for copy in later:
        copy.wait()
    ends[0:1, :] = delays[...].astype(F32)
    ends[1:2, :] = admittances[...]
    at_ends = folded(dot(vb[...], eg[...]))
    launch_part(size, lambda d: waves[d], ends, at_ends, kk, drive, far, near)
    place_copy.wait()


def middle_kernel(
    size, last,
    cols_hbm, place_hbm, drive, wp, eg, mt, node_rows, fault_cols, cg, cs, prm,
    branch_in, filt_in, amps_in, volt_in, peak_in,
    branch, filt, amps, volt, peak, at_ends, *refs,
):
    if last:
        back_hbm, branch_hbm, volt_hbm, peak_hbm, branch_out, moved, back = *refs[:4], *refs[-3:]
        refs = refs[4:-3]
    cols, place, x, vb, pair, sems = refs
    copies = Copies(sems)
    place_copy = copies.start(place_hbm, place)
    cols_copy = copies.start(cols_hbm, cols)
    drives = stacked(drive[...])
    for b in range(size.blocks):
        added = three_terms(dot(drives, mt[b]), size.scen, size.padded)
        v = volt[b] + added
        volt[b] = v
        vb[:, block_lanes(size, b)] = stacked(v)
        magnitude = jnp.abs(v)
        top = magnitude[:8]
        for s in range(8, size.scen, 8):
            top = jnp.maximum(top, magnitude[s : s + 8])
        peak[b] = jnp.maximum(peak[b], top)
    place_copy.wait()
    count = place[size.regions]
    converter_update(size, count, vb, cg, prm, filt, amps, pair)

    def put_next(b, injected):
        history = node_rows[b, 1:2, :] * branch[b] + node_rows[b, 2:3, :] * volt[b]
        branch[b] = history
        site, level = fault_cols[0], fault_cols[1]
        rest = rest_of(size, node_rows, b, history, volt[b], site, level)
        put_turned(size, x, b, rest + injected)

    inject(size, count, pair, cs, put_next)
    cols_copy.wait()
    if last:
        for c in range(0, size.slot_lanes, LANES):
            part = jnp.concatenate([filt[:, c : c + LANES], amps[:, c : c + LANES]], axis=0)
            moved[c : c + LANES, :] = part.T
        moved[size.slot_lanes :, :] = jnp.zeros((size.rows, 2 * size.scen), F32)
        for r in range(size.regions):
            back[r * size.rows : (r + 1) * size.rows, :] = moved[pl.ds(place[r], size.rows), :]
        unpad_blocks(size, lambda b: branch[b], branch_out)
        sent = [
            copies.start(back, back_hbm),
            copies.start(branch_out, branch_hbm),
            copies.start(peak, peak_hbm),
        ]
    apply_inverse(size, cols, x, wp, volt, vb)
    if last:
        sent.append(copies.start(volt, volt_hbm))
    at_ends[...] = folded(dot(vb[...], eg[...]))
    if last:
        for copy in sent:
            copy.wait()


def launch_kernel(size, done, last, at_ends, kk, ends, waves, *refs):
    arrivals, refs = refs[: 2 * done], refs[2 * done :]

    def history(d):
        if d >= done:
            return waves[d - done]
        return arrived(size, arrivals[2 * d], arrivals[2 * d + 1])

    if last:
        refs = refs[1:]
    drive, far, near = refs[:3]
    if last:
        drive_hbm = drive
        _, waves_out, recent, drive, sems = refs[3:]
        copies = Copies(sems)
        for d in range(done):
            recent[d] = history(d)
        sent = [copies.start(recent, waves_out.at[pl.ds(1, done)])]
        kept = size.delays - 1 - done
        sent.append(copies.start(waves.at[pl.ds(0, kept)], waves_out.at[pl.ds(1 + done, kept)]))
    launch_part(size, history, ends, at_ends[...], kk, drive, far, near)
    if last:
        sent.append(copies.start(drive, drive_hbm))
        for copy in sent:
            copy.wait()


def final_kernel(
    size, drive_hbm, volt_hbm, mt_hbm, peak_hbm, voltage_hbm, top_hbm,
    drive, volt, mt, peak, voltage_out, peak_row, peak_out, sems,
):
    copies = Copies(sems)
    drive_copy = copies.start(drive_hbm, drive)
    half = size.blocks // 2
    parts = []
    for i in range(2):
        part = pl.ds(i * half, half)
        parts.append(
            [copies.start(volt_hbm.at[part], volt.at[part]), copies.start(mt_hbm.at[part], mt.at[part])]
        )
    peak_copy = copies.start(peak_hbm, peak)
    drive_copy.wait()
    pair = stacked(drive[...])
    for b in range(size.blocks):
        if b % half == 0:
            for copy in parts[b // half]:
                copy.wait()
        volt[b] = volt[b] + three_terms(dot(pair, mt[b]), size.scen, size.padded)
    peak_copy.wait()

    def largest(b):
        top = jnp.max(jnp.abs(volt[b]), axis=0, keepdims=True)
        return jnp.maximum(top, jnp.max(peak[b], axis=0, keepdims=True))

    unpad_blocks(size, largest, peak_row)
    for i in range(peak_out.shape[0]):
        peak_out[i : i + 1, :] = peak_row[:, i * LANES : (i + 1) * LANES]
    sent = [copies.start(peak_out, top_hbm)]
    unpad_blocks(size, lambda b: volt[b], voltage_out)
    sent.append(copies.start(voltage_out, voltage_hbm))
    for copy in sent:
        copy.wait()


def end_kernel(
    size, dst_hbm, received, far, near, waves_in, state_hbm, waves_out,
    dst, newest, state_out, sems,
):
    copies = Copies(sems)
    dst_copy = copies.start(dst_hbm, dst)
    newest[0] = arrived(size, far, near)
    sent = [copies.start(newest, waves_out.at[pl.ds(0, 1)])]
    parts = jnp.concatenate(split_3(received[...].T), axis=0)
    dst_copy.wait()
    select = one_hot(iota((size.slots, size.convs), 0) == dst[...])
    state = dot(parts, select)
    width = 2 * size.scen
    state = state[:width] + state[width : 2 * width] + state[2 * width :]
    state_out[0] = state[: size.scen]
    state_out[1] = state[size.scen :]
    sent.append(copies.start(state_out, state_hbm))
    for copy in sent:
        copy.wait()


def shape(dims, dtype=F32):
    return jax.ShapeDtypeStruct(dims, dtype)


def in_vmem(*values):
    return [pltpu.with_memory_space_constraint(v, pltpu.VMEM) for v in values]


def in_hbm(*values):
    return [pltpu.with_memory_space_constraint(v, pltpu.HBM) for v in values]


def call(kernel, name, outs, out_specs, args, specs, scratch, limit, aliases=None):
    return pl.pallas_call(
        kernel,
        name=name,
        out_shape=outs,
        in_specs=specs,
        out_specs=out_specs,
        scratch_shapes=list(scratch),
        input_output_aliases=aliases or {},
        compiler_params=pltpu.CompilerParams(vmem_limit_bytes=limit << 20),
    )(*args)


def shards(
    inverse_blocks, block_cols, source_current, node_decay, node_gain, voltage_init, branch_init,
    wave_init, line_node, line_delay, line_admittance, conv_region, conv_node, conv_power,
    conv_gains, conv_init, fault_node, fault_kind,
):
    size = Sizes(inverse_blocks, voltage_init, wave_init, line_node, conv_node)
    regions, rows, scen = size.regions, size.rows, size.scen
    near_pairs = [(i, i ^ 1) for i in range(regions)]
    far_pairs = [(i, (i - 1 if i % 2 == 0 else i + 1) % regions) for i in range(regions)]
    dma = pltpu.SemaphoreType.DMA
    vmem, hbm = pltpu.VMEM, pltpu.HBM

    def row(vector):
        return vector.reshape(1, -1)

    chunk = (regions, rows, 2 * scen)
    packed, dst = call(
        functools.partial(pack_kernel, size),
        "pack",
        [hbm(chunk, F32), hbm((1, size.convs), I32)],
        [HBM] * 2,
        in_hbm(row(conv_region), conv_power, conv_node, conv_gains, conv_init),
        [HBM] * 5,
        [
            vmem((1, size.convs), I32),
            vmem(conv_power.shape, F32),
            vmem(conv_node.shape, I32),
            vmem(conv_gains.shape, F32),
            vmem(conv_init.shape, F32),
            vmem(chunk, F32),
            vmem((1, size.convs), I32),
            dma((8,)),
        ],
        16,
    )
    received = lax.all_to_all(packed, "region", split_axis=0, concat_axis=0, tiled=True)
    received = received.reshape(size.slots, 2 * scen)

    cols = block_cols.T
    cols_scratch = pltpu.SMEM(cols.shape, I32)
    x_scratch = vmem(size.turned, BF)
    wide_scratch = vmem(size.wide, BF)
    place_scratch = pltpu.SMEM((LANES,), I32)
    pair_scratch = vmem((2 * scen, size.slot_lanes), BF)
    moved_scratch = vmem((size.slot_lanes + rows, 2 * scen), F32)
    kept = [
        (size.weights, BF),
        (size.site_rows, BF),
        (size.response, BF),
        (size.coupling, BF),
        (size.wide, BF),
        (size.state, F32),
        (size.state, F32),
        (size.node_rows, F32),
        (size.fault_cols, F32),
    ]
    vectors = (3, 1, size.nodes)
    args = [
        cols, inverse_blocks, row(source_current), row(node_decay), row(node_gain), voltage_init,
        branch_init, row(line_node), row(fault_node), row(fault_kind),
    ]
    wp_hbm, eg_hbm, mt_hbm, kk_hbm, vb_hbm, branch_hbm, rest_hbm, rows_hbm, fault_hbm = call(
        functools.partial(prep_kernel, size),
        "prep",
        [hbm(*item) for item in kept],
        [HBM] * len(kept),
        in_hbm(*args),
        [HBM] * len(args),
        [
            cols_scratch,
            vmem(inverse_blocks.shape, F32),
            vmem(vectors, F32),
            vmem(voltage_init.shape, F32),
            vmem(voltage_init.shape, F32),
            vmem((1, size.ends), I32),
            vmem((2, scen), I32),
            vmem(size.weights, BF),
            vmem(size.site_rows, BF),
            vmem((size.blocks, size.ends, size.padded), BF),
            vmem(size.response, BF),
            vmem((2 * size.ends, size.lanes), BF),
            vmem(size.coupling, BF),
            wide_scratch,
            vmem(size.state, F32),
            vmem(size.state, F32),
            vmem(size.state, F32),
            vmem(size.node_rows, F32),
            vmem(size.fault_cols, F32),
            dma((40,)),
        ],
        48,
    )

    slot_state = vmem((scen, size.slot_lanes), F32)
    outs = [
        vmem(size.weights, BF),
        vmem(size.site_rows, BF),
        vmem(size.response, BF),
        vmem(size.coupling, BF),
        vmem(wave_init.shape, F32),
        vmem((8, size.ends), F32),
        vmem(size.node_rows, F32),
        vmem(size.fault_cols, F32),
        vmem(size.state, F32),
        vmem((size.lanes, size.slot_lanes), BF),
        vmem((size.slot_lanes, size.lanes), BF),
        vmem((8, size.slot_lanes), F32),
        slot_state,
        slot_state,
        vmem(size.state, F32),
        vmem(size.node_rows, F32),
        vmem(size.drive, F32),
        shape(size.exchange),
        shape(size.exchange),
        hbm((LANES,), I32),
    ]
    args = [
        cols, received, wave_init, row(line_delay), row(line_admittance), wp_hbm, eg_hbm,
        mt_hbm, kk_hbm, vb_hbm, branch_hbm, rest_hbm, rows_hbm, fault_hbm,
    ]
    (
        wp, eg, mt, kk, waves, ends, node_rows, fault_cols, branch, cg, cs, prm, filt, amps, volt,
        peak, drive, far, near, place,
    ) = call(
        functools.partial(start_kernel, size),
        "start",
        outs,
        [VMEM] * (len(outs) - 1) + [HBM],
        in_hbm(cols) + in_vmem(received) + in_hbm(*args[2:]),
        [HBM, VMEM] + [HBM] * (len(args) - 2),
        [
            cols_scratch,
            place_scratch,
            vmem((1, size.ends), I32),
            vmem((1, size.ends), F32),
            vmem(size.state, F32),
            x_scratch,
            wide_scratch,
            pair_scratch,
            moved_scratch,
            moved_scratch,
            dma((16,)),
        ],
        10,
    )

    arrivals = []
    for step in range(1, STEPS):
        last = step == STEPS - 1
        from_far = lax.ppermute(far, "region", far_pairs)
        from_near = lax.ppermute(near, "region", near_pairs)
        outs = [
            vmem(size.state, F32),
            slot_state,
            slot_state,
            vmem(size.state, F32),
            vmem(size.node_rows, F32),
            vmem(size.drive, F32),
        ]
        specs = [VMEM] * len(outs)
        scratch = [cols_scratch, place_scratch, x_scratch, wide_scratch, pair_scratch, dma((6,))]
        if last:
            outs += [
                hbm((size.slots, 2 * scen), F32),
                hbm((scen, size.nodes), F32),
                hbm(size.state, F32),
                hbm(size.node_rows, F32),
            ]
            specs += [HBM] * 4
            scratch += [
                vmem((scen, size.nodes), F32),
                moved_scratch,
                vmem((size.slots, 2 * scen), F32),
            ]
        result = call(
            functools.partial(middle_kernel, size, last),
            "middle",
            outs,
            specs,
            in_hbm(cols, place)
            + in_vmem(
                drive, wp, eg, mt, node_rows, fault_cols, cg, cs, prm, branch, filt, amps, volt, peak
            ),
            [HBM] * 2 + [VMEM] * 14,
            scratch,
            12,
            {11: 0, 12: 1, 13: 2, 14: 3, 15: 4},
        )
        branch, filt, amps, volt, peak, at_ends = result[:6]
        arrivals = [from_far, from_near] + arrivals
        args = in_vmem(at_ends, kk, ends, waves) + arrivals
        outs = [vmem(size.drive, F32), shape(size.exchange), shape(size.exchange)]
        in_specs, specs, scratch, aliases = [VMEM] * len(args), [VMEM] * 3, [], {}
        if last:
            back, branch_out, volt, peak = result[6:]
            aliases = {len(args): 3}
            args += in_hbm(back)
            in_specs.append(HBM)
            outs[0] = hbm(size.drive, F32)
            outs += [hbm((size.slots, 2 * scen), F32), hbm(wave_init.shape, F32)]
            specs[0] = HBM
            specs += [HBM, HBM]
            scratch = [vmem((step, *size.drive), F32), vmem(size.drive, F32), dma((4,))]
        drive, far, near, *rest = call(
            functools.partial(launch_kernel, size, step, last),
            "launch",
            outs,
            specs,
            args,
            in_specs,
            scratch,
            4,
            aliases,
        )
    chunks, waves_out = rest
    from_far = lax.ppermute(far, "region", far_pairs)
    from_near = lax.ppermute(near, "region", near_pairs)
    chunks = chunks.reshape(regions, rows, 2 * scen)
    returned = lax.all_to_all(chunks, "region", split_axis=0, concat_axis=0, tiled=True)
    voltage_out, peak_out = call(
        functools.partial(final_kernel, size),
        "final",
        [hbm((scen, size.nodes), F32), hbm((size.nodes // LANES, LANES), F32)],
        [HBM] * 2,
        in_hbm(drive, volt, mt_hbm, peak),
        [HBM] * 4,
        [
            vmem(size.drive, F32),
            vmem(size.state, F32),
            vmem(size.response, BF),
            vmem(size.node_rows, F32),
            vmem((scen, size.nodes), F32),
            vmem((1, size.nodes), F32),
            vmem((size.nodes // LANES, LANES), F32),
            dma((8,)),
        ],
        12,
    )
    others = lax.axis_size("scen")
    peaks = []
    for d in range(1, others):
        if others & (others - 1):
            shift = [(i, (i + d) % others) for i in range(others)]
        else:
            shift = [(i, i ^ d) for i in range(others)]
        peaks.append(lax.ppermute(peak_out, "scen", shift))
    returned = returned.reshape(size.slots, 2 * scen)
    conv_state, wave_history = call(
        functools.partial(end_kernel, size),
        "end",
        [hbm(conv_init.shape, F32), hbm(wave_init.shape, F32)],
        [HBM] * 2,
        in_hbm(dst) + in_vmem(returned, from_far, from_near) + in_hbm(waves_out),
        [HBM, VMEM, VMEM, VMEM, HBM],
        [
            vmem(dst.shape, I32),
            vmem((1, *size.drive), F32),
            vmem(conv_init.shape, F32),
            dma((3,)),
        ],
        16,
        {4: 1},
    )
    envelope, conv_state = lax.optimization_barrier((peak_out, conv_state))
    for peak in peaks:
        envelope = jnp.maximum(envelope, peak)
    return voltage_out, branch_out, wave_history, conv_state, envelope.reshape(-1)


def solution(mesh):
    placed = (
        P("region", None, None, None),
        P("region", None),
        P("region"),
        P("region"),
        P("region"),
        P("scen", "region"),
        P("scen", "region"),
        P(None, "scen", "region"),
        P("region"),
        P("region"),
        P("region"),
        P("region", None),
        P("region"),
        P("region"),
        P(None, "region"),
        P(None, "scen", "region"),
        P("scen"),
        P("scen"),
    )
    return jax.shard_map(
        shards,
        mesh=mesh,
        in_specs=placed,
        out_specs=(
            P("scen", "region"),
            P("scen", "region"),
            P(None, "scen", "region"),
            P(None, "scen", "region"),
            P("region"),
        ),
        check_vma=False,
    )
```

```python
import functools
import math

import jax
import jax.numpy as jnp
from jax import lax
from jax.experimental import pallas as pl
from jax.experimental.pallas import tpu as pltpu
from jax.sharding import PartitionSpec as P

STEPS = 4
LANES = 128
BF = jnp.bfloat16
F32 = jnp.float32
I32 = jnp.int32
VMEM = pl.BlockSpec(memory_space=pltpu.VMEM)
SMEM = pl.BlockSpec(memory_space=pltpu.SMEM)
HBM = pl.BlockSpec(memory_space=pltpu.HBM)


def round_up(value, unit):
    return -(-value // unit) * unit


def iota(shape, dim):
    return lax.broadcasted_iota(I32, shape, dim)


def split_2(value):
    high = value.astype(BF)
    return high, (value - high.astype(F32)).astype(BF)


def split_3(value):
    high = value.astype(BF)
    rest = value - high.astype(F32)
    middle = rest.astype(BF)
    return high, middle, (rest - middle.astype(F32)).astype(BF)


def stacked(value):
    high, low = split_2(value)
    return jnp.concatenate([high, low], axis=0)


def folded(value):
    half = value.shape[0] // 2
    return value[:half] + value[half:]


def dot(left, right):
    return jnp.dot(left, right, preferred_element_type=F32)


def one_hot(mask):
    return jnp.where(mask, 1.0, 0.0).astype(BF)


def padded_index(nodes, width, padded):
    block = jnp.floor((nodes + 0.5) * (1.0 / width))
    return nodes + block * (padded - width)


class Sizes:
    def __init__(self, inverse_blocks, voltage, wave_init, line_node, conv_node):
        self.blocks, self.picks, self.width, _ = inverse_blocks.shape
        self.scen, self.nodes = voltage.shape
        self.delays = wave_init.shape[0]
        self.ends = line_node.shape[0]
        self.lines = self.ends // 2
        self.convs = conv_node.shape[0]
        self.regions = lax.axis_size("region")
        self.capacity = max(2, 12 * self.convs // (5 * self.regions))
        self.rows = round_up(self.capacity + 4, 8)
        self.slots = self.regions * self.rows
        self.slot_lanes = round_up(self.slots, 2 * LANES)
        self.padded = round_up(self.width, LANES)
        self.lanes = self.blocks * self.padded
        self.group = math.lcm(self.width, LANES) // self.width

        self.state = (self.blocks, self.scen, self.padded)
        starts = [k * self.width for k in range(self.picks)]
        self.starts = starts
        self.shifts = sorted({start % LANES for start in starts})
        self.depth = round_up(self.picks * self.width, LANES)
        self.turned = (len(self.shifts), self.blocks, 2 * self.scen, self.padded)
        self.chunk = min(2 * LANES, self.slot_lanes)
        self.chunks = self.slot_lanes // self.chunk
        self.wide = (2 * self.scen, self.lanes)
        self.weights = (self.blocks, self.picks * self.width, 2 * self.padded)
        self.site_rows = (self.lanes, self.ends)
        self.response = (self.blocks, self.ends, 2 * self.padded)
        self.coupling = (self.ends, 2 * self.ends)
        self.node_rows = (self.blocks, 8, self.padded)
        self.fault_cols = (2, self.scen, self.padded)
        self.drive = (self.scen, self.ends)
        self.exchange = (self.scen, self.lines)


class Copies:
    def __init__(self, sems):
        self.sems = sems
        self.count = 0

    def start(self, source, target):
        copy = pltpu.make_async_copy(source, target, self.sems.at[self.count])
        self.count += 1
        copy.start()
        return copy


def pad_blocks(size, source, store):
    group_width = size.group * size.width
    for first in range(0, size.blocks, size.group):
        chunk = source[:, first * size.width : first * size.width + group_width]
        for j in range(size.group):
            part = chunk[:, j * size.width : (j + 1) * size.width]
            zeros = jnp.zeros((part.shape[0], size.padded - size.width), part.dtype)
            store(first + j, jnp.concatenate([part, zeros], axis=1))


def unpad_blocks(size, load, target):
    group_width = size.group * size.width
    for first in range(0, size.blocks, size.group):
        parts = [load(first + j)[:, : size.width] for j in range(size.group)]
        target[:, first * size.width : first * size.width + group_width] = jnp.concatenate(
            parts, axis=1
        )


def block_lanes(size, b):
    return slice(b * size.padded, (b + 1) * size.padded)


def pack_kernel(
    size, region_hbm, power_hbm, node_hbm, gains_hbm, init_hbm, out_hbm, dst_hbm,
    region, power, node, gains, init, out, dst_out, sems,
):
    convs, slots = size.convs, size.slots
    copies = Copies(sems)
    first = copies.start(region_hbm, region)
    second = copies.start(init_hbm, init)
    others = [
        copies.start(power_hbm, power),
        copies.start(node_hbm, node),
        copies.start(gains_hbm, gains),
    ]
    first.wait()
    target = region[...]
    member = iota((round_up(size.regions, 16), convs), 0) == target
    before = one_hot(iota((convs, convs), 0) < iota((convs, convs), 1))
    earlier = dot(one_hot(member), before)
    rank = jnp.sum(jnp.where(member, earlier, 0.0), axis=0, keepdims=True)
    dst = target * size.rows + rank.astype(I32)
    dst_out[...] = dst
    select = one_hot(iota((slots, convs), 0) == dst)
    sent = [copies.start(dst_out, dst_hbm)]
    for copy in others:
        copy.wait()
    rows = [
        power[...].reshape(1, convs),
        gains[...],
        node[...].astype(F32).reshape(1, convs) + 1.0,
        jnp.zeros((LANES - 4, convs), F32),
    ]
    settings = jnp.concatenate(rows, axis=0)
    second.wait()
    state = jnp.concatenate([init[0], init[1]], axis=0)
    payload = jnp.concatenate([state.T, settings.T], axis=1)
    width = state.shape[0]
    rows = sum(dot(select, part) for part in split_3(payload))
    for r in range(size.regions):
        chunk = rows[r * size.rows : (r + 1) * size.rows]
        out[r] = chunk[:, :width]
        filler = jnp.zeros((LANES - size.rows, LANES), F32)
        turned = jnp.concatenate([chunk[:, width:], filler], axis=0).T
        out[r, size.capacity : size.capacity + 4, :] = turned[:4]
    sent.append(copies.start(out, out_hbm))
    for copy in sent:
        copy.wait()


def fault_terms(size, node, kind):
    first = lax.axis_index("region") * size.nodes
    local = (node[...] - first).astype(F32)
    inside = (local >= 0.0) & (local < size.nodes)
    site = jnp.where(inside, padded_index(local, size.width, size.padded), -1.0)
    level = 0.25 * jnp.left_shift(1, kind[...]).astype(F32)
    square = (size.scen, size.scen)
    diagonal = iota(square, 0) == iota(square, 1)

    def column(row):
        spread = jnp.where(diagonal, jnp.broadcast_to(row, square), 0.0)
        return jnp.broadcast_to(jnp.sum(spread, axis=1, keepdims=True), (size.scen, size.padded))

    return column(site), column(level)


def site_products(size, row, chunk, gather, scatter):
    part = row[:, chunk : chunk + LANES]
    block = jnp.floor((part + 0.5) * (1.0 / LANES))
    lane = part - block * LANES
    square = (LANES, LANES)
    down_block = jnp.broadcast_to(block, square).astype(BF)
    across_block = turned_row(block).astype(BF)
    down_lane = one_hot(lane == iota(square, 0).astype(F32))
    across_lane = one_hot(turned_row(lane) == iota(square, 1).astype(F32))
    zeros = jnp.zeros(square, BF)
    for n in range(size.lanes // LANES):
        here = jnp.asarray(n, BF)
        gather(n, jnp.where(down_block == here, down_lane, zeros))
        scatter(n, jnp.where(across_block == here, across_lane, zeros))


def turned_row(row):
    return jnp.broadcast_to(row, (LANES, row.shape[1])).T


def put_turned(size, x, b, value):
    pair = stacked(value)
    for i, shift in enumerate(size.shifts):
        x[i, b] = pltpu.roll(pair, shift, 1) if shift else pair


def picked_product(size, cols, b, x, wp):
    lane = iota((2 * size.scen, LANES), 1)
    tiles = []
    for first in range(0, size.depth, LANES):
        tile = None
        for k, start in enumerate(size.starts):
            if start + size.width <= first or start >= first + LANES:
                continue
            piece = x[size.shifts.index(start % LANES), cols[k, b]]
            tile = piece if tile is None else jnp.where(lane < start - first, tile, piece)
        tiles.append(tile)
    spare = size.depth - size.picks * size.width
    weights = wp[b]
    if spare:
        weights = jnp.concatenate([weights, jnp.zeros((spare, weights.shape[1]), BF)], axis=0)
    return dot(jnp.concatenate(tiles, axis=1), weights)


def three_terms(product, rows, width):
    top, low = product[:rows], product[rows:]
    return top[:, :width] + top[:, width:] + low[:, :width]


def apply_inverse(size, cols, x, wp, volt, vb):
    def block_row(b, carry):
        value = three_terms(picked_product(size, cols, b, x, wp), size.scen, size.padded)
        volt[b] = value
        vb[:, pl.ds(pl.multiple_of(b * size.padded, LANES), size.padded)] = stacked(value)
        return carry

    lax.fori_loop(0, size.blocks, block_row, 0, unroll=16)


def prep_kernel(
    size,
    cols_hbm, inverse, source, decay, gain, voltage, branch_init, line_node, fault_node, fault_kind,
    wp_out, eg_out, mt_out, kk_out, vb_out, branch_out, rest_out, rows_out, fault_out,
    cols, raw, vectors, volt_in, branch_in, nodes, faults,
    wp, eg, es, mt, both, kk, vb, volt, branch, rest, node_rows, fault_cols,
    sems,
):
    copies = Copies(sems)
    cols_copy = copies.start(cols_hbm, cols)
    small = [
        copies.start(line_node, nodes),
        copies.start(fault_node, faults.at[0:1]),
        copies.start(fault_kind, faults.at[1:2]),
    ]
    small += [copies.start(v, vectors.at[i]) for i, v in enumerate((source, decay, gain))]
    large = [copies.start(voltage, volt_in), copies.start(branch_init, branch_in)]
    stages = 4
    stage = size.blocks // stages
    weight_copies = []
    for i in range(stages):
        part = pl.ds(i * stage, stage)
        weight_copies.append(copies.start(inverse.at[part], raw.at[part]))
    sent = []
    for copy in small:
        copy.wait()

    row = padded_index(nodes[...].astype(F32), size.width, size.padded)
    for c in range(0, size.ends, LANES):
        def put_gather(n, value, c=c):
            eg[n * LANES : (n + 1) * LANES, c : c + LANES] = value

        def put_scatter(n, value, c=c):
            b, lane = n * LANES // size.padded, n * LANES % size.padded
            es[b, c : c + LANES, lane : lane + LANES] = value

        site_products(size, row, c, put_gather, put_scatter)
    sent.append(copies.start(eg, eg_out))

    for i in range(3):
        def put_row(b, value, i=i):
            node_rows[b, i : i + 1, :] = value

        pad_blocks(size, vectors.at[i], put_row)
    sent.append(copies.start(node_rows, rows_out))
    site, level = fault_terms(size, faults.at[0:1], faults.at[1:2])
    fault_cols[0] = site
    fault_cols[1] = level
    sent.append(copies.start(fault_cols, fault_out))
    for copy in large:
        copy.wait()

    def put_voltage(b, value):
        volt[b] = value
        vb[:, block_lanes(size, b)] = stacked(value)

    def put_branch(b, value):
        history = node_rows[b, 1:2, :] * value + node_rows[b, 2:3, :] * volt[b]
        branch[b] = history
        rest[b] = rest_of(size, node_rows, b, history, volt[b], site, level)

    pad_blocks(size, volt_in, put_voltage)
    pad_blocks(size, branch_in, put_branch)
    sent.append(copies.start(vb, vb_out))
    sent.append(copies.start(branch, branch_out))
    sent.append(copies.start(rest, rest_out))

    cols_copy.wait()
    zeros = jnp.zeros((size.width, size.padded - size.width), BF)
    zero_rows = jnp.zeros((size.padded - size.width, 2 * size.padded), BF)
    for i, copy in enumerate(weight_copies):
        copy.wait()

        def turn(b, carry):
            parts = []
            for k in range(size.picks):
                high, low = split_2(raw[b, k].T)
                part = jnp.concatenate([high, zeros, low, zeros], axis=1)
                wp[b, k * size.width : (k + 1) * size.width, :] = part
                parts += [part, zero_rows]
            left = jnp.concatenate([es[cols[k, b]] for k in range(size.picks)], axis=1)
            product = dot(left, jnp.concatenate(parts, axis=0))
            high, low = split_2(product[:, : size.padded] + product[:, size.padded :])
            mt[b] = jnp.concatenate([high, low], axis=1)
            both[:, pl.ds(pl.multiple_of(b * size.padded, LANES), size.padded)] = jnp.concatenate(
                [high, low], axis=0
            )
            return carry

        lax.fori_loop(i * stage, (i + 1) * stage, turn, 0, unroll=4)
        part = pl.ds(i * stage, stage)
        sent.append(copies.start(wp.at[part], wp_out.at[part]))
        sent.append(copies.start(mt.at[part], mt_out.at[part]))

    high, low = split_2(folded(dot(both[...], eg[...])))
    kk[...] = jnp.concatenate([high, low], axis=1)
    sent.append(copies.start(kk, kk_out))
    for copy in sent:
        copy.wait()


def rest_of(size, node_rows, b, history, v, site, level):
    lane = iota((size.scen, size.padded), 1).astype(F32)
    first = jnp.asarray(b * size.padded, I32).astype(F32)
    hit = jnp.where(lane + first == site, level, 0.0)
    return node_rows[b, 0:1, :] - history - hit * v


def for_chunks(size, count, work):
    for c in range(size.chunks):
        if c < 2:
            work(c * size.chunk)
        else:
            pl.when(count > c)(functools.partial(work, c * size.chunk))


def inject(size, count, pair, cs, put):
    step = 2 if size.blocks % 2 == 0 else 1
    width = step * size.padded
    least = min(2, size.chunks)

    def inject_from(used):
        left = pair[:, : used * size.chunk]

        def some_blocks(i, carry):
            lanes = pl.ds(pl.multiple_of(i * width, LANES), width)
            both = folded(dot(left, cs[: used * size.chunk, lanes]))
            for j in range(step):
                put(i * step + j, both[:, block_lanes(size, j)])
            return carry

        lax.fori_loop(0, size.blocks // step, some_blocks, 0, unroll=True if used == least else 4)

    for used in range(least, size.chunks + 1):
        if used == least:
            chosen = count <= used
        else:
            chosen = count == used
        pl.when(chosen)(functools.partial(inject_from, used))


def converter_update(size, count, vb, cg, prm, filt, amps, pair):
    def update(first):
        lanes = slice(first, first + size.chunk)
        measured = folded(dot(vb[...], cg[:, lanes]))
        filtered = filt[:, lanes]
        filtered = filtered + prm[2:3, lanes] * (measured - filtered)
        current = amps[:, lanes]
        target = prm[0:1, lanes] * filtered / (1.0 + filtered * filtered)
        current = current + prm[1:2, lanes] * (target - current)
        filt[:, lanes] = filtered
        amps[:, lanes] = current
        pair[:, lanes] = stacked(current)

    for_chunks(size, count, update)


def launch_part(size, history, ends, at_ends, kk, drive_out, far, near):
    drive = jnp.zeros(size.drive, F32)
    for d in range(size.delays):
        drive = jnp.where(ends[0:1, :] == float(d + 1), history(d), drive)
    drive_out[...] = drive
    answer = three_terms(dot(stacked(drive), kk[...]), size.scen, size.ends)
    launch = 2.0 * ends[1:2, :] * (at_ends + answer) - drive
    even = lax.rem(lax.axis_index("region"), 2) == 0
    up, down = launch[:, size.lines :], launch[:, : size.lines]
    far[...] = jnp.where(even, down, up)
    near[...] = jnp.where(even, up, down)


def arrived(size, far, near):
    even = lax.rem(lax.axis_index("region"), 2) == 0
    ahead = jnp.where(even, far[...], near[...])
    after = jnp.where(even, near[...], far[...])
    return jnp.concatenate([ahead, after], axis=1)


def start_kernel(
    size,
    cols_hbm, received, waves_hbm, delay_hbm, admittance_hbm,
    wp_hbm, eg_hbm, mt_hbm, kk_hbm, vb_hbm, branch_hbm, rest_hbm, rows_hbm, fault_hbm,
    wp, eg, mt, kk, waves, ends, node_rows, fault_cols, branch, cg, cs, prm, filt, amps, volt,
    peak, drive, far, near, place_hbm,
    cols, place, delays, admittances, rest, x, vb, pair, moved, moved_settings, sems,
):
    copies = Copies(sems)
    vb_copy = copies.start(vb_hbm, vb)
    rest_copy = copies.start(rest_hbm, rest)
    cols_copy = copies.start(cols_hbm, cols)
    wp_copy = copies.start(wp_hbm, wp)
    later = [
        copies.start(eg_hbm, eg),
        copies.start(delay_hbm, delays),
        copies.start(admittance_hbm, admittances),
        copies.start(waves_hbm, waves),
        copies.start(kk_hbm, kk),
        copies.start(mt_hbm, mt),
        copies.start(branch_hbm, branch),
        copies.start(rows_hbm, node_rows),
        copies.start(fault_hbm, fault_cols),
    ]
    rows, capacity, slots, regions = size.rows, size.capacity, size.slots, size.regions
    total = 0
    for r in range(regions):
        settings = received[r * rows + capacity : r * rows + capacity + 4, :]
        filler = jnp.zeros((LANES - 4, LANES), F32)
        turned = jnp.concatenate([settings[:, :LANES], filler], axis=0).T
        place[r] = total
        moved[pl.ds(total, rows), :] = received[r * rows : (r + 1) * rows, :]
        moved_settings[pl.ds(total, rows), :] = turned[:rows]
        total = total + jnp.sum(jnp.where(settings[3:4, :] > 0.0, 1.0, 0.0)).astype(I32)
    count = lax.div(total + (size.chunk - 1), size.chunk)
    place[regions] = count
    place_copy = copies.start(place, place_hbm)
    for c in range(0, size.slot_lanes, LANES):
        valid = iota((LANES, LANES), 0) + c < total
        turned = jnp.where(valid, moved[c : c + LANES, :], 0.0).T
        filt[:, c : c + LANES] = turned[: size.scen]
        amps[:, c : c + LANES] = turned[size.scen :]
        turned = jnp.where(valid, moved_settings[c : c + LANES, :], 0.0).T
        prm[:, c : c + LANES] = turned[:8]
    row = padded_index(prm[3:4, :] - 1.0, size.width, size.padded)

    def put_products(first):
        for c in range(first, first + size.chunk, LANES):
            def put_gather(n, value, c=c):
                cg[n * LANES : (n + 1) * LANES, c : c + LANES] = value

            def put_scatter(n, value, c=c):
                cs[c : c + LANES, n * LANES : (n + 1) * LANES] = value

            site_products(size, row, c, put_gather, put_scatter)

    for_chunks(size, count, put_products)
    peak[...] = jnp.zeros(peak.shape, F32)

    vb_copy.wait()
    converter_update(size, count, vb, cg, prm, filt, amps, pair)
    rest_copy.wait()

    def put_start(b, injected):
        put_turned(size, x, b, rest[b] + injected)

    inject(size, count, pair, cs, put_start)
    cols_copy.wait()
    wp_copy.wait()
    apply_inverse(size, cols, x, wp, volt, vb)
    for copy in later:
        copy.wait()
    ends[0:1, :] = delays[...].astype(F32)
    ends[1:2, :] = admittances[...]
    at_ends = folded(dot(vb[...], eg[...]))
    launch_part(size, lambda d: waves[d], ends, at_ends, kk, drive, far, near)
    place_copy.wait()


def middle_kernel(
    size, last,
    cols_hbm, place_hbm, drive, wp, eg, mt, node_rows, fault_cols, cg, cs, prm,
    branch_in, filt_in, amps_in, volt_in, peak_in,
    branch, filt, amps, volt, peak, at_ends, *refs,
):
    if last:
        back_hbm, branch_hbm, volt_hbm, peak_hbm, branch_out, moved, back = *refs[:4], *refs[-3:]
        refs = refs[4:-3]
    cols, place, x, vb, pair, sems = refs
    copies = Copies(sems)
    place_copy = copies.start(place_hbm, place)
    cols_copy = copies.start(cols_hbm, cols)
    drives = stacked(drive[...])
    for b in range(size.blocks):
        added = three_terms(dot(drives, mt[b]), size.scen, size.padded)
        v = volt[b] + added
        volt[b] = v
        vb[:, block_lanes(size, b)] = stacked(v)
        magnitude = jnp.abs(v)
        top = magnitude[:8]
        for s in range(8, size.scen, 8):
            top = jnp.maximum(top, magnitude[s : s + 8])
        peak[b] = jnp.maximum(peak[b], top)
    place_copy.wait()
    count = place[size.regions]
    converter_update(size, count, vb, cg, prm, filt, amps, pair)

    def put_next(b, injected):
        history = node_rows[b, 1:2, :] * branch[b] + node_rows[b, 2:3, :] * volt[b]
        branch[b] = history
        site, level = fault_cols[0], fault_cols[1]
        rest = rest_of(size, node_rows, b, history, volt[b], site, level)
        put_turned(size, x, b, rest + injected)

    inject(size, count, pair, cs, put_next)
    cols_copy.wait()
    if last:
        for c in range(0, size.slot_lanes, LANES):
            part = jnp.concatenate([filt[:, c : c + LANES], amps[:, c : c + LANES]], axis=0)
            moved[c : c + LANES, :] = part.T
        moved[size.slot_lanes :, :] = jnp.zeros((size.rows, 2 * size.scen), F32)
        for r in range(size.regions):
            back[r * size.rows : (r + 1) * size.rows, :] = moved[pl.ds(place[r], size.rows), :]
        unpad_blocks(size, lambda b: branch[b], branch_out)
        sent = [
            copies.start(back, back_hbm),
            copies.start(branch_out, branch_hbm),
            copies.start(peak, peak_hbm),
        ]
    apply_inverse(size, cols, x, wp, volt, vb)
    if last:
        sent.append(copies.start(volt, volt_hbm))
    at_ends[...] = folded(dot(vb[...], eg[...]))
    if last:
        for copy in sent:
            copy.wait()


def launch_kernel(size, done, last, at_ends, kk, ends, waves, *refs):
    arrivals, refs = refs[: 2 * done], refs[2 * done :]

    def history(d):
        if d >= done:
            return waves[d - done]
        return arrived(size, arrivals[2 * d], arrivals[2 * d + 1])

    if last:
        refs = refs[1:]
    drive, far, near = refs[:3]
    if last:
        drive_hbm = drive
        _, waves_out, recent, drive, sems = refs[3:]
        copies = Copies(sems)
        for d in range(done):
            recent[d] = history(d)
        sent = [copies.start(recent, waves_out.at[pl.ds(1, done)])]
        kept = size.delays - 1 - done
        sent.append(copies.start(waves.at[pl.ds(0, kept)], waves_out.at[pl.ds(1 + done, kept)]))
    launch_part(size, history, ends, at_ends[...], kk, drive, far, near)
    if last:
        sent.append(copies.start(drive, drive_hbm))
        for copy in sent:
            copy.wait()


def final_kernel(
    size, drive_hbm, volt_hbm, mt_hbm, peak_hbm, voltage_hbm, top_hbm,
    drive, volt, mt, peak, voltage_out, peak_row, peak_out, sems,
):
    copies = Copies(sems)
    drive_copy = copies.start(drive_hbm, drive)
    half = size.blocks // 2
    parts = []
    for i in range(2):
        part = pl.ds(i * half, half)
        parts.append(
            [copies.start(volt_hbm.at[part], volt.at[part]), copies.start(mt_hbm.at[part], mt.at[part])]
        )
    peak_copy = copies.start(peak_hbm, peak)
    drive_copy.wait()
    pair = stacked(drive[...])
    for b in range(size.blocks):
        if b % half == 0:
            for copy in parts[b // half]:
                copy.wait()
        volt[b] = volt[b] + three_terms(dot(pair, mt[b]), size.scen, size.padded)
    peak_copy.wait()

    def largest(b):
        top = jnp.max(jnp.abs(volt[b]), axis=0, keepdims=True)
        return jnp.maximum(top, jnp.max(peak[b], axis=0, keepdims=True))

    unpad_blocks(size, largest, peak_row)
    for i in range(peak_out.shape[0]):
        peak_out[i : i + 1, :] = peak_row[:, i * LANES : (i + 1) * LANES]
    sent = [copies.start(peak_out, top_hbm)]
    unpad_blocks(size, lambda b: volt[b], voltage_out)
    sent.append(copies.start(voltage_out, voltage_hbm))
    for copy in sent:
        copy.wait()


def end_kernel(
    size, dst_hbm, received, far, near, waves_in, state_hbm, waves_out,
    dst, newest, state_out, sems,
):
    copies = Copies(sems)
    dst_copy = copies.start(dst_hbm, dst)
    newest[0] = arrived(size, far, near)
    sent = [copies.start(newest, waves_out.at[pl.ds(0, 1)])]
    parts = jnp.concatenate(split_3(received[...].T), axis=0)
    dst_copy.wait()
    select = one_hot(iota((size.slots, size.convs), 0) == dst[...])
    state = dot(parts, select)
    width = 2 * size.scen
    state = state[:width] + state[width : 2 * width] + state[2 * width :]
    state_out[0] = state[: size.scen]
    state_out[1] = state[size.scen :]
    sent.append(copies.start(state_out, state_hbm))
    for copy in sent:
        copy.wait()


def shape(dims, dtype=F32):
    return jax.ShapeDtypeStruct(dims, dtype)


def in_vmem(*values):
    return [pltpu.with_memory_space_constraint(v, pltpu.VMEM) for v in values]


def in_hbm(*values):
    return [pltpu.with_memory_space_constraint(v, pltpu.HBM) for v in values]


def call(kernel, name, outs, out_specs, args, specs, scratch, limit, aliases=None):
    return pl.pallas_call(
        kernel,
        name=name,
        out_shape=outs,
        in_specs=specs,
        out_specs=out_specs,
        scratch_shapes=list(scratch),
        input_output_aliases=aliases or {},
        compiler_params=pltpu.CompilerParams(vmem_limit_bytes=limit << 20),
    )(*args)


def shards(
    inverse_blocks, block_cols, source_current, node_decay, node_gain, voltage_init, branch_init,
    wave_init, line_node, line_delay, line_admittance, conv_region, conv_node, conv_power,
    conv_gains, conv_init, fault_node, fault_kind,
):
    size = Sizes(inverse_blocks, voltage_init, wave_init, line_node, conv_node)
    regions, rows, scen = size.regions, size.rows, size.scen
    near_pairs = [(i, i ^ 1) for i in range(regions)]
    far_pairs = [(i, (i - 1 if i % 2 == 0 else i + 1) % regions) for i in range(regions)]
    dma = pltpu.SemaphoreType.DMA
    vmem, hbm = pltpu.VMEM, pltpu.HBM

    def row(vector):
        return vector.reshape(1, -1)

    chunk = (regions, rows, 2 * scen)
    packed, dst = call(
        functools.partial(pack_kernel, size),
        "pack",
        [hbm(chunk, F32), hbm((1, size.convs), I32)],
        [HBM] * 2,
        in_hbm(row(conv_region), conv_power, conv_node, conv_gains, conv_init),
        [HBM] * 5,
        [
            vmem((1, size.convs), I32),
            vmem(conv_power.shape, F32),
            vmem(conv_node.shape, I32),
            vmem(conv_gains.shape, F32),
            vmem(conv_init.shape, F32),
            vmem(chunk, F32),
            vmem((1, size.convs), I32),
            dma((8,)),
        ],
        16,
    )
    received = lax.all_to_all(packed, "region", split_axis=0, concat_axis=0, tiled=True)
    received = received.reshape(size.slots, 2 * scen)

    cols = block_cols.T
    cols_scratch = pltpu.SMEM(cols.shape, I32)
    x_scratch = vmem(size.turned, BF)
    wide_scratch = vmem(size.wide, BF)
    place_scratch = pltpu.SMEM((LANES,), I32)
    pair_scratch = vmem((2 * scen, size.slot_lanes), BF)
    moved_scratch = vmem((size.slot_lanes + rows, 2 * scen), F32)
    kept = [
        (size.weights, BF),
        (size.site_rows, BF),
        (size.response, BF),
        (size.coupling, BF),
        (size.wide, BF),
        (size.state, F32),
        (size.state, F32),
        (size.node_rows, F32),
        (size.fault_cols, F32),
    ]
    vectors = (3, 1, size.nodes)
    args = [
        cols, inverse_blocks, row(source_current), row(node_decay), row(node_gain), voltage_init,
        branch_init, row(line_node), row(fault_node), row(fault_kind),
    ]
    wp_hbm, eg_hbm, mt_hbm, kk_hbm, vb_hbm, branch_hbm, rest_hbm, rows_hbm, fault_hbm = call(
        functools.partial(prep_kernel, size),
        "prep",
        [hbm(*item) for item in kept],
        [HBM] * len(kept),
        in_hbm(*args),
        [HBM] * len(args),
        [
            cols_scratch,
            vmem(inverse_blocks.shape, F32),
            vmem(vectors, F32),
            vmem(voltage_init.shape, F32),
            vmem(voltage_init.shape, F32),
            vmem((1, size.ends), I32),
            vmem((2, scen), I32),
            vmem(size.weights, BF),
            vmem(size.site_rows, BF),
            vmem((size.blocks, size.ends, size.padded), BF),
            vmem(size.response, BF),
            vmem((2 * size.ends, size.lanes), BF),
            vmem(size.coupling, BF),
            wide_scratch,
            vmem(size.state, F32),
            vmem(size.state, F32),
            vmem(size.state, F32),
            vmem(size.node_rows, F32),
            vmem(size.fault_cols, F32),
            dma((40,)),
        ],
        48,
    )

    slot_state = vmem((scen, size.slot_lanes), F32)
    outs = [
        vmem(size.weights, BF),
        vmem(size.site_rows, BF),
        vmem(size.response, BF),
        vmem(size.coupling, BF),
        vmem(wave_init.shape, F32),
        vmem((8, size.ends), F32),
        vmem(size.node_rows, F32),
        vmem(size.fault_cols, F32),
        vmem(size.state, F32),
        vmem((size.lanes, size.slot_lanes), BF),
        vmem((size.slot_lanes, size.lanes), BF),
        vmem((8, size.slot_lanes), F32),
        slot_state,
        slot_state,
        vmem(size.state, F32),
        vmem(size.node_rows, F32),
        vmem(size.drive, F32),
        shape(size.exchange),
        shape(size.exchange),
        hbm((LANES,), I32),
    ]
    args = [
        cols, received, wave_init, row(line_delay), row(line_admittance), wp_hbm, eg_hbm,
        mt_hbm, kk_hbm, vb_hbm, branch_hbm, rest_hbm, rows_hbm, fault_hbm,
    ]
    (
        wp, eg, mt, kk, waves, ends, node_rows, fault_cols, branch, cg, cs, prm, filt, amps, volt,
        peak, drive, far, near, place,
    ) = call(
        functools.partial(start_kernel, size),
        "start",
        outs,
        [VMEM] * (len(outs) - 1) + [HBM],
        in_hbm(cols) + in_vmem(received) + in_hbm(*args[2:]),
        [HBM, VMEM] + [HBM] * (len(args) - 2),
        [
            cols_scratch,
            place_scratch,
            vmem((1, size.ends), I32),
            vmem((1, size.ends), F32),
            vmem(size.state, F32),
            x_scratch,
            wide_scratch,
            pair_scratch,
            moved_scratch,
            moved_scratch,
            dma((16,)),
        ],
        10,
    )

    arrivals = []
    for step in range(1, STEPS):
        last = step == STEPS - 1
        from_far = lax.ppermute(far, "region", far_pairs)
        from_near = lax.ppermute(near, "region", near_pairs)
        outs = [
            vmem(size.state, F32),
            slot_state,
            slot_state,
            vmem(size.state, F32),
            vmem(size.node_rows, F32),
            vmem(size.drive, F32),
        ]
        specs = [VMEM] * len(outs)
        scratch = [cols_scratch, place_scratch, x_scratch, wide_scratch, pair_scratch, dma((6,))]
        if last:
            outs += [
                hbm((size.slots, 2 * scen), F32),
                hbm((scen, size.nodes), F32),
                hbm(size.state, F32),
                hbm(size.node_rows, F32),
            ]
            specs += [HBM] * 4
            scratch += [
                vmem((scen, size.nodes), F32),
                moved_scratch,
                vmem((size.slots, 2 * scen), F32),
            ]
        result = call(
            functools.partial(middle_kernel, size, last),
            "middle",
            outs,
            specs,
            in_hbm(cols, place)
            + in_vmem(
                drive, wp, eg, mt, node_rows, fault_cols, cg, cs, prm, branch, filt, amps, volt, peak
            ),
            [HBM] * 2 + [VMEM] * 14,
            scratch,
            12,
            {11: 0, 12: 1, 13: 2, 14: 3, 15: 4},
        )
        branch, filt, amps, volt, peak, at_ends = result[:6]
        arrivals = [from_far, from_near] + arrivals
        args = in_vmem(at_ends, kk, ends, waves) + arrivals
        outs = [vmem(size.drive, F32), shape(size.exchange), shape(size.exchange)]
        in_specs, specs, scratch, aliases = [VMEM] * len(args), [VMEM] * 3, [], {}
        if last:
            back, branch_out, volt, peak = result[6:]
            aliases = {len(args): 3}
            args += in_hbm(back)
            in_specs.append(HBM)
            outs[0] = hbm(size.drive, F32)
            outs += [hbm((size.slots, 2 * scen), F32), hbm(wave_init.shape, F32)]
            specs[0] = HBM
            specs += [HBM, HBM]
            scratch = [vmem((step, *size.drive), F32), vmem(size.drive, F32), dma((4,))]
        drive, far, near, *rest = call(
            functools.partial(launch_kernel, size, step, last),
            "launch",
            outs,
            specs,
            args,
            in_specs,
            scratch,
            4,
            aliases,
        )
    chunks, waves_out = rest
    from_far = lax.ppermute(far, "region", far_pairs)
    from_near = lax.ppermute(near, "region", near_pairs)
    chunks = chunks.reshape(regions, rows, 2 * scen)
    returned = lax.all_to_all(chunks, "region", split_axis=0, concat_axis=0, tiled=True)
    voltage_out, peak_out = call(
        functools.partial(final_kernel, size),
        "final",
        [hbm((scen, size.nodes), F32), hbm((size.nodes // LANES, LANES), F32)],
        [HBM] * 2,
        in_hbm(drive, volt, mt_hbm, peak),
        [HBM] * 4,
        [
            vmem(size.drive, F32),
            vmem(size.state, F32),
            vmem(size.response, BF),
            vmem(size.node_rows, F32),
            vmem((scen, size.nodes), F32),
            vmem((1, size.nodes), F32),
            vmem((size.nodes // LANES, LANES), F32),
            dma((8,)),
        ],
        12,
    )
    others = lax.axis_size("scen")
    peaks = []
    for d in range(1, others):
        if others & (others - 1):
            shift = [(i, (i + d) % others) for i in range(others)]
        else:
            shift = [(i, i ^ d) for i in range(others)]
        peaks.append(lax.ppermute(peak_out, "scen", shift))
    returned = returned.reshape(size.slots, 2 * scen)
    conv_state, wave_history = call(
        functools.partial(end_kernel, size),
        "end",
        [hbm(conv_init.shape, F32), hbm(wave_init.shape, F32)],
        [HBM] * 2,
        in_hbm(dst) + in_vmem(returned, from_far, from_near) + in_hbm(waves_out),
        [HBM, VMEM, VMEM, VMEM, HBM],
        [
            vmem(dst.shape, I32),
            vmem((1, *size.drive), F32),
            vmem(conv_init.shape, F32),
            dma((3,)),
        ],
        16,
        {4: 1},
    )
    envelope, conv_state = lax.optimization_barrier((peak_out, conv_state))
    for peak in peaks:
        envelope = jnp.maximum(envelope, peak)
    return voltage_out, branch_out, wave_history, conv_state, envelope.reshape(-1)


def solution(mesh):
    placed = (
        P("region", None, None, None),
        P("region", None),
        P("region"),
        P("region"),
        P("region"),
        P("scen", "region"),
        P("scen", "region"),
        P(None, "scen", "region"),
        P("region"),
        P("region"),
        P("region"),
        P("region", None),
        P("region"),
        P("region"),
        P(None, "region"),
        P(None, "scen", "region"),
        P("scen"),
        P("scen"),
    )
    return jax.shard_map(
        shards,
        mesh=mesh,
        in_specs=placed,
        out_specs=(
            P("scen", "region"),
            P("scen", "region"),
            P(None, "scen", "region"),
            P(None, "scen", "region"),
            P("region"),
        ),
        check_vma=False,
    )
```

```python
import functools
import math

import jax
import jax.numpy as jnp
from jax import lax
from jax.experimental import pallas as pl
from jax.experimental.pallas import tpu as pltpu
from jax.sharding import PartitionSpec as P

STEPS = 4
LANES = 128
BF = jnp.bfloat16
F32 = jnp.float32
I32 = jnp.int32
VMEM = pl.BlockSpec(memory_space=pltpu.VMEM)
SMEM = pl.BlockSpec(memory_space=pltpu.SMEM)
HBM = pl.BlockSpec(memory_space=pltpu.HBM)


def round_up(value, unit):
    return -(-value // unit) * unit


def iota(shape, dim):
    return lax.broadcasted_iota(I32, shape, dim)


def split_2(value):
    high = value.astype(BF)
    return high, (value - high.astype(F32)).astype(BF)


def stacked(value):
    high, low = split_2(value)
    return jnp.concatenate([high, low], axis=0)


def folded(value):
    half = value.shape[0] // 2
    return value[:half] + value[half:]


def dot(left, right):
    return jnp.dot(left, right, preferred_element_type=F32)


def one_hot(mask):
    return jnp.where(mask, 1.0, 0.0).astype(BF)


def padded_index(nodes, width, padded):
    block = jnp.floor((nodes + 0.5) * (1.0 / width))
    return nodes + block * (padded - width)


class Sizes:
    def __init__(self, inverse_blocks, voltage, wave_init, line_node, conv_node):
        self.blocks, self.picks, self.width, _ = inverse_blocks.shape
        self.scen, self.nodes = voltage.shape
        self.delays = wave_init.shape[0]
        self.ends = line_node.shape[0]
        self.lines = self.ends // 2
        self.convs = conv_node.shape[0]
        self.regions = lax.axis_size("region")
        self.capacity = max(2, 12 * self.convs // (5 * self.regions))
        self.rows = round_up(self.capacity + 4, 8)
        self.slots = self.regions * self.rows
        self.slot_lanes = round_up(self.slots, 2 * LANES)
        self.padded = round_up(self.width, LANES)
        self.lanes = self.blocks * self.padded
        self.group = math.lcm(self.width, LANES) // self.width

        self.state = (self.blocks, self.scen, self.padded)
        starts = [k * self.width for k in range(self.picks)]
        self.starts = starts
        self.shifts = sorted({start % LANES for start in starts})
        self.depth = round_up(self.picks * self.width, LANES)
        self.turned = (len(self.shifts), self.blocks, 2 * self.scen, self.padded)
        self.chunk = min(2 * LANES, self.slot_lanes)
        self.chunks = self.slot_lanes // self.chunk
        self.wide = (2 * self.scen, self.lanes)
        self.weights = (self.blocks, self.picks * self.width, 2 * self.padded)
        self.site_rows = (self.lanes, self.ends)
        self.response = (self.blocks // 2, 2, self.ends, 2 * self.padded)
        self.coupling = (self.ends, 2 * self.ends)
        self.node_rows = (self.blocks, 8, self.padded)
        self.fault_cols = (2, self.scen, self.padded)
        self.drive = (self.scen, self.ends)
        self.exchange = (self.scen, self.lines)


class Copies:
    def __init__(self, sems):
        self.sems = sems
        self.count = 0

    def start(self, source, target):
        copy = pltpu.make_async_copy(source, target, self.sems.at[self.count])
        self.count += 1
        copy.start()
        return copy


def pad_blocks(size, source, store):
    group_width = size.group * size.width
    for first in range(0, size.blocks, size.group):
        chunk = source[:, first * size.width : first * size.width + group_width]
        for j in range(size.group):
            part = chunk[:, j * size.width : (j + 1) * size.width]
            zeros = jnp.zeros((part.shape[0], size.padded - size.width), part.dtype)
            store(first + j, jnp.concatenate([part, zeros], axis=1))


def unpad_blocks(size, load, target):
    group_width = size.group * size.width
    for first in range(0, size.blocks, size.group):
        parts = [load(first + j)[:, : size.width] for j in range(size.group)]
        target[:, first * size.width : first * size.width + group_width] = jnp.concatenate(
            parts, axis=1
        )


def block_lanes(size, b):
    return slice(b * size.padded, (b + 1) * size.padded)


def pack_kernel(
    size, region_hbm, power_hbm, node_hbm, gains_hbm, init_hbm, out_hbm, dst_hbm,
    region, power, node, gains, init, out, dst_out, sems,
):
    convs, slots = size.convs, size.slots
    copies = Copies(sems)
    first = copies.start(region_hbm, region)
    second = copies.start(init_hbm, init)
    others = [
        copies.start(power_hbm, power),
        copies.start(node_hbm, node),
        copies.start(gains_hbm, gains),
    ]
    first.wait()
    target = region[...]
    member = iota((round_up(size.regions, 16), convs), 0) == target
    before = one_hot(iota((convs, convs), 0) < iota((convs, convs), 1))
    earlier = dot(one_hot(member), before)
    rank = jnp.sum(jnp.where(member, earlier, 0.0), axis=0, keepdims=True)
    dst = target * size.rows + rank.astype(I32)
    dst_out[...] = dst
    select = one_hot(iota((slots, convs), 0) == dst)
    sent = [copies.start(dst_out, dst_hbm)]
    for copy in others:
        copy.wait()
    rows = [
        power[...].reshape(1, convs),
        gains[...],
        node[...].astype(F32).reshape(1, convs) + 1.0,
        jnp.zeros((LANES - 4, convs), F32),
    ]
    settings = jnp.concatenate(rows, axis=0)
    second.wait()
    state = jnp.concatenate([init[0], init[1]], axis=0)
    payload = jnp.concatenate([state.T, settings.T], axis=1)
    width = state.shape[0]
    rows = sum(dot(select, part) for part in split_2(payload))
    for r in range(size.regions):
        chunk = rows[r * size.rows : (r + 1) * size.rows]
        out[r] = chunk[:, :width]
        filler = jnp.zeros((LANES - size.rows, LANES), F32)
        turned = jnp.concatenate([chunk[:, width:], filler], axis=0).T
        out[r, size.capacity : size.capacity + 4, :] = turned[:4]
    sent.append(copies.start(out, out_hbm))
    for copy in sent:
        copy.wait()


def fault_terms(size, node, kind):
    first = lax.axis_index("region") * size.nodes
    local = (node[...] - first).astype(F32)
    inside = (local >= 0.0) & (local < size.nodes)
    site = jnp.where(inside, padded_index(local, size.width, size.padded), -1.0)
    level = 0.25 * jnp.left_shift(1, kind[...]).astype(F32)
    square = (size.scen, size.scen)
    diagonal = iota(square, 0) == iota(square, 1)

    def column(row):
        spread = jnp.where(diagonal, jnp.broadcast_to(row, square), 0.0)
        return jnp.broadcast_to(jnp.sum(spread, axis=1, keepdims=True), (size.scen, size.padded))

    return column(site), column(level)


def site_products(size, row, chunk, gather, scatter):
    part = row[:, chunk : chunk + LANES]
    block = jnp.floor((part + 0.5) * (1.0 / LANES))
    lane = part - block * LANES
    square = (LANES, LANES)
    down_block = jnp.broadcast_to(block, square).astype(BF)
    across_block = turned_row(block).astype(BF)
    down_lane = one_hot(lane == iota(square, 0).astype(F32))
    across_lane = one_hot(turned_row(lane) == iota(square, 1).astype(F32))
    zeros = jnp.zeros(square, BF)

    def put(n, carry):
        here = jnp.asarray(n, I32).astype(F32).astype(BF)
        gather(n, jnp.where(down_block == here, down_lane, zeros))
        scatter(n, jnp.where(across_block == here, across_lane, zeros))
        return carry

    lax.fori_loop(0, size.lanes // LANES, put, 0, unroll=True)


def turned_row(row):
    return jnp.broadcast_to(row, (LANES, row.shape[1])).T


def put_turned(size, x, b, value):
    pair = stacked(value)
    for i, shift in enumerate(size.shifts):
        x[i, b] = pltpu.roll(pair, shift, 1) if shift else pair


def picked_product(size, cols, b, x, wp):
    lane = iota((2 * size.scen, LANES), 1)
    tiles = []
    for first in range(0, size.depth, LANES):
        tile = None
        for k, start in enumerate(size.starts):
            if start + size.width <= first or start >= first + LANES:
                continue
            piece = x[size.shifts.index(start % LANES), cols[k, b]]
            tile = piece if tile is None else jnp.where(lane < start - first, tile, piece)
        tiles.append(tile)
    spare = size.depth - size.picks * size.width
    weights = wp[b]
    if spare:
        weights = jnp.concatenate([weights, jnp.zeros((spare, weights.shape[1]), BF)], axis=0)
    return dot(jnp.concatenate(tiles, axis=1), weights)


def three_terms(product, rows, width):
    top, low = product[:rows], product[rows:]
    return top[:, :width] + top[:, width:] + low[:, :width]


def corrections(size, drives, mt, pair):
    high = folded(dot(drives, mt[pair, 0]))
    added = high + dot(drives[: size.scen], mt[pair, 1])
    return [(2 * pair + j, added[:, block_lanes(size, j)]) for j in range(2)]


def apply_inverse(size, cols, x, wp, volt, vb):
    def block_row(b, carry):
        value = three_terms(picked_product(size, cols, b, x, wp), size.scen, size.padded)
        volt[b] = value
        vb[:, pl.ds(pl.multiple_of(b * size.padded, LANES), size.padded)] = stacked(value)
        return carry

    lax.fori_loop(0, size.blocks, block_row, 0, unroll=16)


def prep_kernel(
    size,
    cols_hbm, inverse, source, decay, gain, voltage, branch_init, line_node, fault_node, fault_kind,
    wp_out, eg_out, mt_out, kk_out, vb_out, branch_out, rest_out, rows_out, fault_out,
    cols, raw, vectors, volt_in, branch_in, nodes, faults,
    wp, eg, es, mt, both, kk, vb, volt, branch, rest, node_rows, fault_cols,
    sems,
):
    copies = Copies(sems)
    cols_copy = copies.start(cols_hbm, cols)
    small = [
        copies.start(line_node, nodes),
        copies.start(fault_node, faults.at[0:1]),
        copies.start(fault_kind, faults.at[1:2]),
    ]
    small += [copies.start(v, vectors.at[i]) for i, v in enumerate((source, decay, gain))]
    large = [copies.start(voltage, volt_in), copies.start(branch_init, branch_in)]
    stages = 4
    stage = size.blocks // stages
    weight_copies = []
    for i in range(stages):
        part = pl.ds(i * stage, stage)
        weight_copies.append(copies.start(inverse.at[part], raw.at[part]))
    sent = []
    for copy in small:
        copy.wait()

    row = padded_index(nodes[...].astype(F32), size.width, size.padded)
    for c in range(0, size.ends, LANES):
        def put_gather(n, value, c=c):
            eg[pl.ds(pl.multiple_of(n * LANES, LANES), LANES), c : c + LANES] = value

        def put_scatter(n, value, c=c):
            es[n, c : c + LANES, :] = value

        site_products(size, row, c, put_gather, put_scatter)
    sent.append(copies.start(eg, eg_out))

    for i in range(3):
        def put_row(b, value, i=i):
            node_rows[b, i : i + 1, :] = value

        pad_blocks(size, vectors.at[i], put_row)
    sent.append(copies.start(node_rows, rows_out))
    site, level = fault_terms(size, faults.at[0:1], faults.at[1:2])
    fault_cols[0] = site
    fault_cols[1] = level
    sent.append(copies.start(fault_cols, fault_out))
    for copy in large:
        copy.wait()

    def put_voltage(b, value):
        volt[b] = value
        vb[:, block_lanes(size, b)] = stacked(value)

    def put_branch(b, value):
        history = node_rows[b, 1:2, :] * value + node_rows[b, 2:3, :] * volt[b]
        branch[b] = history
        rest[b] = rest_of(size, node_rows, b, history, volt[b], site, level)

    pad_blocks(size, volt_in, put_voltage)
    pad_blocks(size, branch_in, put_branch)
    sent.append(copies.start(vb, vb_out))
    sent.append(copies.start(branch, branch_out))
    sent.append(copies.start(rest, rest_out))

    cols_copy.wait()
    zeros = jnp.zeros((size.width, size.padded - size.width), BF)
    zero_rows = jnp.zeros((size.padded - size.width, 2 * size.padded), BF)
    for i, copy in enumerate(weight_copies):
        copy.wait()

        def turn(b, carry):
            parts = []
            for k in range(size.picks):
                high, low = split_2(raw[b, k].T)
                part = jnp.concatenate([high, zeros, low, zeros], axis=1)
                wp[b, k * size.width : (k + 1) * size.width, :] = part
                parts += [part, zero_rows]
            left = jnp.concatenate([es[cols[k, b]] for k in range(size.picks)], axis=1)
            product = dot(left, jnp.concatenate(parts, axis=0))
            high, low = split_2(product[:, : size.padded] + product[:, size.padded :])
            half = pl.ds(pl.multiple_of(lax.rem(b, 2) * size.padded, LANES), size.padded)
            mt[lax.div(b, 2), 0, :, half] = high
            mt[lax.div(b, 2), 1, :, half] = low
            both[:, pl.ds(pl.multiple_of(b * size.padded, LANES), size.padded)] = jnp.concatenate(
                [high, low], axis=0
            )
            return carry

        lax.fori_loop(i * stage, (i + 1) * stage, turn, 0, unroll=4)
        part = pl.ds(i * stage, stage)
        sent.append(copies.start(wp.at[part], wp_out.at[part]))
        part = pl.ds(i * stage // 2, stage // 2)
        sent.append(copies.start(mt.at[part], mt_out.at[part]))

    high, low = split_2(folded(dot(both[...], eg[...])))
    kk[...] = jnp.concatenate([high, low], axis=1)
    sent.append(copies.start(kk, kk_out))
    for copy in sent:
        copy.wait()


def rest_of(size, node_rows, b, history, v, site, level):
    lane = iota((size.scen, size.padded), 1).astype(F32)
    first = jnp.asarray(b * size.padded, I32).astype(F32)
    hit = jnp.where(lane + first == site, level, 0.0)
    return node_rows[b, 0:1, :] - history - hit * v


def for_chunks(size, count, work):
    def one(c, carry):
        work(pl.multiple_of(c * size.chunk, LANES))
        return carry

    least = min(2, size.chunks)
    for c in range(least):
        work(c * size.chunk)
    lax.fori_loop(least, count, one, 0)


def inject(size, count, pair, cs, put):
    step = 2 if size.blocks % 2 == 0 else 1
    width = step * size.padded
    least = min(2, size.chunks)

    def inject_from(used):
        left = pair[:, : used * size.chunk]

        def some_blocks(i, carry):
            lanes = pl.ds(pl.multiple_of(i * width, LANES), width)
            both = folded(dot(left, cs[: used * size.chunk, lanes]))
            for j in range(step):
                put(i * step + j, both[:, block_lanes(size, j)])
            return carry

        lax.fori_loop(0, size.blocks // step, some_blocks, 0, unroll=True if used <= least + 1 else 1)

    for used in range(least, size.chunks + 1):
        if used == least:
            chosen = count <= used
        else:
            chosen = count == used
        pl.when(chosen)(functools.partial(inject_from, used))


def converter_update(size, count, vb, cg, prm, filt, amps, pair):
    def update(first):
        lanes = pl.ds(first, size.chunk)
        measured = folded(dot(vb[...], cg[:, lanes]))
        filtered = filt[:, lanes]
        filtered = filtered + prm[2:3, lanes] * (measured - filtered)
        current = amps[:, lanes]
        target = prm[0:1, lanes] * filtered / (1.0 + filtered * filtered)
        current = current + prm[1:2, lanes] * (target - current)
        filt[:, lanes] = filtered
        amps[:, lanes] = current
        pair[:, lanes] = stacked(current)

    for_chunks(size, count, update)


def launch_part(size, history, ends, at_ends, kk, drive_out, far, near):
    drive = jnp.zeros(size.drive, F32)
    for d in range(size.delays):
        drive = jnp.where(ends[0:1, :] == float(d + 1), history(d), drive)
    drive_out[...] = drive
    answer = three_terms(dot(stacked(drive), kk[...]), size.scen, size.ends)
    launch = 2.0 * ends[1:2, :] * (at_ends + answer) - drive
    even = lax.rem(lax.axis_index("region"), 2) == 0
    up, down = launch[:, size.lines :], launch[:, : size.lines]
    far[...] = jnp.where(even, down, up)
    near[...] = jnp.where(even, up, down)


def arrived(size, far, near):
    even = lax.rem(lax.axis_index("region"), 2) == 0
    ahead = jnp.where(even, far[...], near[...])
    after = jnp.where(even, near[...], far[...])
    return jnp.concatenate([ahead, after], axis=1)


def start_kernel(
    size,
    cols_hbm, received, waves_hbm, delay_hbm, admittance_hbm,
    wp_hbm, eg_hbm, mt_hbm, kk_hbm, vb_hbm, branch_hbm, rest_hbm, rows_hbm, fault_hbm,
    wp, eg, mt, kk, waves, ends, node_rows, fault_cols, branch, cg, cs, prm, filt, amps, volt,
    peak, drive, far, near, place_hbm,
    cols, place, delays, admittances, rest, x, vb, pair, moved, moved_settings, sems,
):
    copies = Copies(sems)
    vb_copy = copies.start(vb_hbm, vb)
    rest_copy = copies.start(rest_hbm, rest)
    cols_copy = copies.start(cols_hbm, cols)
    wp_copy = copies.start(wp_hbm, wp)
    later = [
        copies.start(eg_hbm, eg),
        copies.start(delay_hbm, delays),
        copies.start(admittance_hbm, admittances),
        copies.start(waves_hbm, waves),
        copies.start(kk_hbm, kk),
        copies.start(mt_hbm, mt),
        copies.start(branch_hbm, branch),
        copies.start(rows_hbm, node_rows),
        copies.start(fault_hbm, fault_cols),
    ]
    rows, capacity, slots, regions = size.rows, size.capacity, size.slots, size.regions
    total = 0
    for r in range(regions):
        settings = received[r * rows + capacity : r * rows + capacity + 4, :]
        filler = jnp.zeros((LANES - 4, LANES), F32)
        turned = jnp.concatenate([settings[:, :LANES], filler], axis=0).T
        place[r] = total
        moved[pl.ds(total, rows), :] = received[r * rows : (r + 1) * rows, :]
        moved_settings[pl.ds(total, rows), :] = turned[:rows]
        total = total + jnp.sum(jnp.where(settings[3:4, :] > 0.0, 1.0, 0.0)).astype(I32)
    count = lax.div(total + (size.chunk - 1), size.chunk)
    place[regions] = count
    place_copy = copies.start(place, place_hbm)
    for c in range(0, size.slot_lanes, LANES):
        valid = iota((LANES, LANES), 0) + c < total
        turned = jnp.where(valid, moved[c : c + LANES, :], 0.0).T
        filt[:, c : c + LANES] = turned[: size.scen]
        amps[:, c : c + LANES] = turned[size.scen :]
        turned = jnp.where(valid, moved_settings[c : c + LANES, :], 0.0).T
        prm[:, c : c + LANES] = turned[:8]
    def put_products(first):
        row = padded_index(prm[3:4, pl.ds(first, size.chunk)] - 1.0, size.width, size.padded)
        for c in range(0, size.chunk, LANES):
            lanes = pl.ds(pl.multiple_of(first + c, LANES), LANES)

            def put_gather(n, value, lanes=lanes):
                cg[pl.ds(pl.multiple_of(n * LANES, LANES), LANES), lanes] = value

            def put_scatter(n, value, lanes=lanes):
                cs[lanes, pl.ds(pl.multiple_of(n * LANES, LANES), LANES)] = value

            site_products(size, row, c, put_gather, put_scatter)

    for_chunks(size, count, put_products)
    peak[...] = jnp.zeros(peak.shape, F32)

    vb_copy.wait()
    converter_update(size, count, vb, cg, prm, filt, amps, pair)
    rest_copy.wait()

    def put_start(b, injected):
        put_turned(size, x, b, rest[b] + injected)

    inject(size, count, pair, cs, put_start)
    cols_copy.wait()
    wp_copy.wait()
    apply_inverse(size, cols, x, wp, volt, vb)
    for copy in later:
        copy.wait()
    ends[0:1, :] = delays[...].astype(F32)
    ends[1:2, :] = admittances[...]
    at_ends = folded(dot(vb[...], eg[...]))
    launch_part(size, lambda d: waves[d], ends, at_ends, kk, drive, far, near)
    place_copy.wait()


def middle_kernel(
    size, last,
    cols_hbm, place_hbm, drive, wp, eg, mt, node_rows, fault_cols, cg, cs, prm,
    branch_in, filt_in, amps_in, volt_in, peak_in,
    branch, filt, amps, volt, peak, at_ends, *refs,
):
    if last:
        back_hbm, branch_hbm, volt_hbm, peak_hbm, branch_out, moved, back = *refs[:4], *refs[-3:]
        refs = refs[4:-3]
    cols, place, x, vb, pair, sems = refs
    copies = Copies(sems)
    place_copy = copies.start(place_hbm, place)
    cols_copy = copies.start(cols_hbm, cols)
    drives = stacked(drive[...])
    for b, added in (c for p in range(size.blocks // 2) for c in corrections(size, drives, mt, p)):
        v = volt[b] + added
        volt[b] = v
        vb[:, block_lanes(size, b)] = stacked(v)
        magnitude = jnp.abs(v)
        top = magnitude[:8]
        for s in range(8, size.scen, 8):
            top = jnp.maximum(top, magnitude[s : s + 8])
        peak[b] = jnp.maximum(peak[b], top)
    place_copy.wait()
    count = place[size.regions]
    converter_update(size, count, vb, cg, prm, filt, amps, pair)

    def put_next(b, injected):
        history = node_rows[b, 1:2, :] * branch[b] + node_rows[b, 2:3, :] * volt[b]
        branch[b] = history
        site, level = fault_cols[0], fault_cols[1]
        rest = rest_of(size, node_rows, b, history, volt[b], site, level)
        put_turned(size, x, b, rest + injected)

    inject(size, count, pair, cs, put_next)
    cols_copy.wait()
    if last:
        for c in range(0, size.slot_lanes, LANES):
            part = jnp.concatenate([filt[:, c : c + LANES], amps[:, c : c + LANES]], axis=0)
            moved[c : c + LANES, :] = part.T
        moved[size.slot_lanes :, :] = jnp.zeros((size.rows, 2 * size.scen), F32)
        for r in range(size.regions):
            back[r * size.rows : (r + 1) * size.rows, :] = moved[pl.ds(place[r], size.rows), :]
        unpad_blocks(size, lambda b: branch[b], branch_out)
        sent = [
            copies.start(back, back_hbm),
            copies.start(branch_out, branch_hbm),
            copies.start(peak, peak_hbm),
        ]
    apply_inverse(size, cols, x, wp, volt, vb)
    if last:
        sent.append(copies.start(volt, volt_hbm))
    at_ends[...] = folded(dot(vb[...], eg[...]))
    if last:
        for copy in sent:
            copy.wait()


def launch_kernel(size, done, last, at_ends, kk, ends, waves, *refs):
    arrivals, refs = refs[: 2 * done], refs[2 * done :]

    def history(d):
        if d >= done:
            return waves[d - done]
        return arrived(size, arrivals[2 * d], arrivals[2 * d + 1])

    if last:
        refs = refs[1:]
    drive, far, near = refs[:3]
    if last:
        drive_hbm = drive
        _, waves_out, recent, drive, sems = refs[3:]
        copies = Copies(sems)
        for d in range(done):
            recent[d] = history(d)
        sent = [copies.start(recent, waves_out.at[pl.ds(1, done)])]
        kept = size.delays - 1 - done
        sent.append(copies.start(waves.at[pl.ds(0, kept)], waves_out.at[pl.ds(1 + done, kept)]))
    launch_part(size, history, ends, at_ends[...], kk, drive, far, near)
    if last:
        sent.append(copies.start(drive, drive_hbm))
        for copy in sent:
            copy.wait()


def final_kernel(
    size, drive_hbm, volt_hbm, mt_hbm, peak_hbm, voltage_hbm, top_hbm,
    drive, volt, mt, peak, voltage_out, peak_row, peak_out, sems,
):
    copies = Copies(sems)
    drive_copy = copies.start(drive_hbm, drive)
    pieces = 4 if size.blocks % 8 == 0 else 1
    pairs = size.blocks // 2 // pieces
    parts = []
    for i in range(pieces):
        part, blocks = pl.ds(i * pairs, pairs), pl.ds(2 * i * pairs, 2 * pairs)
        parts.append(
            [
                copies.start(volt_hbm.at[blocks], volt.at[blocks]),
                copies.start(mt_hbm.at[part], mt.at[part]),
            ]
        )
    peak_copy = copies.start(peak_hbm, peak)
    drive_copy.wait()
    drives = stacked(drive[...])
    for p in range(size.blocks // 2):
        if p % pairs == 0:
            for copy in parts[p // pairs]:
                copy.wait()
        for b, added in corrections(size, drives, mt, p):
            volt[b] = volt[b] + added
    peak_copy.wait()

    def largest(b):
        top = jnp.max(jnp.abs(volt[b]), axis=0, keepdims=True)
        return jnp.maximum(top, jnp.max(peak[b], axis=0, keepdims=True))

    unpad_blocks(size, largest, peak_row)
    for i in range(peak_out.shape[0]):
        peak_out[i : i + 1, :] = peak_row[:, i * LANES : (i + 1) * LANES]
    sent = [copies.start(peak_out, top_hbm)]
    unpad_blocks(size, lambda b: volt[b], voltage_out)
    sent.append(copies.start(voltage_out, voltage_hbm))
    for copy in sent:
        copy.wait()


def end_kernel(
    size, dst_hbm, received, far, near, waves_in, state_hbm, waves_out,
    dst, newest, state_out, sems,
):
    copies = Copies(sems)
    dst_copy = copies.start(dst_hbm, dst)
    newest[0] = arrived(size, far, near)
    sent = [copies.start(newest, waves_out.at[pl.ds(0, 1)])]
    parts = stacked(received[...].T)
    dst_copy.wait()
    select = one_hot(iota((size.slots, size.convs), 0) == dst[...])
    state = folded(dot(parts, select))
    state_out[0] = state[: size.scen]
    state_out[1] = state[size.scen :]
    sent.append(copies.start(state_out, state_hbm))
    for copy in sent:
        copy.wait()


def shape(dims, dtype=F32):
    return jax.ShapeDtypeStruct(dims, dtype)


def in_vmem(*values):
    return [pltpu.with_memory_space_constraint(v, pltpu.VMEM) for v in values]


def in_hbm(*values):
    return [pltpu.with_memory_space_constraint(v, pltpu.HBM) for v in values]


def call(kernel, name, outs, out_specs, args, specs, scratch, limit, aliases=None):
    return pl.pallas_call(
        kernel,
        name=name,
        out_shape=outs,
        in_specs=specs,
        out_specs=out_specs,
        scratch_shapes=list(scratch),
        input_output_aliases=aliases or {},
        compiler_params=pltpu.CompilerParams(vmem_limit_bytes=limit << 20),
    )(*args)


def shards(
    inverse_blocks, block_cols, source_current, node_decay, node_gain, voltage_init, branch_init,
    wave_init, line_node, line_delay, line_admittance, conv_region, conv_node, conv_power,
    conv_gains, conv_init, fault_node, fault_kind,
):
    size = Sizes(inverse_blocks, voltage_init, wave_init, line_node, conv_node)
    regions, rows, scen = size.regions, size.rows, size.scen
    near_pairs = [(i, i ^ 1) for i in range(regions)]
    far_pairs = [(i, (i - 1 if i % 2 == 0 else i + 1) % regions) for i in range(regions)]
    dma = pltpu.SemaphoreType.DMA
    vmem, hbm = pltpu.VMEM, pltpu.HBM

    def row(vector):
        return vector.reshape(1, -1)

    chunk = (regions, rows, 2 * scen)
    packed, dst = call(
        functools.partial(pack_kernel, size),
        "pack",
        [hbm(chunk, F32), hbm((1, size.convs), I32)],
        [HBM] * 2,
        in_hbm(row(conv_region), conv_power, conv_node, conv_gains, conv_init),
        [HBM] * 5,
        [
            vmem((1, size.convs), I32),
            vmem(conv_power.shape, F32),
            vmem(conv_node.shape, I32),
            vmem(conv_gains.shape, F32),
            vmem(conv_init.shape, F32),
            vmem(chunk, F32),
            vmem((1, size.convs), I32),
            dma((8,)),
        ],
        16,
    )
    received = lax.all_to_all(packed, "region", split_axis=0, concat_axis=0, tiled=True)
    received = received.reshape(size.slots, 2 * scen)

    cols = block_cols.T
    cols_scratch = pltpu.SMEM(cols.shape, I32)
    x_scratch = vmem(size.turned, BF)
    wide_scratch = vmem(size.wide, BF)
    place_scratch = pltpu.SMEM((LANES,), I32)
    pair_scratch = vmem((2 * scen, size.slot_lanes), BF)
    moved_scratch = vmem((size.slot_lanes + rows, 2 * scen), F32)
    kept = [
        (size.weights, BF),
        (size.site_rows, BF),
        (size.response, BF),
        (size.coupling, BF),
        (size.wide, BF),
        (size.state, F32),
        (size.state, F32),
        (size.node_rows, F32),
        (size.fault_cols, F32),
    ]
    vectors = (3, 1, size.nodes)
    args = [
        cols, inverse_blocks, row(source_current), row(node_decay), row(node_gain), voltage_init,
        branch_init, row(line_node), row(fault_node), row(fault_kind),
    ]
    wp_hbm, eg_hbm, mt_hbm, kk_hbm, vb_hbm, branch_hbm, rest_hbm, rows_hbm, fault_hbm = call(
        functools.partial(prep_kernel, size),
        "prep",
        [hbm(*item) for item in kept],
        [HBM] * len(kept),
        in_hbm(*args),
        [HBM] * len(args),
        [
            cols_scratch,
            vmem(inverse_blocks.shape, F32),
            vmem(vectors, F32),
            vmem(voltage_init.shape, F32),
            vmem(voltage_init.shape, F32),
            vmem((1, size.ends), I32),
            vmem((2, scen), I32),
            vmem(size.weights, BF),
            vmem(size.site_rows, BF),
            vmem((size.blocks, size.ends, size.padded), BF),
            vmem(size.response, BF),
            vmem((2 * size.ends, size.lanes), BF),
            vmem(size.coupling, BF),
            wide_scratch,
            vmem(size.state, F32),
            vmem(size.state, F32),
            vmem(size.state, F32),
            vmem(size.node_rows, F32),
            vmem(size.fault_cols, F32),
            dma((40,)),
        ],
        48,
    )

    slot_state = vmem((scen, size.slot_lanes), F32)
    outs = [
        vmem(size.weights, BF),
        vmem(size.site_rows, BF),
        vmem(size.response, BF),
        vmem(size.coupling, BF),
        vmem(wave_init.shape, F32),
        vmem((8, size.ends), F32),
        vmem(size.node_rows, F32),
        vmem(size.fault_cols, F32),
        vmem(size.state, F32),
        vmem((size.lanes, size.slot_lanes), BF),
        vmem((size.slot_lanes, size.lanes), BF),
        vmem((8, size.slot_lanes), F32),
        slot_state,
        slot_state,
        vmem(size.state, F32),
        vmem(size.node_rows, F32),
        vmem(size.drive, F32),
        shape(size.exchange),
        shape(size.exchange),
        hbm((LANES,), I32),
    ]
    args = [
        cols, received, wave_init, row(line_delay), row(line_admittance), wp_hbm, eg_hbm,
        mt_hbm, kk_hbm, vb_hbm, branch_hbm, rest_hbm, rows_hbm, fault_hbm,
    ]
    (
        wp, eg, mt, kk, waves, ends, node_rows, fault_cols, branch, cg, cs, prm, filt, amps, volt,
        peak, drive, far, near, place,
    ) = call(
        functools.partial(start_kernel, size),
        "start",
        outs,
        [VMEM] * (len(outs) - 1) + [HBM],
        in_hbm(cols) + in_vmem(received) + in_hbm(*args[2:]),
        [HBM, VMEM] + [HBM] * (len(args) - 2),
        [
            cols_scratch,
            place_scratch,
            vmem((1, size.ends), I32),
            vmem((1, size.ends), F32),
            vmem(size.state, F32),
            x_scratch,
            wide_scratch,
            pair_scratch,
            moved_scratch,
            moved_scratch,
            dma((16,)),
        ],
        10,
    )

    arrivals = []
    for step in range(1, STEPS):
        last = step == STEPS - 1
        from_far = lax.ppermute(far, "region", far_pairs)
        from_near = lax.ppermute(near, "region", near_pairs)
        outs = [
            vmem(size.state, F32),
            slot_state,
            slot_state,
            vmem(size.state, F32),
            vmem(size.node_rows, F32),
            vmem(size.drive, F32),
        ]
        specs = [VMEM] * len(outs)
        scratch = [cols_scratch, place_scratch, x_scratch, wide_scratch, pair_scratch, dma((6,))]
        if last:
            outs += [
                hbm((size.slots, 2 * scen), F32),
                hbm((scen, size.nodes), F32),
                hbm(size.state, F32),
                hbm(size.node_rows, F32),
            ]
            specs += [HBM] * 4
            scratch += [
                vmem((scen, size.nodes), F32),
                moved_scratch,
                vmem((size.slots, 2 * scen), F32),
            ]
        result = call(
            functools.partial(middle_kernel, size, last),
            "middle",
            outs,
            specs,
            in_hbm(cols, place)
            + in_vmem(
                drive, wp, eg, mt, node_rows, fault_cols, cg, cs, prm, branch, filt, amps, volt, peak
            ),
            [HBM] * 2 + [VMEM] * 14,
            scratch,
            12,
            {11: 0, 12: 1, 13: 2, 14: 3, 15: 4},
        )
        branch, filt, amps, volt, peak, at_ends = result[:6]
        arrivals = [from_far, from_near] + arrivals
        args = in_vmem(at_ends, kk, ends, waves) + arrivals
        outs = [vmem(size.drive, F32), shape(size.exchange), shape(size.exchange)]
        in_specs, specs, scratch, aliases = [VMEM] * len(args), [VMEM] * 3, [], {}
        if last:
            back, branch_out, volt, peak = result[6:]
            aliases = {len(args): 3}
            args += in_hbm(back)
            in_specs.append(HBM)
            outs[0] = hbm(size.drive, F32)
            outs += [hbm((size.slots, 2 * scen), F32), hbm(wave_init.shape, F32)]
            specs[0] = HBM
            specs += [HBM, HBM]
            scratch = [vmem((step, *size.drive), F32), vmem(size.drive, F32), dma((4,))]
        drive, far, near, *rest = call(
            functools.partial(launch_kernel, size, step, last),
            "launch",
            outs,
            specs,
            args,
            in_specs,
            scratch,
            4,
            aliases,
        )
    chunks, waves_out = rest
    from_far = lax.ppermute(far, "region", far_pairs)
    from_near = lax.ppermute(near, "region", near_pairs)
    chunks = chunks.reshape(regions, rows, 2 * scen)
    returned = lax.all_to_all(chunks, "region", split_axis=0, concat_axis=0, tiled=True)
    voltage_out, peak_out = call(
        functools.partial(final_kernel, size),
        "final",
        [hbm((scen, size.nodes), F32), hbm((size.nodes // LANES, LANES), F32)],
        [HBM] * 2,
        in_hbm(drive, volt, mt_hbm, peak),
        [HBM] * 4,
        [
            vmem(size.drive, F32),
            vmem(size.state, F32),
            vmem(size.response, BF),
            vmem(size.node_rows, F32),
            vmem((scen, size.nodes), F32),
            vmem((1, size.nodes), F32),
            vmem((size.nodes // LANES, LANES), F32),
            dma((12,)),
        ],
        12,
    )
    others = lax.axis_size("scen")
    peaks = []
    for d in range(1, others):
        if others & (others - 1):
            shift = [(i, (i + d) % others) for i in range(others)]
        else:
            shift = [(i, i ^ d) for i in range(others)]
        peaks.append(lax.ppermute(peak_out, "scen", shift))
    returned = returned.reshape(size.slots, 2 * scen)
    conv_state, wave_history = call(
        functools.partial(end_kernel, size),
        "end",
        [hbm(conv_init.shape, F32), hbm(wave_init.shape, F32)],
        [HBM] * 2,
        in_hbm(dst) + in_vmem(returned, from_far, from_near) + in_hbm(waves_out),
        [HBM, VMEM, VMEM, VMEM, HBM],
        [
            vmem(dst.shape, I32),
            vmem((1, *size.drive), F32),
            vmem(conv_init.shape, F32),
            dma((3,)),
        ],
        16,
        {4: 1},
    )
    envelope, conv_state = lax.optimization_barrier((peak_out, conv_state))
    for peak in peaks:
        envelope = jnp.maximum(envelope, peak)
    return voltage_out, branch_out, wave_history, conv_state, envelope.reshape(-1)


def solution(mesh):
    placed = (
        P("region", None, None, None),
        P("region", None),
        P("region"),
        P("region"),
        P("region"),
        P("scen", "region"),
        P("scen", "region"),
        P(None, "scen", "region"),
        P("region"),
        P("region"),
        P("region"),
        P("region", None),
        P("region"),
        P("region"),
        P(None, "region"),
        P(None, "scen", "region"),
        P("scen"),
        P("scen"),
    )
    return jax.shard_map(
        shards,
        mesh=mesh,
        in_specs=placed,
        out_specs=(
            P("scen", "region"),
            P("scen", "region"),
            P(None, "scen", "region"),
            P(None, "scen", "region"),
            P("region"),
        ),
        check_vma=False,
    )
```

```python
import functools
import math

import jax
import jax.numpy as jnp
from jax import lax
from jax.experimental import pallas as pl
from jax.experimental.pallas import tpu as pltpu
from jax.sharding import PartitionSpec as P

STEPS = 4
LANES = 128
BF = jnp.bfloat16
F32 = jnp.float32
I32 = jnp.int32
VMEM = pl.BlockSpec(memory_space=pltpu.VMEM)
SMEM = pl.BlockSpec(memory_space=pltpu.SMEM)
HBM = pl.BlockSpec(memory_space=pltpu.HBM)


def round_up(value, unit):
    return -(-value // unit) * unit


def iota(shape, dim):
    return lax.broadcasted_iota(I32, shape, dim)


def split_2(value):
    high = value.astype(BF)
    return high, (value - high.astype(F32)).astype(BF)


def stacked(value):
    high, low = split_2(value)
    return jnp.concatenate([high, low], axis=0)


def folded(value):
    half = value.shape[0] // 2
    return value[:half] + value[half:]


def dot(left, right):
    return jnp.dot(left, right, preferred_element_type=F32)


def one_hot(mask):
    return jnp.where(mask, 1.0, 0.0).astype(BF)


def padded_index(nodes, width, padded):
    block = jnp.floor((nodes + 0.5) * (1.0 / width))
    return nodes + block * (padded - width)


class Sizes:
    def __init__(self, inverse_blocks, voltage, wave_init, line_node, conv_node):
        self.blocks, self.picks, self.width, _ = inverse_blocks.shape
        self.scen, self.nodes = voltage.shape
        self.delays = wave_init.shape[0]
        self.ends = line_node.shape[0]
        self.lines = self.ends // 2
        self.convs = conv_node.shape[0]
        self.regions = lax.axis_size("region")
        self.capacity = max(2, 12 * self.convs // (5 * self.regions))
        self.rows = round_up(self.capacity + 4, 8)
        self.slots = self.regions * self.rows
        self.slot_lanes = round_up(self.slots, 2 * LANES)
        self.padded = round_up(self.width, LANES)
        self.lanes = self.blocks * self.padded
        self.group = math.lcm(self.width, LANES) // self.width

        self.state = (self.blocks, self.scen, self.padded)
        starts = [k * self.width for k in range(self.picks)]
        self.starts = starts
        self.shifts = sorted({start % LANES for start in starts})
        self.depth = round_up(self.picks * self.width, LANES)
        self.turned = (len(self.shifts), self.blocks, 2 * self.scen, self.padded)
        self.chunk = min(2 * LANES, self.slot_lanes)
        self.chunks = self.slot_lanes // self.chunk
        self.wide = (2 * self.scen, self.lanes)
        self.weights = (self.blocks, self.picks * self.width, 2 * self.padded)
        self.site_rows = (self.lanes, self.ends)
        self.response = (self.blocks // 2, 2, self.ends, 2 * self.padded)
        self.coupling = (self.ends, 2 * self.ends)
        self.node_rows = (self.blocks, 8, self.padded)
        self.fault_cols = (2, self.scen, self.padded)
        self.drive = (self.scen, self.ends)
        self.exchange = (self.scen, self.lines)


class Copies:
    def __init__(self, sems):
        self.sems = sems
        self.count = 0

    def start(self, source, target):
        copy = pltpu.make_async_copy(source, target, self.sems.at[self.count])
        self.count += 1
        copy.start()
        return copy


def pad_blocks(size, source, store):
    group_width = size.group * size.width
    for first in range(0, size.blocks, size.group):
        chunk = source[:, first * size.width : first * size.width + group_width]
        for j in range(size.group):
            part = chunk[:, j * size.width : (j + 1) * size.width]
            zeros = jnp.zeros((part.shape[0], size.padded - size.width), part.dtype)
            store(first + j, jnp.concatenate([part, zeros], axis=1))


def unpad_blocks(size, load, target):
    group_width = size.group * size.width
    for first in range(0, size.blocks, size.group):
        parts = [load(first + j)[:, : size.width] for j in range(size.group)]
        target[:, first * size.width : first * size.width + group_width] = jnp.concatenate(
            parts, axis=1
        )


def block_lanes(size, b):
    return slice(b * size.padded, (b + 1) * size.padded)


def pack_kernel(
    size, region_hbm, power_hbm, node_hbm, gains_hbm, init_hbm, out_hbm, dst_hbm,
    region, power, node, gains, init, out, dst_out, sems,
):
    convs, slots = size.convs, size.slots
    copies = Copies(sems)
    first = copies.start(region_hbm, region)
    second = copies.start(init_hbm, init)
    others = [
        copies.start(power_hbm, power),
        copies.start(node_hbm, node),
        copies.start(gains_hbm, gains),
    ]
    first.wait()
    target = region[...]
    member = iota((round_up(size.regions, 16), convs), 0) == target
    before = one_hot(iota((convs, convs), 0) < iota((convs, convs), 1))
    earlier = dot(one_hot(member), before)
    rank = jnp.sum(jnp.where(member, earlier, 0.0), axis=0, keepdims=True)
    dst = target * size.rows + rank.astype(I32)
    dst_out[...] = dst
    select = one_hot(iota((slots, convs), 0) == dst)
    sent = [copies.start(dst_out, dst_hbm)]
    for copy in others:
        copy.wait()
    rows = [
        power[...].reshape(1, convs),
        gains[...],
        node[...].astype(F32).reshape(1, convs) + 1.0,
        jnp.zeros((LANES - 4, convs), F32),
    ]
    settings = jnp.concatenate(rows, axis=0)
    second.wait()
    state = jnp.concatenate([init[0], init[1]], axis=0)
    payload = jnp.concatenate([state.T, settings.T], axis=1)
    width = state.shape[0]
    rows = sum(dot(select, part) for part in split_2(payload))
    for r in range(size.regions):
        chunk = rows[r * size.rows : (r + 1) * size.rows]
        out[r] = chunk[:, :width]
        filler = jnp.zeros((LANES - size.rows, LANES), F32)
        turned = jnp.concatenate([chunk[:, width:], filler], axis=0).T
        out[r, size.capacity : size.capacity + 4, :] = turned[:4]
    sent.append(copies.start(out, out_hbm))
    for copy in sent:
        copy.wait()


def fault_terms(size, node, kind):
    first = lax.axis_index("region") * size.nodes
    local = (node[...] - first).astype(F32)
    inside = (local >= 0.0) & (local < size.nodes)
    site = jnp.where(inside, padded_index(local, size.width, size.padded), -1.0)
    level = 0.25 * jnp.left_shift(1, kind[...]).astype(F32)
    square = (size.scen, size.scen)
    diagonal = iota(square, 0) == iota(square, 1)

    def column(row):
        spread = jnp.where(diagonal, jnp.broadcast_to(row, square), 0.0)
        return jnp.broadcast_to(jnp.sum(spread, axis=1, keepdims=True), (size.scen, size.padded))

    return column(site), column(level)


def site_products(size, row, chunk, gather, scatter):
    part = row[:, chunk : chunk + LANES]
    block = jnp.floor((part + 0.5) * (1.0 / LANES))
    lane = part - block * LANES
    square = (LANES, LANES)
    down_block = jnp.broadcast_to(block, square).astype(BF)
    across_block = turned_row(block).astype(BF)
    down_lane = one_hot(lane == iota(square, 0).astype(F32))
    across_lane = one_hot(turned_row(lane) == iota(square, 1).astype(F32))
    zeros = jnp.zeros(square, BF)

    def put(n, carry):
        here = jnp.asarray(n, I32).astype(F32).astype(BF)
        gather(n, jnp.where(down_block == here, down_lane, zeros))
        scatter(n, jnp.where(across_block == here, across_lane, zeros))
        return carry

    lax.fori_loop(0, size.lanes // LANES, put, 0, unroll=True)


def turned_row(row):
    return jnp.broadcast_to(row, (LANES, row.shape[1])).T


def put_turned(size, x, b, value):
    pair = stacked(value)
    for i, shift in enumerate(size.shifts):
        x[i, b] = pltpu.roll(pair, shift, 1) if shift else pair


def picked_product(size, cols, b, x, wp):
    lane = iota((2 * size.scen, LANES), 1)
    tiles = []
    for first in range(0, size.depth, LANES):
        tile = None
        for k, start in enumerate(size.starts):
            if start + size.width <= first or start >= first + LANES:
                continue
            piece = x[size.shifts.index(start % LANES), cols[k, b]]
            tile = piece if tile is None else jnp.where(lane < start - first, tile, piece)
        tiles.append(tile)
    spare = size.depth - size.picks * size.width
    weights = wp[b]
    if spare:
        weights = jnp.concatenate([weights, jnp.zeros((spare, weights.shape[1]), BF)], axis=0)
    return dot(jnp.concatenate(tiles, axis=1), weights)


def three_terms(product, rows, width):
    top, low = product[:rows], product[rows:]
    return top[:, :width] + top[:, width:] + low[:, :width]


def corrections(size, drives, mt, pair):
    high = folded(dot(drives, mt[pair, 0]))
    added = high + dot(drives[: size.scen], mt[pair, 1])
    return [(2 * pair + j, added[:, block_lanes(size, j)]) for j in range(2)]


def apply_inverse(size, cols, x, wp, volt, vb):
    def block_row(b, carry):
        value = three_terms(picked_product(size, cols, b, x, wp), size.scen, size.padded)
        volt[b] = value
        vb[:, pl.ds(pl.multiple_of(b * size.padded, LANES), size.padded)] = stacked(value)
        return carry

    lax.fori_loop(0, size.blocks, block_row, 0, unroll=16)


def prep_kernel(
    size,
    cols_hbm, inverse, source, decay, gain, voltage, branch_init, line_node, fault_node, fault_kind,
    wp_out, eg_out, mt_out, kk_out, vb_out, branch_out, rest_out, rows_out, fault_out,
    cols, raw, vectors, volt_in, branch_in, nodes, faults,
    wp, eg, es, mt, both, kk, vb, volt, branch, rest, node_rows, fault_cols,
    sems,
):
    copies = Copies(sems)
    cols_copy = copies.start(cols_hbm, cols)
    small = [
        copies.start(line_node, nodes),
        copies.start(fault_node, faults.at[0:1]),
        copies.start(fault_kind, faults.at[1:2]),
    ]
    small += [copies.start(v, vectors.at[i]) for i, v in enumerate((source, decay, gain))]
    large = [copies.start(voltage, volt_in), copies.start(branch_init, branch_in)]
    stages = 4
    stage = size.blocks // stages
    weight_copies = []
    for i in range(stages):
        part = pl.ds(i * stage, stage)
        weight_copies.append(copies.start(inverse.at[part], raw.at[part]))
    sent = []
    for copy in small:
        copy.wait()

    row = padded_index(nodes[...].astype(F32), size.width, size.padded)
    for c in range(0, size.ends, LANES):
        def put_gather(n, value, c=c):
            eg[pl.ds(pl.multiple_of(n * LANES, LANES), LANES), c : c + LANES] = value

        def put_scatter(n, value, c=c):
            es[n, c : c + LANES, :] = value

        site_products(size, row, c, put_gather, put_scatter)
    sent.append(copies.start(eg, eg_out))

    for i in range(3):
        def put_row(b, value, i=i):
            node_rows[b, i : i + 1, :] = value

        pad_blocks(size, vectors.at[i], put_row)
    sent.append(copies.start(node_rows, rows_out))
    site, level = fault_terms(size, faults.at[0:1], faults.at[1:2])
    fault_cols[0] = site
    fault_cols[1] = level
    sent.append(copies.start(fault_cols, fault_out))
    for copy in large:
        copy.wait()

    def put_voltage(b, value):
        volt[b] = value
        vb[:, block_lanes(size, b)] = stacked(value)

    def put_branch(b, value):
        history = node_rows[b, 1:2, :] * value + node_rows[b, 2:3, :] * volt[b]
        branch[b] = history
        rest[b] = rest_of(size, node_rows, b, history, volt[b], site, level)

    pad_blocks(size, volt_in, put_voltage)
    pad_blocks(size, branch_in, put_branch)
    sent.append(copies.start(vb, vb_out))
    sent.append(copies.start(branch, branch_out))
    sent.append(copies.start(rest, rest_out))

    cols_copy.wait()
    zeros = jnp.zeros((size.width, size.padded - size.width), BF)
    zero_rows = jnp.zeros((size.padded - size.width, 2 * size.padded), BF)
    for i, copy in enumerate(weight_copies):
        copy.wait()

        def turn(b, carry):
            parts = []
            for k in range(size.picks):
                high, low = split_2(raw[b, k].T)
                part = jnp.concatenate([high, zeros, low, zeros], axis=1)
                wp[b, k * size.width : (k + 1) * size.width, :] = part
                parts += [part, zero_rows]
            left = jnp.concatenate([es[cols[k, b]] for k in range(size.picks)], axis=1)
            product = dot(left, jnp.concatenate(parts, axis=0))
            high, low = split_2(product[:, : size.padded] + product[:, size.padded :])
            half = pl.ds(pl.multiple_of(lax.rem(b, 2) * size.padded, LANES), size.padded)
            mt[lax.div(b, 2), 0, :, half] = high
            mt[lax.div(b, 2), 1, :, half] = low
            both[:, pl.ds(pl.multiple_of(b * size.padded, LANES), size.padded)] = jnp.concatenate(
                [high, low], axis=0
            )
            return carry

        lax.fori_loop(i * stage, (i + 1) * stage, turn, 0, unroll=4)
        part = pl.ds(i * stage, stage)
        sent.append(copies.start(wp.at[part], wp_out.at[part]))
        part = pl.ds(i * stage // 2, stage // 2)
        sent.append(copies.start(mt.at[part], mt_out.at[part]))

    high, low = split_2(folded(dot(both[...], eg[...])))
    kk[...] = jnp.concatenate([high, low], axis=1)
    sent.append(copies.start(kk, kk_out))
    for copy in sent:
        copy.wait()


def rest_of(size, node_rows, b, history, v, site, level):
    lane = iota((size.scen, size.padded), 1).astype(F32)
    first = jnp.asarray(b * size.padded, I32).astype(F32)
    hit = jnp.where(lane + first == site, level, 0.0)
    return node_rows[b, 0:1, :] - history - hit * v


def for_chunks(size, count, work):
    def one(c, carry):
        work(pl.multiple_of(c * size.chunk, LANES))
        return carry

    least = min(2, size.chunks)
    for c in range(least):
        work(c * size.chunk)
    lax.fori_loop(least, count, one, 0)


def inject(size, count, pair, cs, put):
    step = 2 if size.blocks % 2 == 0 else 1
    width = step * size.padded
    least = min(2, size.chunks)

    def inject_from(used):
        left = pair[:, : used * size.chunk]

        def some_blocks(i, carry):
            lanes = pl.ds(pl.multiple_of(i * width, LANES), width)
            both = folded(dot(left, cs[: used * size.chunk, lanes]))
            for j in range(step):
                put(i * step + j, both[:, block_lanes(size, j)])
            return carry

        lax.fori_loop(0, size.blocks // step, some_blocks, 0, unroll=True if used <= least + 1 else 1)

    for used in range(least, size.chunks + 1):
        if used == least:
            chosen = count <= used
        else:
            chosen = count == used
        pl.when(chosen)(functools.partial(inject_from, used))


def converter_update(size, count, vb, cg, prm, filt, amps, pair):
    def update(first):
        lanes = pl.ds(first, size.chunk)
        measured = folded(dot(vb[...], cg[:, lanes]))
        filtered = filt[:, lanes]
        filtered = filtered + prm[2:3, lanes] * (measured - filtered)
        current = amps[:, lanes]
        target = prm[0:1, lanes] * filtered / (1.0 + filtered * filtered)
        current = current + prm[1:2, lanes] * (target - current)
        filt[:, lanes] = filtered
        amps[:, lanes] = current
        pair[:, lanes] = stacked(current)

    for_chunks(size, count, update)


def launch_part(size, history, ends, at_ends, kk, drive_out, far, near):
    drive = jnp.zeros(size.drive, F32)
    for d in range(size.delays):
        drive = jnp.where(ends[0:1, :] == float(d + 1), history(d), drive)
    drive_out[...] = drive
    answer = three_terms(dot(stacked(drive), kk[...]), size.scen, size.ends)
    launch = 2.0 * ends[1:2, :] * (at_ends + answer) - drive
    even = lax.rem(lax.axis_index("region"), 2) == 0
    up, down = launch[:, size.lines :], launch[:, : size.lines]
    far[...] = jnp.where(even, down, up)
    near[...] = jnp.where(even, up, down)


def arrived(size, far, near):
    even = lax.rem(lax.axis_index("region"), 2) == 0
    ahead = jnp.where(even, far[...], near[...])
    after = jnp.where(even, near[...], far[...])
    return jnp.concatenate([ahead, after], axis=1)


def start_kernel(
    size,
    cols_hbm, received, waves_hbm, delay_hbm, admittance_hbm,
    wp_hbm, eg_hbm, mt_hbm, kk_hbm, vb_hbm, branch_hbm, rest_hbm, rows_hbm, fault_hbm,
    wp, eg, mt, kk, waves, ends, node_rows, fault_cols, branch, cg, cs, prm, filt, amps, volt,
    peak, drive, far, near, place_hbm,
    cols, place, delays, admittances, rest, x, vb, pair, moved, moved_settings, sems,
):
    copies = Copies(sems)
    vb_copy = copies.start(vb_hbm, vb)
    rest_copy = copies.start(rest_hbm, rest)
    cols_copy = copies.start(cols_hbm, cols)
    wp_copy = copies.start(wp_hbm, wp)
    later = [
        copies.start(eg_hbm, eg),
        copies.start(delay_hbm, delays),
        copies.start(admittance_hbm, admittances),
        copies.start(waves_hbm, waves),
        copies.start(kk_hbm, kk),
        copies.start(mt_hbm, mt),
        copies.start(branch_hbm, branch),
        copies.start(rows_hbm, node_rows),
        copies.start(fault_hbm, fault_cols),
    ]
    rows, capacity, slots, regions = size.rows, size.capacity, size.slots, size.regions
    total = 0
    for r in range(regions):
        settings = received[r * rows + capacity : r * rows + capacity + 4, :]
        filler = jnp.zeros((LANES - 4, LANES), F32)
        turned = jnp.concatenate([settings[:, :LANES], filler], axis=0).T
        place[r] = total
        moved[pl.ds(total, rows), :] = received[r * rows : (r + 1) * rows, :]
        moved_settings[pl.ds(total, rows), :] = turned[:rows]
        total = total + jnp.sum(jnp.where(settings[3:4, :] > 0.0, 1.0, 0.0)).astype(I32)
    count = lax.div(total + (size.chunk - 1), size.chunk)
    place[regions] = count
    place_copy = copies.start(place, place_hbm)
    for c in range(0, size.slot_lanes, LANES):
        valid = iota((LANES, LANES), 0) + c < total
        turned = jnp.where(valid, moved[c : c + LANES, :], 0.0).T
        filt[:, c : c + LANES] = turned[: size.scen]
        amps[:, c : c + LANES] = turned[size.scen :]
        turned = jnp.where(valid, moved_settings[c : c + LANES, :], 0.0).T
        prm[:, c : c + LANES] = turned[:8]
    def put_products(first):
        row = padded_index(prm[3:4, pl.ds(first, size.chunk)] - 1.0, size.width, size.padded)
        for c in range(0, size.chunk, LANES):
            lanes = pl.ds(pl.multiple_of(first + c, LANES), LANES)

            def put_gather(n, value, lanes=lanes):
                cg[pl.ds(pl.multiple_of(n * LANES, LANES), LANES), lanes] = value

            def put_scatter(n, value, lanes=lanes):
                cs[lanes, pl.ds(pl.multiple_of(n * LANES, LANES), LANES)] = value

            site_products(size, row, c, put_gather, put_scatter)

    for_chunks(size, count, put_products)
    peak[...] = jnp.zeros(peak.shape, F32)

    vb_copy.wait()
    converter_update(size, count, vb, cg, prm, filt, amps, pair)
    rest_copy.wait()

    def put_start(b, injected):
        put_turned(size, x, b, rest[b] + injected)

    inject(size, count, pair, cs, put_start)
    cols_copy.wait()
    wp_copy.wait()
    apply_inverse(size, cols, x, wp, volt, vb)
    for copy in later:
        copy.wait()
    ends[0:1, :] = delays[...].astype(F32)
    ends[1:2, :] = admittances[...]
    at_ends = folded(dot(vb[...], eg[...]))
    launch_part(size, lambda d: waves[d], ends, at_ends, kk, drive, far, near)
    place_copy.wait()


def middle_kernel(
    size, last,
    cols_hbm, place_hbm, drive, wp, eg, mt, node_rows, fault_cols, cg, cs, prm,
    branch_in, filt_in, amps_in, volt_in, peak_in, *refs,
):
    if last:
        dst_hbm, refs = refs[0], refs[1:]
    branch, filt, amps, volt, peak, at_ends, *refs = refs
    if last:
        back_hbm, branch_hbm, volt_hbm, peak_hbm, *refs = refs
        branch_out, moved, back, dst = refs[-4:]
        refs = refs[:-4]
    cols, place, x, vb, pair, sems = refs
    copies = Copies(sems)
    place_copy = copies.start(place_hbm, place)
    cols_copy = copies.start(cols_hbm, cols)
    if last:
        dst_copy = copies.start(dst_hbm, dst)
    drives = stacked(drive[...])
    for b, added in (c for p in range(size.blocks // 2) for c in corrections(size, drives, mt, p)):
        v = volt[b] + added
        volt[b] = v
        vb[:, block_lanes(size, b)] = stacked(v)
        magnitude = jnp.abs(v)
        top = magnitude[:8]
        for s in range(8, size.scen, 8):
            top = jnp.maximum(top, magnitude[s : s + 8])
        peak[b] = jnp.maximum(peak[b], top)
    place_copy.wait()
    count = place[size.regions]
    converter_update(size, count, vb, cg, prm, filt, amps, pair)

    def put_next(b, injected):
        history = node_rows[b, 1:2, :] * branch[b] + node_rows[b, 2:3, :] * volt[b]
        branch[b] = history
        site, level = fault_cols[0], fault_cols[1]
        rest = rest_of(size, node_rows, b, history, volt[b], site, level)
        put_turned(size, x, b, rest + injected)

    inject(size, count, pair, cs, put_next)
    cols_copy.wait()
    if last:
        for c in range(0, size.slot_lanes, LANES):
            part = jnp.concatenate([filt[:, c : c + LANES], amps[:, c : c + LANES]], axis=0)
            moved[c : c + LANES, :] = part.T
        moved[size.slot_lanes :, :] = jnp.zeros((size.rows, 2 * size.scen), F32)
        for r in range(size.regions):
            back[r * size.rows : (r + 1) * size.rows, :] = moved[pl.ds(place[r], size.rows), :]
        dst_copy.wait()
        for row, lanes in own_rows(size):
            back[pl.ds(row, 1), :] = dst[:, lanes].astype(F32)
        unpad_blocks(size, lambda b: branch[b], branch_out)
        sent = [
            copies.start(back, back_hbm),
            copies.start(branch_out, branch_hbm),
            copies.start(peak, peak_hbm),
        ]
    apply_inverse(size, cols, x, wp, volt, vb)
    if last:
        sent.append(copies.start(volt, volt_hbm))
    at_ends[...] = folded(dot(vb[...], eg[...]))
    if last:
        for copy in sent:
            copy.wait()


def own_rows(size):
    width = 2 * size.scen
    first = lax.axis_index("region") * size.rows + size.capacity
    return [(first + i, slice(i * width, (i + 1) * width)) for i in range(size.convs // width)]


def launch_kernel(size, done, last, at_ends, kk, ends, waves, *refs):
    arrivals, refs = refs[: 2 * done], refs[2 * done :]

    def history(d):
        if d >= done:
            return waves[d - done]
        return arrived(size, arrivals[2 * d], arrivals[2 * d + 1])

    if last:
        refs = refs[1:]
    drive, far, near = refs[:3]
    if last:
        drive_hbm = drive
        _, waves_out, recent, drive, sems = refs[3:]
        copies = Copies(sems)
        for d in range(done):
            recent[d] = history(d)
        sent = [copies.start(recent, waves_out.at[pl.ds(1, done)])]
        kept = size.delays - 1 - done
        sent.append(copies.start(waves.at[pl.ds(0, kept)], waves_out.at[pl.ds(1 + done, kept)]))
    launch_part(size, history, ends, at_ends[...], kk, drive, far, near)
    if last:
        sent.append(copies.start(drive, drive_hbm))
        for copy in sent:
            copy.wait()


def final_kernel(
    size, drive_hbm, volt_hbm, mt_hbm, peak_hbm, voltage_hbm, top_hbm,
    drive, volt, mt, peak, voltage_out, peak_row, peak_out, sems,
):
    copies = Copies(sems)
    drive_copy = copies.start(drive_hbm, drive)
    pieces = 4 if size.blocks % 8 == 0 else 1
    pairs = size.blocks // 2 // pieces
    parts = []
    for i in range(pieces):
        part, blocks = pl.ds(i * pairs, pairs), pl.ds(2 * i * pairs, 2 * pairs)
        parts.append(
            [
                copies.start(volt_hbm.at[blocks], volt.at[blocks]),
                copies.start(mt_hbm.at[part], mt.at[part]),
            ]
        )
    peak_copy = copies.start(peak_hbm, peak)
    drive_copy.wait()
    drives = stacked(drive[...])
    for p in range(size.blocks // 2):
        if p % pairs == 0:
            for copy in parts[p // pairs]:
                copy.wait()
        for b, added in corrections(size, drives, mt, p):
            volt[b] = volt[b] + added
    peak_copy.wait()

    def largest(b):
        top = jnp.max(jnp.abs(volt[b]), axis=0, keepdims=True)
        return jnp.maximum(top, jnp.max(peak[b], axis=0, keepdims=True))

    unpad_blocks(size, largest, peak_row)
    for i in range(peak_out.shape[0]):
        peak_out[i : i + 1, :] = peak_row[:, i * LANES : (i + 1) * LANES]
    sent = [copies.start(peak_out, top_hbm)]
    unpad_blocks(size, lambda b: volt[b], voltage_out)
    sent.append(copies.start(voltage_out, voltage_hbm))
    for copy in sent:
        copy.wait()


def end_kernel(
    size, received, far, near, waves_in, state_hbm, waves_out, newest, state_out, sems
):
    copies = Copies(sems)
    newest[0] = arrived(size, far, near)
    sent = [copies.start(newest, waves_out.at[pl.ds(0, 1)])]
    parts = stacked(received[...].T)
    dst = jnp.concatenate([received[pl.ds(row, 1), :] for row, _ in own_rows(size)], axis=1)
    select = one_hot(iota((size.slots, size.convs), 0) == dst.astype(I32))
    state = folded(dot(parts, select))
    state_out[0] = state[: size.scen]
    state_out[1] = state[size.scen :]
    sent.append(copies.start(state_out, state_hbm))
    for copy in sent:
        copy.wait()


def shape(dims, dtype=F32):
    return jax.ShapeDtypeStruct(dims, dtype)


def in_vmem(*values):
    return [pltpu.with_memory_space_constraint(v, pltpu.VMEM) for v in values]


def in_hbm(*values):
    return [pltpu.with_memory_space_constraint(v, pltpu.HBM) for v in values]


def call(kernel, name, outs, out_specs, args, specs, scratch, limit, aliases=None):
    return pl.pallas_call(
        kernel,
        name=name,
        out_shape=outs,
        in_specs=specs,
        out_specs=out_specs,
        scratch_shapes=list(scratch),
        input_output_aliases=aliases or {},
        compiler_params=pltpu.CompilerParams(vmem_limit_bytes=limit << 20),
    )(*args)


def shards(
    inverse_blocks, block_cols, source_current, node_decay, node_gain, voltage_init, branch_init,
    wave_init, line_node, line_delay, line_admittance, conv_region, conv_node, conv_power,
    conv_gains, conv_init, fault_node, fault_kind,
):
    size = Sizes(inverse_blocks, voltage_init, wave_init, line_node, conv_node)
    regions, rows, scen = size.regions, size.rows, size.scen
    near_pairs = [(i, i ^ 1) for i in range(regions)]
    far_pairs = [(i, (i - 1 if i % 2 == 0 else i + 1) % regions) for i in range(regions)]
    dma = pltpu.SemaphoreType.DMA
    vmem, hbm = pltpu.VMEM, pltpu.HBM

    def row(vector):
        return vector.reshape(1, -1)

    chunk = (regions, rows, 2 * scen)
    packed, dst = call(
        functools.partial(pack_kernel, size),
        "pack",
        [hbm(chunk, F32), hbm((1, size.convs), I32)],
        [HBM] * 2,
        in_hbm(row(conv_region), conv_power, conv_node, conv_gains, conv_init),
        [HBM] * 5,
        [
            vmem((1, size.convs), I32),
            vmem(conv_power.shape, F32),
            vmem(conv_node.shape, I32),
            vmem(conv_gains.shape, F32),
            vmem(conv_init.shape, F32),
            vmem(chunk, F32),
            vmem((1, size.convs), I32),
            dma((8,)),
        ],
        16,
    )
    received = lax.all_to_all(packed, "region", split_axis=0, concat_axis=0, tiled=True)
    received = received.reshape(size.slots, 2 * scen)

    cols = block_cols.T
    cols_scratch = pltpu.SMEM(cols.shape, I32)
    x_scratch = vmem(size.turned, BF)
    wide_scratch = vmem(size.wide, BF)
    place_scratch = pltpu.SMEM((LANES,), I32)
    pair_scratch = vmem((2 * scen, size.slot_lanes), BF)
    moved_scratch = vmem((size.slot_lanes + rows, 2 * scen), F32)
    kept = [
        (size.weights, BF),
        (size.site_rows, BF),
        (size.response, BF),
        (size.coupling, BF),
        (size.wide, BF),
        (size.state, F32),
        (size.state, F32),
        (size.node_rows, F32),
        (size.fault_cols, F32),
    ]
    vectors = (3, 1, size.nodes)
    args = [
        cols, inverse_blocks, row(source_current), row(node_decay), row(node_gain), voltage_init,
        branch_init, row(line_node), row(fault_node), row(fault_kind),
    ]
    wp_hbm, eg_hbm, mt_hbm, kk_hbm, vb_hbm, branch_hbm, rest_hbm, rows_hbm, fault_hbm = call(
        functools.partial(prep_kernel, size),
        "prep",
        [hbm(*item) for item in kept],
        [HBM] * len(kept),
        in_hbm(*args),
        [HBM] * len(args),
        [
            cols_scratch,
            vmem(inverse_blocks.shape, F32),
            vmem(vectors, F32),
            vmem(voltage_init.shape, F32),
            vmem(voltage_init.shape, F32),
            vmem((1, size.ends), I32),
            vmem((2, scen), I32),
            vmem(size.weights, BF),
            vmem(size.site_rows, BF),
            vmem((size.blocks, size.ends, size.padded), BF),
            vmem(size.response, BF),
            vmem((2 * size.ends, size.lanes), BF),
            vmem(size.coupling, BF),
            wide_scratch,
            vmem(size.state, F32),
            vmem(size.state, F32),
            vmem(size.state, F32),
            vmem(size.node_rows, F32),
            vmem(size.fault_cols, F32),
            dma((40,)),
        ],
        48,
    )

    slot_state = vmem((scen, size.slot_lanes), F32)
    outs = [
        vmem(size.weights, BF),
        vmem(size.site_rows, BF),
        vmem(size.response, BF),
        vmem(size.coupling, BF),
        vmem(wave_init.shape, F32),
        vmem((8, size.ends), F32),
        vmem(size.node_rows, F32),
        vmem(size.fault_cols, F32),
        vmem(size.state, F32),
        vmem((size.lanes, size.slot_lanes), BF),
        vmem((size.slot_lanes, size.lanes), BF),
        vmem((8, size.slot_lanes), F32),
        slot_state,
        slot_state,
        vmem(size.state, F32),
        vmem(size.node_rows, F32),
        vmem(size.drive, F32),
        shape(size.exchange),
        shape(size.exchange),
        hbm((LANES,), I32),
    ]
    args = [
        cols, received, wave_init, row(line_delay), row(line_admittance), wp_hbm, eg_hbm,
        mt_hbm, kk_hbm, vb_hbm, branch_hbm, rest_hbm, rows_hbm, fault_hbm,
    ]
    (
        wp, eg, mt, kk, waves, ends, node_rows, fault_cols, branch, cg, cs, prm, filt, amps, volt,
        peak, drive, far, near, place,
    ) = call(
        functools.partial(start_kernel, size),
        "start",
        outs,
        [VMEM] * (len(outs) - 1) + [HBM],
        in_hbm(cols) + in_vmem(received) + in_hbm(*args[2:]),
        [HBM, VMEM] + [HBM] * (len(args) - 2),
        [
            cols_scratch,
            place_scratch,
            vmem((1, size.ends), I32),
            vmem((1, size.ends), F32),
            vmem(size.state, F32),
            x_scratch,
            wide_scratch,
            pair_scratch,
            moved_scratch,
            moved_scratch,
            dma((16,)),
        ],
        10,
    )

    arrivals = []
    for step in range(1, STEPS):
        last = step == STEPS - 1
        from_far = lax.ppermute(far, "region", far_pairs)
        from_near = lax.ppermute(near, "region", near_pairs)
        outs = [
            vmem(size.state, F32),
            slot_state,
            slot_state,
            vmem(size.state, F32),
            vmem(size.node_rows, F32),
            vmem(size.drive, F32),
        ]
        specs = [VMEM] * len(outs)
        scratch = [cols_scratch, place_scratch, x_scratch, wide_scratch, pair_scratch, dma((7,))]
        if last:
            outs += [
                hbm((size.slots, 2 * scen), F32),
                hbm((scen, size.nodes), F32),
                hbm(size.state, F32),
                hbm(size.node_rows, F32),
            ]
            specs += [HBM] * 4
            scratch += [
                vmem((scen, size.nodes), F32),
                moved_scratch,
                vmem((size.slots, 2 * scen), F32),
                vmem(dst.shape, I32),
            ]
        result = call(
            functools.partial(middle_kernel, size, last),
            "middle",
            outs,
            specs,
            in_hbm(cols, place)
            + in_vmem(
                drive, wp, eg, mt, node_rows, fault_cols, cg, cs, prm, branch, filt, amps, volt, peak
            )
            + (in_hbm(dst) if last else []),
            [HBM] * 2 + [VMEM] * 14 + ([HBM] if last else []),
            scratch,
            12,
            {11: 0, 12: 1, 13: 2, 14: 3, 15: 4},
        )
        branch, filt, amps, volt, peak, at_ends = result[:6]
        arrivals = [from_far, from_near] + arrivals
        args = in_vmem(at_ends, kk, ends, waves) + arrivals
        outs = [vmem(size.drive, F32), shape(size.exchange), shape(size.exchange)]
        in_specs, specs, scratch, aliases = [VMEM] * len(args), [VMEM] * 3, [], {}
        if last:
            back, branch_out, volt, peak = result[6:]
            aliases = {len(args): 3}
            args += in_hbm(back)
            in_specs.append(HBM)
            outs[0] = hbm(size.drive, F32)
            outs += [hbm((size.slots, 2 * scen), F32), hbm(wave_init.shape, F32)]
            specs[0] = HBM
            specs += [HBM, HBM]
            scratch = [vmem((step, *size.drive), F32), vmem(size.drive, F32), dma((4,))]
        drive, far, near, *rest = call(
            functools.partial(launch_kernel, size, step, last),
            "launch",
            outs,
            specs,
            args,
            in_specs,
            scratch,
            4,
            aliases,
        )
    chunks, waves_out = rest
    from_far = lax.ppermute(far, "region", far_pairs)
    from_near = lax.ppermute(near, "region", near_pairs)
    chunks = chunks.reshape(regions, rows, 2 * scen)
    returned = lax.all_to_all(chunks, "region", split_axis=0, concat_axis=0, tiled=True)
    voltage_out, peak_out = call(
        functools.partial(final_kernel, size),
        "final",
        [hbm((scen, size.nodes), F32), hbm((size.nodes // LANES, LANES), F32)],
        [HBM] * 2,
        in_hbm(drive, volt, mt_hbm, peak),
        [HBM] * 4,
        [
            vmem(size.drive, F32),
            vmem(size.state, F32),
            vmem(size.response, BF),
            vmem(size.node_rows, F32),
            vmem((scen, size.nodes), F32),
            vmem((1, size.nodes), F32),
            vmem((size.nodes // LANES, LANES), F32),
            dma((12,)),
        ],
        12,
    )
    others = lax.axis_size("scen")
    peaks = []
    for d in range(1, others):
        if others & (others - 1):
            shift = [(i, (i + d) % others) for i in range(others)]
        else:
            shift = [(i, i ^ d) for i in range(others)]
        peaks.append(lax.ppermute(peak_out, "scen", shift))
    returned = returned.reshape(size.slots, 2 * scen)
    conv_state, wave_history = call(
        functools.partial(end_kernel, size),
        "end",
        [hbm(conv_init.shape, F32), hbm(wave_init.shape, F32)],
        [HBM] * 2,
        in_vmem(returned, from_far, from_near) + in_hbm(waves_out),
        [VMEM, VMEM, VMEM, HBM],
        [
            vmem((1, *size.drive), F32),
            vmem(conv_init.shape, F32),
            dma((2,)),
        ],
        16,
        {3: 1},
    )
    envelope, conv_state = lax.optimization_barrier((peak_out, conv_state))
    for peak in peaks:
        envelope = jnp.maximum(envelope, peak)
    return voltage_out, branch_out, wave_history, conv_state, envelope.reshape(-1)


def solution(mesh):
    placed = (
        P("region", None, None, None),
        P("region", None),
        P("region"),
        P("region"),
        P("region"),
        P("scen", "region"),
        P("scen", "region"),
        P(None, "scen", "region"),
        P("region"),
        P("region"),
        P("region"),
        P("region", None),
        P("region"),
        P("region"),
        P(None, "region"),
        P(None, "scen", "region"),
        P("scen"),
        P("scen"),
    )
    return jax.shard_map(
        shards,
        mesh=mesh,
        in_specs=placed,
        out_specs=(
            P("scen", "region"),
            P("scen", "region"),
            P(None, "scen", "region"),
            P(None, "scen", "region"),
            P("region"),
        ),
        check_vma=False,
    )
```

```python
import functools
import math

import jax
import jax.numpy as jnp
from jax import lax
from jax.experimental import pallas as pl
from jax.experimental.pallas import tpu as pltpu
from jax.sharding import PartitionSpec as P

STEPS = 4
LANES = 128
BF = jnp.bfloat16
F32 = jnp.float32
I32 = jnp.int32
VMEM = pl.BlockSpec(memory_space=pltpu.VMEM)
SMEM = pl.BlockSpec(memory_space=pltpu.SMEM)
HBM = pl.BlockSpec(memory_space=pltpu.HBM)


def round_up(value, unit):
    return -(-value // unit) * unit


def iota(shape, dim):
    return lax.broadcasted_iota(I32, shape, dim)


def split_2(value):
    high = value.astype(BF)
    return high, (value - high.astype(F32)).astype(BF)


def stacked(value):
    high, low = split_2(value)
    return jnp.concatenate([high, low], axis=0)


def folded(value):
    half = value.shape[0] // 2
    return value[:half] + value[half:]


def dot(left, right):
    return jnp.dot(left, right, preferred_element_type=F32)


def one_hot(mask):
    return jnp.where(mask, 1.0, 0.0).astype(BF)


def padded_index(nodes, width, padded):
    block = jnp.floor((nodes + 0.5) * (1.0 / width))
    return nodes + block * (padded - width)


class Sizes:
    def __init__(self, inverse_blocks, voltage, wave_init, line_node, conv_node):
        self.blocks, self.picks, self.width, _ = inverse_blocks.shape
        self.scen, self.nodes = voltage.shape
        self.delays = wave_init.shape[0]
        self.ends = line_node.shape[0]
        self.lines = self.ends // 2
        self.convs = conv_node.shape[0]
        self.regions = lax.axis_size("region")
        self.capacity = max(2, 12 * self.convs // (5 * self.regions))
        self.rows = round_up(self.capacity + 4, 8)
        self.slots = self.regions * self.rows
        self.slot_lanes = round_up(self.slots, 2 * LANES)
        self.padded = round_up(self.width, LANES)
        self.lanes = self.blocks * self.padded
        self.group = math.lcm(self.width, LANES) // self.width

        self.state = (self.blocks, self.scen, self.padded)
        starts = [k * self.width for k in range(self.picks)]
        self.starts = starts
        self.shifts = sorted({start % LANES for start in starts})
        self.depth = round_up(self.picks * self.width, LANES)
        self.turned = (len(self.shifts), self.blocks, 2 * self.scen, self.padded)
        self.chunk = min(2 * LANES, self.slot_lanes)
        self.chunks = self.slot_lanes // self.chunk
        self.wide = (2 * self.scen, self.lanes)
        self.weights = (self.blocks, self.picks * self.width, 2 * self.padded)
        self.site_rows = (self.lanes, self.ends)
        self.response = (self.blocks // 2, 2, self.ends, 2 * self.padded)
        self.coupling = (self.ends, 2 * self.ends)
        self.node_rows = (self.blocks, 8, self.padded)
        self.fault_cols = (2, self.scen, self.padded)
        self.drive = (self.scen, self.ends)
        self.exchange = (self.scen, self.lines)


class Copies:
    def __init__(self, sems):
        self.sems = sems
        self.count = 0

    def start(self, source, target):
        copy = pltpu.make_async_copy(source, target, self.sems.at[self.count])
        self.count += 1
        copy.start()
        return copy


def pad_blocks(size, source, store):
    group_width = size.group * size.width
    for first in range(0, size.blocks, size.group):
        chunk = source[:, first * size.width : first * size.width + group_width]
        for j in range(size.group):
            part = chunk[:, j * size.width : (j + 1) * size.width]
            zeros = jnp.zeros((part.shape[0], size.padded - size.width), part.dtype)
            store(first + j, jnp.concatenate([part, zeros], axis=1))


def unpad_blocks(size, load, target):
    group_width = size.group * size.width
    for first in range(0, size.blocks, size.group):
        parts = [load(first + j)[:, : size.width] for j in range(size.group)]
        target[:, first * size.width : first * size.width + group_width] = jnp.concatenate(
            parts, axis=1
        )


def block_lanes(size, b):
    return slice(b * size.padded, (b + 1) * size.padded)


def pack_kernel(
    size, region_hbm, power_hbm, node_hbm, gains_hbm, init_hbm, out_hbm, dst_hbm,
    region, power, node, gains, init, out, dst_out, sems,
):
    convs, slots = size.convs, size.slots
    copies = Copies(sems)
    first = copies.start(region_hbm, region)
    second = copies.start(init_hbm, init)
    others = [
        copies.start(power_hbm, power),
        copies.start(node_hbm, node),
        copies.start(gains_hbm, gains),
    ]
    first.wait()
    target = region[...]
    member = iota((round_up(size.regions, 16), convs), 0) == target
    before = one_hot(iota((convs, convs), 0) < iota((convs, convs), 1))
    earlier = dot(one_hot(member), before)
    rank = jnp.sum(jnp.where(member, earlier, 0.0), axis=0, keepdims=True)
    dst = target * size.rows + rank.astype(I32)
    dst_out[...] = dst
    select = one_hot(iota((slots, convs), 0) == dst)
    sent = [copies.start(dst_out, dst_hbm)]
    for copy in others:
        copy.wait()
    rows = [
        power[...].reshape(1, convs),
        gains[...],
        node[...].astype(F32).reshape(1, convs) + 1.0,
        jnp.zeros((LANES - 4, convs), F32),
    ]
    settings = jnp.concatenate(rows, axis=0)
    second.wait()
    state = jnp.concatenate([init[0], init[1]], axis=0)
    payload = jnp.concatenate([state.T, settings.T], axis=1)
    width = state.shape[0]
    rows = sum(dot(select, part) for part in split_2(payload))
    for r in range(size.regions):
        chunk = rows[r * size.rows : (r + 1) * size.rows]
        out[r] = chunk[:, :width]
        filler = jnp.zeros((LANES - size.rows, LANES), F32)
        turned = jnp.concatenate([chunk[:, width:], filler], axis=0).T
        out[r, size.capacity : size.capacity + 4, :] = turned[:4]
        sent.append(copies.start(out.at[r], out_hbm.at[r]))
    for copy in sent:
        copy.wait()


def fault_terms(size, node, kind):
    first = lax.axis_index("region") * size.nodes
    local = (node[...] - first).astype(F32)
    inside = (local >= 0.0) & (local < size.nodes)
    site = jnp.where(inside, padded_index(local, size.width, size.padded), -1.0)
    level = 0.25 * jnp.left_shift(1, kind[...]).astype(F32)
    square = (size.scen, size.scen)
    diagonal = iota(square, 0) == iota(square, 1)

    def column(row):
        spread = jnp.where(diagonal, jnp.broadcast_to(row, square), 0.0)
        return jnp.broadcast_to(jnp.sum(spread, axis=1, keepdims=True), (size.scen, size.padded))

    return column(site), column(level)


def site_products(size, row, chunk, gather, scatter):
    part = row[:, chunk : chunk + LANES]
    block = jnp.floor((part + 0.5) * (1.0 / LANES))
    lane = part - block * LANES
    square = (LANES, LANES)
    down_block = jnp.broadcast_to(block, square).astype(BF)
    across_block = turned_row(block).astype(BF)
    down_lane = one_hot(lane == iota(square, 0).astype(F32))
    across_lane = one_hot(turned_row(lane) == iota(square, 1).astype(F32))
    zeros = jnp.zeros(square, BF)

    def put(n, carry):
        here = jnp.asarray(n, I32).astype(F32).astype(BF)
        gather(n, jnp.where(down_block == here, down_lane, zeros))
        scatter(n, jnp.where(across_block == here, across_lane, zeros))
        return carry

    lax.fori_loop(0, size.lanes // LANES, put, 0, unroll=True)


def turned_row(row):
    return jnp.broadcast_to(row, (LANES, row.shape[1])).T


def put_turned(size, x, b, value):
    pair = stacked(value)
    for i, shift in enumerate(size.shifts):
        x[i, b] = pltpu.roll(pair, shift, 1) if shift else pair


def picked_product(size, cols, b, x, wp):
    lane = iota((2 * size.scen, LANES), 1)
    tiles = []
    for first in range(0, size.depth, LANES):
        tile = None
        for k, start in enumerate(size.starts):
            if start + size.width <= first or start >= first + LANES:
                continue
            piece = x[size.shifts.index(start % LANES), cols[k, b]]
            tile = piece if tile is None else jnp.where(lane < start - first, tile, piece)
        tiles.append(tile)
    spare = size.depth - size.picks * size.width
    weights = wp[b]
    if spare:
        weights = jnp.concatenate([weights, jnp.zeros((spare, weights.shape[1]), BF)], axis=0)
    return dot(jnp.concatenate(tiles, axis=1), weights)


def three_terms(product, rows, width):
    top, low = product[:rows], product[rows:]
    return top[:, :width] + top[:, width:] + low[:, :width]


def corrections(size, drives, mt, pair):
    high = folded(dot(drives, mt[pair, 0]))
    added = high + dot(drives, mt[pair, 1])[: size.scen]
    return [(2 * pair + j, added[:, block_lanes(size, j)]) for j in range(2)]


def apply_inverse(size, cols, x, wp, volt, vb):
    def block_row(b, carry):
        value = three_terms(picked_product(size, cols, b, x, wp), size.scen, size.padded)
        volt[b] = value
        vb[:, pl.ds(pl.multiple_of(b * size.padded, LANES), size.padded)] = stacked(value)
        return carry

    lax.fori_loop(0, size.blocks, block_row, 0, unroll=16)


def prep_kernel(
    size,
    cols_hbm, inverse, source, decay, gain, voltage, branch_init, line_node, fault_node, fault_kind,
    wp_out, eg_out, mt_out, kk_out, vb_out, branch_out, rest_out, rows_out, fault_out,
    cols, raw, vectors, volt_in, branch_in, nodes, faults,
    wp, eg, es, mt, both, kk, vb, volt, branch, rest, node_rows, fault_cols,
    sems,
):
    copies = Copies(sems)
    cols_copy = copies.start(cols_hbm, cols)
    small = [
        copies.start(line_node, nodes),
        copies.start(fault_node, faults.at[0:1]),
        copies.start(fault_kind, faults.at[1:2]),
    ]
    small += [copies.start(v, vectors.at[i]) for i, v in enumerate((source, decay, gain))]
    large = [copies.start(voltage, volt_in), copies.start(branch_init, branch_in)]
    stages = 4
    stage = size.blocks // stages
    weight_copies = []
    for i in range(stages):
        part = pl.ds(i * stage, stage)
        weight_copies.append(copies.start(inverse.at[part], raw.at[part]))
    sent = []
    for copy in small:
        copy.wait()

    row = padded_index(nodes[...].astype(F32), size.width, size.padded)
    for c in range(0, size.ends, LANES):
        def put_gather(n, value, c=c):
            eg[pl.ds(pl.multiple_of(n * LANES, LANES), LANES), c : c + LANES] = value

        def put_scatter(n, value, c=c):
            es[n, c : c + LANES, :] = value

        site_products(size, row, c, put_gather, put_scatter)
    sent.append(copies.start(eg, eg_out))

    for i in range(3):
        def put_row(b, value, i=i):
            node_rows[b, i : i + 1, :] = value

        pad_blocks(size, vectors.at[i], put_row)
    sent.append(copies.start(node_rows, rows_out))
    site, level = fault_terms(size, faults.at[0:1], faults.at[1:2])
    fault_cols[0] = site
    fault_cols[1] = level
    sent.append(copies.start(fault_cols, fault_out))
    for copy in large:
        copy.wait()

    def put_voltage(b, value):
        volt[b] = value
        vb[:, block_lanes(size, b)] = stacked(value)

    def put_branch(b, value):
        history = node_rows[b, 1:2, :] * value + node_rows[b, 2:3, :] * volt[b]
        branch[b] = history
        rest[b] = rest_of(size, node_rows, b, history, volt[b], site, level)

    pad_blocks(size, volt_in, put_voltage)
    pad_blocks(size, branch_in, put_branch)
    sent.append(copies.start(vb, vb_out))
    sent.append(copies.start(branch, branch_out))
    sent.append(copies.start(rest, rest_out))

    cols_copy.wait()
    zeros = jnp.zeros((size.width, size.padded - size.width), BF)
    zero_rows = jnp.zeros((size.padded - size.width, 2 * size.padded), BF)
    for i, copy in enumerate(weight_copies):
        copy.wait()

        def turn(b, carry):
            parts = []
            for k in range(size.picks):
                high, low = split_2(raw[b, k].T)
                part = jnp.concatenate([high, zeros, low, zeros], axis=1)
                wp[b, k * size.width : (k + 1) * size.width, :] = part
                parts += [part, zero_rows]
            left = jnp.concatenate([es[cols[k, b]] for k in range(size.picks)], axis=1)
            product = dot(left, jnp.concatenate(parts, axis=0))
            high, low = split_2(product[:, : size.padded] + product[:, size.padded :])
            half = pl.ds(pl.multiple_of(lax.rem(b, 2) * size.padded, LANES), size.padded)
            mt[lax.div(b, 2), 0, :, half] = high
            mt[lax.div(b, 2), 1, :, half] = low
            both[:, pl.ds(pl.multiple_of(b * size.padded, LANES), size.padded)] = jnp.concatenate(
                [high, low], axis=0
            )
            return carry

        lax.fori_loop(i * stage, (i + 1) * stage, turn, 0, unroll=4)
        part = pl.ds(i * stage, stage)
        sent.append(copies.start(wp.at[part], wp_out.at[part]))
        part = pl.ds(i * stage // 2, stage // 2)
        sent.append(copies.start(mt.at[part], mt_out.at[part]))

    high, low = split_2(folded(dot(both[...], eg[...])))
    kk[...] = jnp.concatenate([high, low], axis=1)
    sent.append(copies.start(kk, kk_out))
    for copy in sent:
        copy.wait()


def rest_of(size, node_rows, b, history, v, site, level):
    lane = iota((size.scen, size.padded), 1).astype(F32)
    first = jnp.asarray(b * size.padded, I32).astype(F32)
    hit = jnp.where(lane + first == site, level, 0.0)
    return node_rows[b, 0:1, :] - history - hit * v


def for_chunks(size, count, work):
    def one(c, carry):
        work(pl.multiple_of(c * size.chunk, LANES))
        return carry

    least = min(2, size.chunks)
    for c in range(least):
        work(c * size.chunk)
    lax.fori_loop(least, count, one, 0)


def inject(size, count, pair, cs, put):
    step = 2 if size.blocks % 2 == 0 else 1
    width = step * size.padded
    least = min(2, size.chunks)

    def inject_from(used):
        left = pair[:, : used * size.chunk]

        def some_blocks(i, carry):
            lanes = pl.ds(pl.multiple_of(i * width, LANES), width)
            both = folded(dot(left, cs[: used * size.chunk, lanes]))
            for j in range(step):
                put(i * step + j, both[:, block_lanes(size, j)])
            return carry

        lax.fori_loop(0, size.blocks // step, some_blocks, 0, unroll=True if used <= least + 1 else 1)

    for used in range(least, size.chunks + 1):
        if used == least:
            chosen = count <= used
        else:
            chosen = count == used
        pl.when(chosen)(functools.partial(inject_from, used))


def converter_update(size, count, vb, cg, prm, filt, amps, pair):
    def update(first):
        lanes = pl.ds(first, size.chunk)
        measured = folded(dot(vb[...], cg[:, lanes]))
        filtered = filt[:, lanes]
        filtered = filtered + prm[2:3, lanes] * (measured - filtered)
        current = amps[:, lanes]
        target = prm[0:1, lanes] * filtered / (1.0 + filtered * filtered)
        current = current + prm[1:2, lanes] * (target - current)
        filt[:, lanes] = filtered
        amps[:, lanes] = current
        pair[:, lanes] = stacked(current)

    for_chunks(size, count, update)


def launch_part(size, history, ends, at_ends, kk, drive_out, far, near):
    drive = jnp.zeros(size.drive, F32)
    for d in range(size.delays):
        drive = jnp.where(ends[0:1, :] == float(d + 1), history(d), drive)
    drive_out[...] = drive
    answer = three_terms(dot(stacked(drive), kk[...]), size.scen, size.ends)
    launch = 2.0 * ends[1:2, :] * (at_ends + answer) - drive
    even = lax.rem(lax.axis_index("region"), 2) == 0
    up, down = launch[:, size.lines :], launch[:, : size.lines]
    far[...] = jnp.where(even, down, up)
    near[...] = jnp.where(even, up, down)


def arrived(size, far, near):
    even = lax.rem(lax.axis_index("region"), 2) == 0
    ahead = jnp.where(even, far[...], near[...])
    after = jnp.where(even, near[...], far[...])
    return jnp.concatenate([ahead, after], axis=1)


def start_kernel(
    size,
    cols_hbm, received, waves_hbm, delay_hbm, admittance_hbm,
    wp_hbm, eg_hbm, mt_hbm, kk_hbm, vb_hbm, branch_hbm, rest_hbm, rows_hbm, fault_hbm,
    wp, eg, mt, kk, waves, ends, node_rows, fault_cols, branch, cg, cs, prm, filt, amps, volt,
    peak, drive, far, near, place_hbm,
    cols, place, delays, admittances, rest, x, vb, pair, moved, moved_settings, sems,
):
    copies = Copies(sems)
    vb_copy = copies.start(vb_hbm, vb)
    rest_copy = copies.start(rest_hbm, rest)
    cols_copy = copies.start(cols_hbm, cols)
    wp_copy = copies.start(wp_hbm, wp)
    later = [
        copies.start(eg_hbm, eg),
        copies.start(delay_hbm, delays),
        copies.start(admittance_hbm, admittances),
        copies.start(waves_hbm, waves),
        copies.start(kk_hbm, kk),
        copies.start(mt_hbm, mt),
        copies.start(branch_hbm, branch),
        copies.start(rows_hbm, node_rows),
        copies.start(fault_hbm, fault_cols),
    ]
    rows, capacity, slots, regions = size.rows, size.capacity, size.slots, size.regions
    total = 0
    for r in range(regions):
        settings = received[r * rows + capacity : r * rows + capacity + 4, :]
        filler = jnp.zeros((LANES - 4, LANES), F32)
        turned = jnp.concatenate([settings[:, :LANES], filler], axis=0).T
        place[r] = total
        moved[pl.ds(total, rows), :] = received[r * rows : (r + 1) * rows, :]
        moved_settings[pl.ds(total, rows), :] = turned[:rows]
        total = total + jnp.sum(jnp.where(settings[3:4, :] > 0.0, 1.0, 0.0)).astype(I32)
    count = lax.div(total + (size.chunk - 1), size.chunk)
    place[regions] = count
    place_copy = copies.start(place, place_hbm)
    for c in range(0, size.slot_lanes, LANES):
        valid = iota((LANES, LANES), 0) + c < total
        turned = jnp.where(valid, moved[c : c + LANES, :], 0.0).T
        filt[:, c : c + LANES] = turned[: size.scen]
        amps[:, c : c + LANES] = turned[size.scen :]
        turned = jnp.where(valid, moved_settings[c : c + LANES, :], 0.0).T
        prm[:, c : c + LANES] = turned[:8]
    def put_products(first):
        row = padded_index(prm[3:4, pl.ds(first, size.chunk)] - 1.0, size.width, size.padded)
        for c in range(0, size.chunk, LANES):
            lanes = pl.ds(pl.multiple_of(first + c, LANES), LANES)

            def put_gather(n, value, lanes=lanes):
                cg[pl.ds(pl.multiple_of(n * LANES, LANES), LANES), lanes] = value

            def put_scatter(n, value, lanes=lanes):
                cs[lanes, pl.ds(pl.multiple_of(n * LANES, LANES), LANES)] = value

            site_products(size, row, c, put_gather, put_scatter)

    for_chunks(size, count, put_products)
    peak[...] = jnp.zeros(peak.shape, F32)

    vb_copy.wait()
    converter_update(size, count, vb, cg, prm, filt, amps, pair)
    rest_copy.wait()

    def put_start(b, injected):
        put_turned(size, x, b, rest[b] + injected)

    inject(size, count, pair, cs, put_start)
    cols_copy.wait()
    wp_copy.wait()
    apply_inverse(size, cols, x, wp, volt, vb)
    for copy in later:
        copy.wait()
    ends[0:1, :] = delays[...].astype(F32)
    ends[1:2, :] = admittances[...]
    at_ends = folded(dot(vb[...], eg[...]))
    launch_part(size, lambda d: waves[d], ends, at_ends, kk, drive, far, near)
    place_copy.wait()


def middle_kernel(
    size, last,
    cols_hbm, place_hbm, drive, wp, eg, mt, node_rows, fault_cols, cg, cs, prm,
    branch_in, filt_in, amps_in, volt_in, peak_in, *refs,
):
    if last:
        dst_hbm, refs = refs[0], refs[1:]
    branch, filt, amps, volt, peak, at_ends, *refs = refs
    if last:
        back_hbm, branch_hbm, volt_hbm, peak_hbm, *refs = refs
        branch_out, moved, back, dst = refs[-4:]
        refs = refs[:-4]
    cols, place, x, vb, pair, sems = refs
    copies = Copies(sems)
    place_copy = copies.start(place_hbm, place)
    cols_copy = copies.start(cols_hbm, cols)
    if last:
        dst_copy = copies.start(dst_hbm, dst)
    drives = stacked(drive[...])
    for b, added in (c for p in range(size.blocks // 2) for c in corrections(size, drives, mt, p)):
        v = volt[b] + added
        volt[b] = v
        vb[:, block_lanes(size, b)] = stacked(v)
        magnitude = jnp.abs(v)
        top = magnitude[:8]
        for s in range(8, size.scen, 8):
            top = jnp.maximum(top, magnitude[s : s + 8])
        peak[b] = jnp.maximum(peak[b], top)
    place_copy.wait()
    count = place[size.regions]
    converter_update(size, count, vb, cg, prm, filt, amps, pair)

    def put_next(b, injected):
        history = node_rows[b, 1:2, :] * branch[b] + node_rows[b, 2:3, :] * volt[b]
        branch[b] = history
        site, level = fault_cols[0], fault_cols[1]
        rest = rest_of(size, node_rows, b, history, volt[b], site, level)
        put_turned(size, x, b, rest + injected)

    inject(size, count, pair, cs, put_next)
    cols_copy.wait()
    if last:
        for c in range(0, size.slot_lanes, LANES):
            part = jnp.concatenate([filt[:, c : c + LANES], amps[:, c : c + LANES]], axis=0)
            moved[c : c + LANES, :] = part.T
        moved[size.slot_lanes :, :] = jnp.zeros((size.rows, 2 * size.scen), F32)
        for r in range(size.regions):
            back[r * size.rows : (r + 1) * size.rows, :] = moved[pl.ds(place[r], size.rows), :]
        dst_copy.wait()
        for row, lanes in own_rows(size):
            back[pl.ds(row, 1), :] = dst[:, lanes].astype(F32)
        unpad_blocks(size, lambda b: branch[b], branch_out)
        sent = [
            copies.start(back, back_hbm),
            copies.start(branch_out, branch_hbm),
            copies.start(peak, peak_hbm),
        ]
    apply_inverse(size, cols, x, wp, volt, vb)
    if last:
        sent.append(copies.start(volt, volt_hbm))
    at_ends[...] = folded(dot(vb[...], eg[...]))
    if last:
        for copy in sent:
            copy.wait()


def own_rows(size):
    width = 2 * size.scen
    first = lax.axis_index("region") * size.rows + size.capacity
    return [(first + i, slice(i * width, (i + 1) * width)) for i in range(size.convs // width)]


def launch_kernel(size, done, last, at_ends, kk, ends, waves, *refs):
    arrivals, refs = refs[: 2 * done], refs[2 * done :]

    def history(d):
        if d >= done:
            return waves[d - done]
        return arrived(size, arrivals[2 * d], arrivals[2 * d + 1])

    if last:
        refs = refs[1:]
    drive, far, near = refs[:3]
    if last:
        drive_hbm = drive
        _, waves_out, recent, drive, sems = refs[3:]
        copies = Copies(sems)
        for d in range(done):
            recent[d] = history(d)
        sent = [copies.start(recent, waves_out.at[pl.ds(1, done)])]
        kept = size.delays - 1 - done
        sent.append(copies.start(waves.at[pl.ds(0, kept)], waves_out.at[pl.ds(1 + done, kept)]))
    launch_part(size, history, ends, at_ends[...], kk, drive, far, near)
    if last:
        sent.append(copies.start(drive, drive_hbm))
        for copy in sent:
            copy.wait()


def final_kernel(
    size, drive_hbm, volt_hbm, mt_hbm, peak_hbm, voltage_hbm, top_hbm,
    drive, volt, mt, peak, voltage_out, peak_row, peak_out, sems,
):
    copies = Copies(sems)
    drive_copy = copies.start(drive_hbm, drive)
    pieces = 4 if size.blocks % 8 == 0 else 1
    pairs = size.blocks // 2 // pieces
    parts = []
    for i in range(pieces):
        part, blocks = pl.ds(i * pairs, pairs), pl.ds(2 * i * pairs, 2 * pairs)
        parts.append(
            [
                copies.start(volt_hbm.at[blocks], volt.at[blocks]),
                copies.start(mt_hbm.at[part], mt.at[part]),
            ]
        )
    peak_copy = copies.start(peak_hbm, peak)
    drive_copy.wait()
    drives = stacked(drive[...])
    for p in range(size.blocks // 2):
        if p % pairs == 0:
            for copy in parts[p // pairs]:
                copy.wait()
        for b, added in corrections(size, drives, mt, p):
            volt[b] = volt[b] + added
    peak_copy.wait()

    def largest(b):
        top = jnp.max(jnp.abs(volt[b]), axis=0, keepdims=True)
        return jnp.maximum(top, jnp.max(peak[b], axis=0, keepdims=True))

    unpad_blocks(size, largest, peak_row)
    for i in range(peak_out.shape[0]):
        peak_out[i : i + 1, :] = peak_row[:, i * LANES : (i + 1) * LANES]
    sent = [copies.start(peak_out, top_hbm)]
    unpad_blocks(size, lambda b: volt[b], voltage_out)
    sent.append(copies.start(voltage_out, voltage_hbm))
    for copy in sent:
        copy.wait()


def end_kernel(
    size, received, far, near, waves_in, state_hbm, waves_out, newest, state_out, sems
):
    copies = Copies(sems)
    newest[0] = arrived(size, far, near)
    sent = [copies.start(newest, waves_out.at[pl.ds(0, 1)])]
    parts = stacked(received[...].T)
    dst = jnp.concatenate([received[pl.ds(row, 1), :] for row, _ in own_rows(size)], axis=1)
    select = one_hot(iota((size.slots, size.convs), 0) == dst.astype(I32))
    state = folded(dot(parts, select))
    state_out[0] = state[: size.scen]
    state_out[1] = state[size.scen :]
    sent.append(copies.start(state_out, state_hbm))
    for copy in sent:
        copy.wait()


def shape(dims, dtype=F32):
    return jax.ShapeDtypeStruct(dims, dtype)


def in_vmem(*values):
    return [pltpu.with_memory_space_constraint(v, pltpu.VMEM) for v in values]


def in_hbm(*values):
    return [pltpu.with_memory_space_constraint(v, pltpu.HBM) for v in values]


def call(kernel, name, outs, out_specs, args, specs, scratch, limit, aliases=None):
    return pl.pallas_call(
        kernel,
        name=name,
        out_shape=outs,
        in_specs=specs,
        out_specs=out_specs,
        scratch_shapes=list(scratch),
        input_output_aliases=aliases or {},
        compiler_params=pltpu.CompilerParams(vmem_limit_bytes=limit << 20),
    )(*args)


def shards(
    inverse_blocks, block_cols, source_current, node_decay, node_gain, voltage_init, branch_init,
    wave_init, line_node, line_delay, line_admittance, conv_region, conv_node, conv_power,
    conv_gains, conv_init, fault_node, fault_kind,
):
    size = Sizes(inverse_blocks, voltage_init, wave_init, line_node, conv_node)
    regions, rows, scen = size.regions, size.rows, size.scen
    near_pairs = [(i, i ^ 1) for i in range(regions)]
    far_pairs = [(i, (i - 1 if i % 2 == 0 else i + 1) % regions) for i in range(regions)]
    dma = pltpu.SemaphoreType.DMA
    vmem, hbm = pltpu.VMEM, pltpu.HBM

    def row(vector):
        return vector.reshape(1, -1)

    chunk = (regions, rows, 2 * scen)
    packed, dst = call(
        functools.partial(pack_kernel, size),
        "pack",
        [hbm(chunk, F32), hbm((1, size.convs), I32)],
        [HBM] * 2,
        in_hbm(row(conv_region), conv_power, conv_node, conv_gains, conv_init),
        [HBM] * 5,
        [
            vmem((1, size.convs), I32),
            vmem(conv_power.shape, F32),
            vmem(conv_node.shape, I32),
            vmem(conv_gains.shape, F32),
            vmem(conv_init.shape, F32),
            vmem(chunk, F32),
            vmem((1, size.convs), I32),
            dma((8 + regions,)),
        ],
        16,
    )
    received = lax.all_to_all(packed, "region", split_axis=0, concat_axis=0, tiled=True)
    received = received.reshape(size.slots, 2 * scen)

    cols = block_cols.T
    cols_scratch = pltpu.SMEM(cols.shape, I32)
    x_scratch = vmem(size.turned, BF)
    wide_scratch = vmem(size.wide, BF)
    place_scratch = pltpu.SMEM((LANES,), I32)
    pair_scratch = vmem((2 * scen, size.slot_lanes), BF)
    moved_scratch = vmem((size.slot_lanes + rows, 2 * scen), F32)
    kept = [
        (size.weights, BF),
        (size.site_rows, BF),
        (size.response, BF),
        (size.coupling, BF),
        (size.wide, BF),
        (size.state, F32),
        (size.state, F32),
        (size.node_rows, F32),
        (size.fault_cols, F32),
    ]
    vectors = (3, 1, size.nodes)
    args = [
        cols, inverse_blocks, row(source_current), row(node_decay), row(node_gain), voltage_init,
        branch_init, row(line_node), row(fault_node), row(fault_kind),
    ]
    wp_hbm, eg_hbm, mt_hbm, kk_hbm, vb_hbm, branch_hbm, rest_hbm, rows_hbm, fault_hbm = call(
        functools.partial(prep_kernel, size),
        "prep",
        [hbm(*item) for item in kept],
        [HBM] * len(kept),
        in_hbm(*args),
        [HBM] * len(args),
        [
            cols_scratch,
            vmem(inverse_blocks.shape, F32),
            vmem(vectors, F32),
            vmem(voltage_init.shape, F32),
            vmem(voltage_init.shape, F32),
            vmem((1, size.ends), I32),
            vmem((2, scen), I32),
            vmem(size.weights, BF),
            vmem(size.site_rows, BF),
            vmem((size.blocks, size.ends, size.padded), BF),
            vmem(size.response, BF),
            vmem((2 * size.ends, size.lanes), BF),
            vmem(size.coupling, BF),
            wide_scratch,
            vmem(size.state, F32),
            vmem(size.state, F32),
            vmem(size.state, F32),
            vmem(size.node_rows, F32),
            vmem(size.fault_cols, F32),
            dma((40,)),
        ],
        48,
    )

    slot_state = vmem((scen, size.slot_lanes), F32)
    outs = [
        vmem(size.weights, BF),
        vmem(size.site_rows, BF),
        vmem(size.response, BF),
        vmem(size.coupling, BF),
        vmem(wave_init.shape, F32),
        vmem((8, size.ends), F32),
        vmem(size.node_rows, F32),
        vmem(size.fault_cols, F32),
        vmem(size.state, F32),
        vmem((size.lanes, size.slot_lanes), BF),
        vmem((size.slot_lanes, size.lanes), BF),
        vmem((8, size.slot_lanes), F32),
        slot_state,
        slot_state,
        vmem(size.state, F32),
        vmem(size.node_rows, F32),
        vmem(size.drive, F32),
        shape(size.exchange),
        shape(size.exchange),
        hbm((LANES,), I32),
    ]
    args = [
        cols, received, wave_init, row(line_delay), row(line_admittance), wp_hbm, eg_hbm,
        mt_hbm, kk_hbm, vb_hbm, branch_hbm, rest_hbm, rows_hbm, fault_hbm,
    ]
    (
        wp, eg, mt, kk, waves, ends, node_rows, fault_cols, branch, cg, cs, prm, filt, amps, volt,
        peak, drive, far, near, place,
    ) = call(
        functools.partial(start_kernel, size),
        "start",
        outs,
        [VMEM] * (len(outs) - 1) + [HBM],
        in_hbm(cols) + in_vmem(received) + in_hbm(*args[2:]),
        [HBM, VMEM] + [HBM] * (len(args) - 2),
        [
            cols_scratch,
            place_scratch,
            vmem((1, size.ends), I32),
            vmem((1, size.ends), F32),
            vmem(size.state, F32),
            x_scratch,
            wide_scratch,
            pair_scratch,
            moved_scratch,
            moved_scratch,
            dma((16,)),
        ],
        10,
    )

    arrivals = []
    for step in range(1, STEPS):
        last = step == STEPS - 1
        from_far = lax.ppermute(far, "region", far_pairs)
        from_near = lax.ppermute(near, "region", near_pairs)
        outs = [
            vmem(size.state, F32),
            slot_state,
            slot_state,
            vmem(size.state, F32),
            vmem(size.node_rows, F32),
            vmem(size.drive, F32),
        ]
        specs = [VMEM] * len(outs)
        scratch = [cols_scratch, place_scratch, x_scratch, wide_scratch, pair_scratch, dma((7,))]
        if last:
            outs += [
                hbm((size.slots, 2 * scen), F32),
                hbm((scen, size.nodes), F32),
                hbm(size.state, F32),
                hbm(size.node_rows, F32),
            ]
            specs += [HBM] * 4
            scratch += [
                vmem((scen, size.nodes), F32),
                moved_scratch,
                vmem((size.slots, 2 * scen), F32),
                vmem(dst.shape, I32),
            ]
        result = call(
            functools.partial(middle_kernel, size, last),
            "middle",
            outs,
            specs,
            in_hbm(cols, place)
            + in_vmem(
                drive, wp, eg, mt, node_rows, fault_cols, cg, cs, prm, branch, filt, amps, volt, peak
            )
            + (in_hbm(dst) if last else []),
            [HBM] * 2 + [VMEM] * 14 + ([HBM] if last else []),
            scratch,
            12,
            {11: 0, 12: 1, 13: 2, 14: 3, 15: 4},
        )
        branch, filt, amps, volt, peak, at_ends = result[:6]
        arrivals = [from_far, from_near] + arrivals
        args = in_vmem(at_ends, kk, ends, waves) + arrivals
        outs = [vmem(size.drive, F32), shape(size.exchange), shape(size.exchange)]
        in_specs, specs, scratch, aliases = [VMEM] * len(args), [VMEM] * 3, [], {}
        if last:
            back, branch_out, volt, peak = result[6:]
            aliases = {len(args): 3}
            args += in_hbm(back)
            in_specs.append(HBM)
            outs[0] = hbm(size.drive, F32)
            outs += [hbm((size.slots, 2 * scen), F32), hbm(wave_init.shape, F32)]
            specs[0] = HBM
            specs += [HBM, HBM]
            scratch = [vmem((step, *size.drive), F32), vmem(size.drive, F32), dma((4,))]
        drive, far, near, *rest = call(
            functools.partial(launch_kernel, size, step, last),
            "launch",
            outs,
            specs,
            args,
            in_specs,
            scratch,
            4,
            aliases,
        )
    chunks, waves_out = rest
    from_far = lax.ppermute(far, "region", far_pairs)
    from_near = lax.ppermute(near, "region", near_pairs)
    chunks = chunks.reshape(regions, rows, 2 * scen)
    returned = lax.all_to_all(chunks, "region", split_axis=0, concat_axis=0, tiled=True)
    voltage_out, peak_out = call(
        functools.partial(final_kernel, size),
        "final",
        [hbm((scen, size.nodes), F32), hbm((size.nodes // LANES, LANES), F32)],
        [HBM] * 2,
        in_hbm(drive, volt, mt_hbm, peak),
        [HBM] * 4,
        [
            vmem(size.drive, F32),
            vmem(size.state, F32),
            vmem(size.response, BF),
            vmem(size.node_rows, F32),
            vmem((scen, size.nodes), F32),
            vmem((1, size.nodes), F32),
            vmem((size.nodes // LANES, LANES), F32),
            dma((12,)),
        ],
        12,
    )
    others = lax.axis_size("scen")
    peaks = []
    for d in range(1, others):
        if others & (others - 1):
            shift = [(i, (i + d) % others) for i in range(others)]
        else:
            shift = [(i, i ^ d) for i in range(others)]
        peaks.append(lax.ppermute(peak_out, "scen", shift))
    returned = returned.reshape(size.slots, 2 * scen)
    conv_state, wave_history = call(
        functools.partial(end_kernel, size),
        "end",
        [hbm(conv_init.shape, F32), hbm(wave_init.shape, F32)],
        [HBM] * 2,
        in_vmem(returned, from_far, from_near) + in_hbm(waves_out),
        [VMEM, VMEM, VMEM, HBM],
        [
            vmem((1, *size.drive), F32),
            vmem(conv_init.shape, F32),
            dma((2,)),
        ],
        16,
        {3: 1},
    )
    envelope, conv_state = lax.optimization_barrier((peak_out, conv_state))
    for peak in peaks:
        envelope = jnp.maximum(envelope, peak)
    return voltage_out, branch_out, wave_history, conv_state, envelope.reshape(-1)


def solution(mesh):
    placed = (
        P("region", None, None, None),
        P("region", None),
        P("region"),
        P("region"),
        P("region"),
        P("scen", "region"),
        P("scen", "region"),
        P(None, "scen", "region"),
        P("region"),
        P("region"),
        P("region"),
        P("region", None),
        P("region"),
        P("region"),
        P(None, "region"),
        P(None, "scen", "region"),
        P("scen"),
        P("scen"),
    )
    return jax.shard_map(
        shards,
        mesh=mesh,
        in_specs=placed,
        out_specs=(
            P("scen", "region"),
            P("scen", "region"),
            P(None, "scen", "region"),
            P(None, "scen", "region"),
            P("region"),
        ),
        check_vma=False,
    )
```
